128 devices in a mesh: grp: 8 (over y, core), sub: 16 (over z, x).
Axes of the slice: x: 4, y: 4, z: 4, core: 2. Of those that a mesh axis runs over, the one named last changes fastest.
Arguments:
- feats: bfloat16 [1024, 8, 8, 512], P(('grp', 'sub')), may hold values from -6 to 6
- neighbours: int32 [1024, 6], P(('grp', 'sub')), may hold values from -1 to 1023, as said below
- w_fine: bfloat16 [7, 64, 64], replicated, may hold values from -0.25 to 0.25
- w_down: bfloat16 [512, 256], replicated, may hold values from -0.25 to 0.25
- w_lift: bfloat16 [256, 512], replicated, may hold values from -0.375 to 0.375
- coarse_nbrs: int32 [128, 6], replicated, may hold values from -1 to 127, as said below
- w_coarse: bfloat16 [7, 512, 512], replicated, may hold values from -0.09375 to 0.09375
- w_back: bfloat16 [512, 256], replicated, may hold values from -0.25 to 0.25
- w_up: bfloat16 [256, 512], replicated, may hold values from -0.375 to 0.375
- grad_out: bfloat16 [1024, 8, 8, 512], P(('grp', 'sub')), may hold values from -6 to 6
Outputs:
- fine_out: bfloat16 [1024, 8, 8, 512], P(('grp', 'sub'))
- feats_grad: bfloat16 [1024, 8, 8, 512], P(('grp', 'sub'))
- w_fine_grad: float32 [7, 64, 64], replicated
- w_down_grad: float32 [512, 256], replicated
- w_lift_grad: float32 [256, 512], replicated
- w_coarse_grad: float32 [7, 512, 512], replicated
- w_back_grad: float32 [512, 256], replicated
- w_up_grad: float32 [256, 512], replicated
The draws below stay inside these ranges and needn't reach their ends.
Inputs may be any that keep to these rules, and one draw needn't show every extreme that they name: `neighbours`: each entry is -1 or a brick of the same device or of a device at most 2 away in the device order of the bricks (device i holds bricks i*8 to (i+1)*8 - 1); one device's entries name bricks of one other device at most 6 times, and exactly 6 times for some other device. `coarse_nbrs`: each entry is -1 or a node.
All inputs are finite; a program needn't handle non-finite values.
Results may differ from the reference program's by a relative error of at most 0.012.
Values may be sent and summed in bfloat16 or wider, within the bound.
A program may use at most 128 MiB of HBM per device.

```python
import jax
import jax.numpy as jnp
from jax import lax

SIDE = 8
CH_FINE = 64
CH_POOL = 256
CH_COARSE = 512
BRICKS_DEV = 8
CAPACITY = 6
BRICKS = 1024
NODES = 128


def assemble_field(noise, shared):
    field = noise.reshape(NODES, 8 * SIDE * SIDE * SIDE, CH_FINE) + shared[:, None, :]
    field = jnp.clip(field, -6.0, 6.0)
    return field.reshape(BRICKS, SIDE, SIDE, SIDE * CH_FINE).astype(jnp.bfloat16)


def draw_feats(key, part):
    key = jax.random.fold_in(key, 21)
    keys = jax.random.split(key, 2)
    shape_all = (BRICKS, SIDE, SIDE, SIDE * CH_FINE)
    noise = jax.random.normal(keys[0], shape_all, jnp.float32)
    shared = 0.5 * jax.random.normal(keys[1], (NODES, CH_FINE), jnp.float32)
    return assemble_field(noise, shared)


def draw_grad_out(key, part):
    key = jax.random.fold_in(key, 29)
    keys = jax.random.split(key, 2)
    shape_all = (BRICKS, SIDE, SIDE, SIDE * CH_FINE)
    noise = jax.random.normal(keys[0], shape_all, jnp.float32)
    shared = 0.5 * jax.random.normal(keys[1], (NODES, CH_FINE), jnp.float32)
    return assemble_field(noise, shared)


def draw_neighbours(key, part):
    key = jax.random.fold_in(key, 7)
    keys = jax.random.split(key, 6)
    devices_all = BRICKS // BRICKS_DEV
    pairs = BRICKS_DEV * 6
    device_ids = jnp.arange(devices_all, dtype=jnp.int32)
    offsets = jnp.array([-2, -1, 1, 2], jnp.int32)
    target = device_ids[:, None] + offsets[None, :]
    usable = (target >= 0) & (target < devices_all)
    counts = jax.random.randint(keys[0], (devices_all, 4), CAPACITY // 2, CAPACITY + 1)
    forced = jax.random.randint(keys[1], (devices_all,), 0, 4)
    forced_ok = jnp.take_along_axis(usable, forced[:, None], axis=1)[:, 0]
    forced = jnp.where(forced_ok, forced, 3 - forced)
    counts = jnp.where(jnp.arange(4)[None, :] == forced[:, None], CAPACITY, counts)
    counts = jnp.where(usable, counts, 0)
    bounds = jnp.cumsum(counts, axis=1)
    order = jax.vmap(lambda sub_key: jax.random.permutation(sub_key, pairs))(jax.random.split(keys[2], devices_all))
    places = jnp.argsort(order, axis=1)
    classes = jnp.sum(places[:, :, None] >= bounds[:, None, :], axis=2)
    remote_owner = device_ids[:, None] + offsets[jnp.minimum(classes, 3)]
    remote_pick = jax.random.randint(keys[3], (devices_all, pairs), 0, BRICKS_DEV)
    absent = jax.random.randint(keys[4], (devices_all, pairs), 0, 8) == 0
    local_pick = jax.random.randint(keys[5], (devices_all, pairs), 0, BRICKS_DEV)
    remote_id = remote_owner * BRICKS_DEV + remote_pick
    local_id = jnp.where(absent, -1, device_ids[:, None] * BRICKS_DEV + local_pick)
    chosen = jnp.where(classes < 4, remote_id, local_id)
    return chosen.reshape(BRICKS, 6).astype(jnp.int32)


def draw_coarse_nbrs(key, part):
    key = jax.random.fold_in(key, 13)
    keys = jax.random.split(key, 2)
    picks = jax.random.randint(keys[0], (NODES, 6), 0, NODES)
    absent = jax.random.randint(keys[1], (NODES, 6), 0, 6) == 0
    return jnp.where(absent, -1, picks).astype(jnp.int32)


def bell_draw(key, shape, scale, most, held_as=jnp.bfloat16):
    return jnp.clip(scale * jax.random.normal(key, shape, jnp.float32), -most, most).astype(held_as)


def setup_inputs(seed: int = 0) -> dict:
    seeds = jax.random.split(jax.random.key(seed), 11)
    feats = draw_feats(jax.random.fold_in(seeds[10], 71), 0)
    neighbours = draw_neighbours(jax.random.fold_in(seeds[10], 71), 0)
    w_fine = bell_draw(seeds[2], (7, CH_FINE, CH_FINE), (7 * CH_FINE) ** -0.5, 0.25)
    w_down = bell_draw(seeds[3], (8 * CH_FINE, CH_POOL), (8 * CH_FINE) ** -0.5, 0.25)
    w_lift = bell_draw(seeds[4], (CH_POOL, CH_COARSE), CH_POOL ** -0.5, 0.375)
    coarse_nbrs = draw_coarse_nbrs(jax.random.fold_in(seeds[10], 71), 0)
    w_coarse = bell_draw(seeds[6], (7, CH_COARSE, CH_COARSE), (7 * CH_COARSE) ** -0.5, 0.09375)
    w_back = bell_draw(seeds[7], (CH_COARSE, CH_POOL), CH_COARSE ** -0.5, 0.25)
    w_up = bell_draw(seeds[8], (CH_POOL, 8 * CH_FINE), CH_POOL ** -0.5, 0.375)
    grad_out = draw_grad_out(jax.random.fold_in(seeds[10], 71), 0)
    return {"feats": feats, "neighbours": neighbours, "w_fine": w_fine, "w_down": w_down, "w_lift": w_lift, "coarse_nbrs": coarse_nbrs, "w_coarse": w_coarse, "w_back": w_back, "w_up": w_up, "grad_out": grad_out}


def split_faces(voxels):
    return jnp.stack([voxels[:, -1], voxels[:, 0], voxels[:, :, -1], voxels[:, :, 0], voxels[:, :, :, -1], voxels[:, :, :, 0]], axis=1)


def shifted_copies(voxels, rim_values):
    return [voxels,
            jnp.concatenate([voxels[:, 1:], rim_values[:, 0][:, None]], axis=1),
            jnp.concatenate([rim_values[:, 1][:, None], voxels[:, :-1]], axis=1),
            jnp.concatenate([voxels[:, :, 1:], rim_values[:, 2][:, :, None]], axis=2),
            jnp.concatenate([rim_values[:, 3][:, :, None], voxels[:, :, :-1]], axis=2),
            jnp.concatenate([voxels[:, :, :, 1:], rim_values[:, 4][:, :, :, None]], axis=3),
            jnp.concatenate([rim_values[:, 5][:, :, :, None], voxels[:, :, :, :-1]], axis=3)]


def spread_back(terms):
    inner = terms[0]
    inner = inner + jnp.concatenate([jnp.zeros_like(terms[1][:, :1]), terms[1][:, :-1]], axis=1)
    inner = inner + jnp.concatenate([terms[2][:, 1:], jnp.zeros_like(terms[2][:, :1])], axis=1)
    inner = inner + jnp.concatenate([jnp.zeros_like(terms[3][:, :, :1]), terms[3][:, :, :-1]], axis=2)
    inner = inner + jnp.concatenate([terms[4][:, :, 1:], jnp.zeros_like(terms[4][:, :, :1])], axis=2)
    inner = inner + jnp.concatenate([jnp.zeros_like(terms[5][:, :, :, :1]), terms[5][:, :, :, :-1]], axis=3)
    inner = inner + jnp.concatenate([terms[6][:, :, :, 1:], jnp.zeros_like(terms[6][:, :, :, :1])], axis=3)
    border = jnp.stack([terms[1][:, -1], terms[2][:, 0], terms[3][:, :, -1], terms[4][:, :, 0], terms[5][:, :, :, -1], terms[6][:, :, :, 0]], axis=1)
    return inner, border


def add_faces(total, face_grads):
    total = total.at[:, -1].add(face_grads[:, 0])
    total = total.at[:, 0].add(face_grads[:, 1])
    total = total.at[:, :, -1].add(face_grads[:, 2])
    total = total.at[:, :, 0].add(face_grads[:, 3])
    total = total.at[:, :, :, -1].add(face_grads[:, 4])
    total = total.at[:, :, :, 0].add(face_grads[:, 5])
    return total


def to_pooled(voxels):
    bricks_here = voxels.shape[0]
    half_side = voxels.shape[1] // 2
    channels = voxels.shape[-1]
    shaped = voxels.reshape(bricks_here, half_side, 2, half_side, 2, half_side, 2, channels)
    return shaped.transpose(0, 1, 3, 5, 2, 4, 6, 7).reshape(bricks_here, half_side ** 3, 8 * channels)


def from_pooled(values, channels):
    bricks_here = values.shape[0]
    half_side = round_cube(values.shape[1])
    shaped = values.reshape(bricks_here, half_side, half_side, half_side, 2, 2, 2, channels)
    return shaped.transpose(0, 1, 4, 2, 5, 3, 6, 7).reshape(bricks_here, 2 * half_side, 2 * half_side, 2 * half_side, channels)


def round_cube(volume):
    edge = 1
    while edge * edge * edge < volume:
        edge = edge + 1
    return edge


def silu_slope(value):
    logistic = jax.nn.sigmoid(value)
    return logistic * (1.0 + value * (1.0 - logistic))


def fine_front(voxels, rim_values, w_fine, w_down):
    bricks_here = voxels.shape[0]
    channels = voxels.shape[-1]
    shifted = shifted_copies(voxels, rim_values)
    conv_pre = jnp.zeros(voxels.shape, jnp.float32)
    for tap_index in range(7):
        product = jnp.dot(shifted[tap_index].reshape(-1, channels), w_fine[tap_index], preferred_element_type=jnp.float32)
        conv_pre = conv_pre + product.reshape(voxels.shape)
    hidden = jax.nn.silu(conv_pre).astype(jnp.bfloat16)
    hidden_pooled = to_pooled(hidden)
    pool_pre = jnp.dot(hidden_pooled.reshape(-1, hidden_pooled.shape[-1]), w_down, preferred_element_type=jnp.float32)
    pool_pre = pool_pre.reshape(bricks_here, hidden_pooled.shape[1], -1)
    pooled = jax.nn.silu(pool_pre).astype(jnp.bfloat16)
    return shifted, conv_pre, hidden, hidden_pooled, pool_pre, pooled


def fine_back(voxels, grad_vox, grad_merged, front, back_nodes, mean_grad, w_fine, w_down, w_up):
    shifted, conv_pre, hidden, hidden_pooled, pool_pre, pooled = front
    bricks_here = voxels.shape[0]
    channels = voxels.shape[-1]
    pool_voxels = pooled.shape[1]
    ch_pool = pooled.shape[-1]
    back_rows = jnp.repeat(back_nodes, 8, axis=0)[:, None, :]
    merged = (pooled.astype(jnp.float32) + back_rows).astype(jnp.bfloat16)
    merged_flat = merged.reshape(-1, ch_pool)
    lifted = jnp.dot(merged_flat, w_up, preferred_element_type=jnp.float32).reshape(bricks_here, pool_voxels, -1)
    fine_out = (voxels.astype(jnp.float32) + hidden.astype(jnp.float32) + from_pooled(lifted, channels)).astype(jnp.bfloat16)
    grad_rows = to_pooled(grad_vox).reshape(-1, w_up.shape[1])
    up_grad = jnp.dot(merged_flat.T, grad_rows, preferred_element_type=jnp.float32)
    mean_rows = jnp.repeat(mean_grad, 8, axis=0)[:, None, :] / (8.0 * pool_voxels)
    grad_pool = grad_merged.reshape(bricks_here, pool_voxels, ch_pool) + mean_rows
    pool_dpre = (grad_pool * silu_slope(pool_pre)).astype(jnp.bfloat16).reshape(-1, ch_pool)
    down_grad = jnp.dot(hidden_pooled.reshape(-1, hidden_pooled.shape[-1]).T, pool_dpre, preferred_element_type=jnp.float32)
    hidden_back = jnp.dot(pool_dpre, w_down.T, preferred_element_type=jnp.float32).reshape(bricks_here, pool_voxels, -1)
    grad_hidden = grad_vox.astype(jnp.float32) + from_pooled(hidden_back, channels)
    conv_dpre = (grad_hidden * silu_slope(conv_pre)).astype(jnp.bfloat16)
    flat_grad = conv_dpre.reshape(-1, channels)
    fine_grad = jnp.stack([jnp.dot(shifted[tap_index].reshape(-1, channels).T, flat_grad, preferred_element_type=jnp.float32) for tap_index in range(7)])
    terms = [jnp.dot(flat_grad, w_fine[tap_index].T, preferred_element_type=jnp.float32).reshape(voxels.shape) for tap_index in range(7)]
    inner, border = spread_back(terms)
    return fine_out, grad_vox.astype(jnp.float32) + inner, border.astype(jnp.bfloat16), fine_grad, down_grad, up_grad


def coarse_level(coarse_in, node_grad, coarse_nbrs, w_coarse, w_back):
    nodes_all = coarse_in.shape[0]
    width = coarse_in.shape[1]
    rows = jnp.where(coarse_nbrs >= 0, coarse_nbrs, nodes_all).astype(jnp.int32)
    padded = jnp.concatenate([coarse_in, jnp.zeros((1, width), coarse_in.dtype)], axis=0)
    inputs = [coarse_in] + [padded[rows[:, direction]] for direction in range(6)]
    coarse_pre = jnp.zeros((nodes_all, width), jnp.float32)
    for tap_index in range(7):
        coarse_pre = coarse_pre + jnp.dot(inputs[tap_index], w_coarse[tap_index], preferred_element_type=jnp.float32)
    coarse_out = jax.nn.silu(coarse_pre).astype(jnp.bfloat16)
    back = jnp.dot(coarse_out, w_back, preferred_element_type=jnp.float32)
    back_grad = jnp.dot(coarse_out.T, node_grad, preferred_element_type=jnp.float32)
    coarse_dout = jnp.dot(node_grad, w_back.T, preferred_element_type=jnp.float32)
    coarse_dpre = (coarse_dout * silu_slope(coarse_pre)).astype(jnp.bfloat16)
    coarse_grad = jnp.stack([jnp.dot(inputs[tap_index].T, coarse_dpre, preferred_element_type=jnp.float32) for tap_index in range(7)])
    input_grad = jnp.dot(coarse_dpre, w_coarse[0].T, preferred_element_type=jnp.float32)
    for direction in range(6):
        contrib = jnp.dot(coarse_dpre, w_coarse[direction + 1].T, preferred_element_type=jnp.float32)
        input_grad = input_grad + jnp.zeros((nodes_all + 1, width), jnp.float32).at[rows[:, direction]].add(contrib)[:nodes_all]
    return back, back_grad, coarse_grad, input_grad.astype(jnp.bfloat16)


def reference(feats, neighbours, w_fine, w_down, w_lift, coarse_nbrs, w_coarse, w_back, w_up, grad_out):
    block = BRICKS_DEV
    blocks = BRICKS // BRICKS_DEV
    shape_vox = (BRICKS, SIDE, SIDE, SIDE, CH_FINE)
    voxels_all = feats.reshape(shape_vox)
    grads_all = grad_out.reshape(shape_vox)
    width = SIDE * SIDE * CH_FINE
    faces_all = split_faces(voxels_all).reshape(BRICKS * 6, width)
    faces_pad = jnp.concatenate([faces_all, jnp.zeros((1, width), faces_all.dtype)], axis=0)
    flipped = jnp.array([1, 0, 3, 2, 5, 4], jnp.int32)
    rows = jnp.where(neighbours >= 0, neighbours * 6 + flipped[None, :], BRICKS * 6).astype(jnp.int32)

    def block_inputs(block_id):
        anchor = (block_id * block).astype(jnp.int32)
        voxels = lax.dynamic_slice_in_dim(voxels_all, anchor, block, 0)
        grad_vox = lax.dynamic_slice_in_dim(grads_all, anchor, block, 0)
        rows_here = lax.dynamic_slice_in_dim(rows, anchor, block, 0)
        rim_values = faces_pad[rows_here.reshape(-1)].reshape(block, 6, SIDE, SIDE, CH_FINE)
        front = fine_front(voxels, rim_values, w_fine, w_down)
        grad_rows = to_pooled(grad_vox).reshape(-1, w_up.shape[1])
        grad_merged = jnp.dot(grad_rows, w_up.T, preferred_element_type=jnp.float32)
        return voxels, grad_vox, grad_merged, front

    def first_pass(block_id):
        voxels, grad_vox, grad_merged, front = block_inputs(block_id)
        pooled = front[5]
        means = pooled.astype(jnp.float32).reshape(block // 8, -1, CH_POOL).mean(axis=1)
        node_sums = grad_merged.reshape(block // 8, -1, CH_POOL).sum(axis=1)
        return means, node_sums

    means, node_sums = lax.map(first_pass, jnp.arange(blocks, dtype=jnp.int32))
    node_mean = means.reshape(NODES, CH_POOL).astype(jnp.bfloat16)
    node_grad = node_sums.reshape(NODES, CH_POOL).astype(jnp.bfloat16)
    coarse_in = jnp.dot(node_mean, w_lift, preferred_element_type=jnp.float32).astype(jnp.bfloat16)
    back, back_grad, coarse_grad, coarse_in_grad = coarse_level(coarse_in, node_grad, coarse_nbrs, w_coarse, w_back)
    lift_grad = jnp.dot(node_mean.T, coarse_in_grad, preferred_element_type=jnp.float32)
    mean_grad = jnp.dot(coarse_in_grad, w_lift.T, preferred_element_type=jnp.float32)

    def second_pass(carry, block_id):
        voxels, grad_vox, grad_merged, front = block_inputs(block_id)
        node_anchor = (block_id * (block // 8)).astype(jnp.int32)
        back_nodes = lax.dynamic_slice_in_dim(back, node_anchor, block // 8, 0)
        mean_nodes = lax.dynamic_slice_in_dim(mean_grad, node_anchor, block // 8, 0)
        result = fine_back(voxels, grad_vox, grad_merged, front, back_nodes, mean_nodes, w_fine, w_down, w_up)
        fine_out, inner, border, fine_grad, down_grad, up_grad = result
        carry = (carry[0] + fine_grad, carry[1] + down_grad, carry[2] + up_grad)
        return carry, (fine_out, inner, border)

    start = (jnp.zeros(w_fine.shape, jnp.float32), jnp.zeros(w_down.shape, jnp.float32), jnp.zeros(w_up.shape, jnp.float32))
    sums, outputs = lax.scan(second_pass, start, jnp.arange(blocks, dtype=jnp.int32))
    fine_out = outputs[0].reshape(BRICKS, SIDE, SIDE, SIDE * CH_FINE)
    inner = outputs[1].reshape(shape_vox)
    border = outputs[2].reshape(BRICKS * 6, width).astype(jnp.float32)
    face_grads = jnp.zeros((BRICKS * 6 + 1, width), jnp.float32).at[rows.reshape(-1)].add(border)[:BRICKS * 6]
    total = add_faces(inner, face_grads.reshape(BRICKS, 6, SIDE, SIDE, CH_FINE))
    feats_grad = total.astype(jnp.bfloat16).reshape(BRICKS, SIDE, SIDE, SIDE * CH_FINE)
    return fine_out, feats_grad, sums[0], sums[1], lift_grad, coarse_grad, back_grad, sums[2]
```

```python
import functools

import jax
import jax.numpy as jnp
from jax import lax
from jax.experimental import pallas as pl
from jax.experimental.pallas import tpu as pltpu
from jax.sharding import PartitionSpec as P

F32 = jnp.float32
BF16 = jnp.bfloat16
MESH = pl.DeviceIdType.MESH
VMEM_LIMIT = 56 * 1024 * 1024
OFFSETS = (-2, -1, 1, 2)
SLOTS = 6
ENTRIES = 48
REMOTE = len(OFFSETS) * SLOTS
TABLE = ENTRIES + REMOTE + 1


def dot(x, y):
    return jnp.dot(x, y, preferred_element_type=F32)


def dot_nt(x, y):
    return lax.dot_general(x, y, (((1,), (1,)), ((), ())), preferred_element_type=F32)


def dot_tn(x, y):
    return lax.dot_general(x, y, (((0,), (0,)), ((), ())), preferred_element_type=F32)


def sigmoid(v):
    return 1.0 / (1.0 + jnp.exp(-v))


def perm_index(y):
    a, e = (y >> 8) & 1, (y >> 7) & 1
    u, w, b = (y >> 5) & 3, (y >> 3) & 3, y & 7
    return b * 64 + (2 * u + a) * 8 + 2 * w + e


def perm_to():
    rows = lax.broadcasted_iota(jnp.int32, (512, 512), 0)
    cols = lax.broadcasted_iota(jnp.int32, (512, 512), 1)
    return (perm_index(rows) == cols).astype(F32).astype(BF16)


def perm_from():
    rows = lax.broadcasted_iota(jnp.int32, (512, 512), 0)
    cols = lax.broadcasted_iota(jnp.int32, (512, 512), 1)
    return (perm_index(cols) == rows).astype(F32).astype(BF16)


def load_natural(ref):
    return ref[...].astype(F32).reshape(512, 512).astype(BF16)


def pooled_rows(x, perm, out_ref, wide_ref=None):
    y = dot(perm, x)
    for z in range(4):
        for ae in range(4):
            block = y[ae * 128 : (ae + 1) * 128, z * 128 : (z + 1) * 128]
            where = (pl.ds(z * 128, 128), pl.ds(ae * 128, 128))
            out_ref[where] = block.astype(BF16)
            if wide_ref is not None:
                wide_ref[where] = block


def natural_rows(q, perm_back):
    y = jnp.concatenate(
        [
            jnp.concatenate(
                [q[z * 128 : (z + 1) * 128, ae * 128 : (ae + 1) * 128] for z in range(4)], axis=1
            )
            for ae in range(4)
        ],
        axis=0,
    )
    return dot(perm_back, y).reshape(64, 8, 512).astype(BF16)


def low_lanes(rows):
    return lax.broadcasted_iota(jnp.int32, (rows, 128), 1) < 64


def layer(ref, axis, place, parity):
    if axis == 0:
        return jnp.concatenate(
            [
                ref[z * 128 + place * 32 : z * 128 + place * 32 + 32, parity * 256 : parity * 256 + 256]
                for z in range(4)
            ],
            axis=0,
        )
    if axis == 1:
        parts = []
        for a in range(2):
            lane = (a * 2 + parity) * 128
            parts.append(
                jnp.concatenate(
                    [ref[zu * 32 + place * 8 : zu * 32 + place * 8 + 8, lane : lane + 128] for zu in range(16)],
                    axis=0,
                )
            )
        return jnp.concatenate(parts, axis=1)
    parts = []
    for a in range(2):
        first = ref[place * 128 : place * 128 + 128, a * 256 : a * 256 + 128]
        second = ref[place * 128 : place * 128 + 128, a * 256 + 128 : a * 256 + 256]
        if parity == 0:
            second = pltpu.roll(second, 64, 1)
        else:
            first = pltpu.roll(first, 64, 1)
        parts.append(jnp.where(low_lanes(128), first, second))
    return jnp.concatenate(parts, axis=1)


def add_layer(ref, axis, place, parity, value):
    if axis == 0:
        for z in range(4):
            rows = pl.ds(z * 128 + place * 32, 32)
            ref[rows, parity * 256 : parity * 256 + 256] += value[z * 32 : z * 32 + 32]
    elif axis == 1:
        for a in range(2):
            lane = (a * 2 + parity) * 128
            for zu in range(16):
                rows = pl.ds(zu * 32 + place * 8, 8)
                ref[rows, lane : lane + 128] += value[zu * 8 : zu * 8 + 8, a * 128 : a * 128 + 128]
    else:
        low = low_lanes(128)
        rows = pl.ds(place * 128, 128)
        for a in range(2):
            part = value[:, a * 128 : a * 128 + 128]
            turned = pltpu.roll(part, 64, 1)
            first, second = (part, turned) if parity == 0 else (turned, part)
            keep = low if parity == 0 else ~low
            ref[rows, a * 256 : a * 256 + 128] += jnp.where(keep, first, 0.0)
            ref[rows, a * 256 + 128 : a * 256 + 256] += jnp.where(keep, second, 0.0)


def brick_faces(value, stage, out_ref, which):
    for half in range(2):
        lanes = slice(half * 128, half * 128 + 128)
        stage[half] = value[:, lanes]
        for b in range(8):
            out_ref[b * 6 + which, :, lanes] = stage[half, pl.ds(b, 16, stride=8), :].astype(BF16)


FACES = ((0, 3, 1), (0, 0, 0), (1, 3, 1), (1, 0, 0), (2, 3, 1), (2, 0, 0))
BEYOND = ((0, 3, 0), (0, 0, 1), (1, 3, 0), (1, 0, 1), (2, 3, 0), (2, 0, 1))


def prepare_kernel(nodes, feats, grad, neighbours, q_out, g_out, faces, rows_of, wanted, entry_of, wide, stage):
    subs = lax.axis_size("sub")
    me = lax.axis_index("grp") * subs + lax.axis_index("sub")
    for place in range(len(OFFSETS)):
        for slot in range(8):
            wanted[place, 0, slot] = ENTRIES
            entry_of[place, slot] = ENTRIES

    def one(entry, counts):
        n = neighbours[entry // 6, entry % 6]
        face = lax.bitwise_xor(entry % 6, 1)
        offset = (n >> 3) - me
        row = (n & 7) * 6 + face
        present = n >= 0
        result = []
        rows_of[entry] = jnp.where(present, row, TABLE - 1)
        for place, off in enumerate(OFFSETS):
            hit = present & (offset == off)
            count = counts[place]

            @pl.when(hit)
            def _(place=place, count=count):
                wanted[place, 0, count] = row
                entry_of[place, count] = entry
                rows_of[entry] = ENTRIES + place * SLOTS + count

            result.append(count + hit.astype(jnp.int32))
        return tuple(result)

    lax.fori_loop(0, ENTRIES, one, (jnp.int32(0),) * 4)
    perm = perm_to()
    pooled_rows(load_natural(feats), perm, q_out, wide)
    pooled_rows(load_natural(grad), perm, g_out)
    for f, (axis, place, parity) in enumerate(FACES):
        brick_faces(layer(wide, axis, place, parity), stage, faces, f)


def coords(groups, subs, offset):
    nodes = groups * subs
    at = lax.axis_index("grp") * subs + lax.axis_index("sub")
    to = lax.rem(at + offset + nodes, nodes)
    return (to // subs, lax.rem(to, subs))


def halo_kernel(groups, subs, faces, wanted, table, asked, numbers, send, sems_a, sems_b, sem_c):
    barrier = pltpu.get_barrier_semaphore()
    peers = [coords(groups, subs, off) for off in OFFSETS]
    for peer in peers:
        pl.semaphore_signal(barrier, inc=1, device_id=peer, device_id_type=MESH)
    pl.semaphore_wait(barrier, len(OFFSETS))
    copies = []
    for p in range(4):
        copy = pltpu.make_async_remote_copy(
            src_ref=wanted.at[p],
            dst_ref=asked.at[3 - p],
            send_sem=sems_a.at[0, p],
            recv_sem=sems_a.at[1, 3 - p],
            device_id=peers[p],
            device_id_type=MESH,
        )
        copy.start()
        copies.append(copy)
    table[0:ENTRIES] = faces[...]
    table[TABLE - 1] = jnp.zeros((16, 256), BF16)
    for copy in copies:
        copy.wait()
    local = pltpu.make_async_copy(asked, numbers, sem_c)
    local.start()
    local.wait()
    copies = []
    for p in range(4):
        for s in range(SLOTS):
            row = jnp.minimum(numbers[p, 0, s], ENTRIES - 1)
            send[p, s] = faces[row]
        copy = pltpu.make_async_remote_copy(
            src_ref=send.at[p],
            dst_ref=table.at[pl.ds(ENTRIES + (3 - p) * SLOTS, SLOTS)],
            send_sem=sems_b.at[0, p],
            recv_sem=sems_b.at[1, 3 - p],
            device_id=peers[p],
            device_id_type=MESH,
        )
        copy.start()
        copies.append(copy)
    for copy in copies:
        copy.wait()


def build_mats(wm, m0, mx, my, mz):
    zero = jnp.zeros((128, 128), BF16)

    def put(ref, i, j, value):
        ref[i * 128 : (i + 1) * 128, j * 128 : (j + 1) * 128] = value

    c, d1, d2, d3, d4, ez = (wm[i] for i in range(6))
    for a in range(2):
        for e in range(2):
            i = a * 2 + e
            put(m0, i, i, c)
            put(m0, i, (1 - a) * 2 + e, d1 if a == 1 else d2)
            put(m0, i, a * 2 + (1 - e), d3 if e == 1 else d4)
            put(m0, i, 3 - i, zero)
    for i in range(2):
        for j in range(2):
            put(mx.at[0], i, j, d1 if i == j else zero)
            put(mx.at[1], i, j, d2 if i == j else zero)
            put(mz, i, j, ez if i == j else zero)
    put(my, 0, 0, zero)
    put(my, 1, 1, zero)
    put(my, 0, 1, d3)
    put(my, 1, 0, d4)


def forward_kernel(
    rows_of, table, q, g, wm, w_down, w_up,
    sx, sy, sz, hidden, slope, pooled, pool_slope, grad_merged, node,
    rim, m0, mx, my, mz,
):
    for d in range(6):
        for b in range(8):
            face = table[rows_of[b * 6 + d]].astype(F32)
            rim[d, 0, pl.ds(b, 16, stride=8), :] = face[:, 0:128]
            rim[d, 1, pl.ds(b, 16, stride=8), :] = face[:, 128:256]
    build_mats(wm, m0, mx, my, mz)
    for z in range(4):
        at = z * 128
        sx[at : at + 96, 0:256] = q[at + 32 : at + 128, 0:256]
        for half in range(2):
            low, high = slice(half * 128, half * 128 + 128), slice(half * 128 + 256, half * 128 + 384)
            sx[at + 96 : at + 128, low] = rim[0, half, z * 32 : z * 32 + 32, :].astype(BF16)
            sx[at : at + 32, high] = rim[1, half, z * 32 : z * 32 + 32, :].astype(BF16)
        sx[at + 32 : at + 128, 256:512] = q[at : at + 96, 256:512]
    for a in range(2):
        lanes = slice(a * 256, a * 256 + 128)
        part = q[:, lanes].astype(F32).reshape(16, 32, 128)
        edge = rim[2, a].reshape(16, 8, 128)
        sy[:, lanes] = jnp.concatenate([part[:, 8:], edge], axis=1).reshape(512, 128).astype(BF16)
        lanes = slice(a * 256 + 128, a * 256 + 256)
        part = q[:, lanes].astype(F32).reshape(16, 32, 128)
        edge = rim[3, a].reshape(16, 8, 128)
        sy[:, lanes] = jnp.concatenate([edge, part[:, :24]], axis=1).reshape(512, 128).astype(BF16)
    low = low_lanes(512)
    for a in range(2):
        above = rim[4, a]
        below = rim[5, a]
        for e in range(2):
            lanes = slice((a * 2 + e) * 128, (a * 2 + e) * 128 + 128)
            part = q[:, lanes].astype(F32)
            edge_up = above if e == 0 else pltpu.roll(above, 64, 1)
            edge_down = pltpu.roll(below, 64, 1) if e == 0 else below
            up = jnp.concatenate([part[128:], edge_up], axis=0)
            down = jnp.concatenate([edge_down, part[:384]], axis=0)
            sz[:, lanes] = jnp.where(low, up, down).astype(BF16)
    base = dot(q[...], m0[...])
    for a in range(2):
        lanes = slice(a * 256, a * 256 + 256)
        other = slice(256 - a * 256, 512 - a * 256)
        pre = (
            base[:, lanes]
            + dot(sx[:, other], mx[1 - a])
            + dot(sy[:, lanes], my[...])
            + dot(sz[:, lanes], mz[...])
        )
        s = sigmoid(pre)
        hidden[:, lanes] = (pre * s).astype(BF16)
        slope[:, lanes] = s * (1.0 + pre * (1.0 - s))
    pre = dot(hidden[...], w_down[...])
    s = sigmoid(pre)
    value = (pre * s).astype(BF16)
    pooled[...] = value
    pool_slope[...] = s * (1.0 + pre * (1.0 - s))
    mean = jnp.sum(value.astype(F32), axis=0, keepdims=True) * (1.0 / 512.0)
    merged_grad = dot_nt(g[...], w_up[...])
    grad_merged[...] = merged_grad
    total = jnp.sum(merged_grad, axis=0, keepdims=True)
    mean = mean.astype(BF16).astype(F32)
    total = total.astype(BF16).astype(F32)
    for half in range(2):
        node[half : half + 1, :] = mean[:, half * 128 : half * 128 + 128]
        node[2 + half : 3 + half, :] = total[:, half * 128 : half * 128 + 128]


def gather_kernel(groups, subs, node, slab, first, pack, sems_a, sems_b):
    g, s = lax.axis_index("grp"), lax.axis_index("sub")
    barrier = pltpu.get_barrier_semaphore()
    over_grp = [(lax.rem(g + k, groups), s) for k in range(1, groups)]
    over_sub = [(g, lax.rem(s + k, subs)) for k in range(1, subs)]
    for peer in over_grp + over_sub:
        pl.semaphore_signal(barrier, inc=1, device_id=peer, device_id_type=MESH)
    pl.semaphore_wait(barrier, len(over_grp) + len(over_sub))
    copies = []
    for k, peer in enumerate(over_grp):
        copy = pltpu.make_async_remote_copy(
            src_ref=node,
            dst_ref=first.at[g],
            send_sem=sems_a.at[0, k],
            recv_sem=sems_a.at[1, k],
            device_id=peer,
            device_id_type=MESH,
        )
        copy.start()
        copies.append(copy)
    first[g] = node[...]
    for copy in copies:
        copy.wait()
    for i in range(groups):
        pack[4 * i : 4 * i + 4, :] = first[i]
    slab[s] = pack[...].astype(BF16)
    copies = []
    for k, peer in enumerate(over_sub):
        copy = pltpu.make_async_remote_copy(
            src_ref=slab.at[s],
            dst_ref=slab.at[s],
            send_sem=sems_b.at[0, k],
            recv_sem=sems_b.at[1, k],
            device_id=peer,
            device_id_type=MESH,
        )
        copy.start()
        copies.append(copy)
    for copy in copies:
        copy.wait()


def backward_kernel(
    groups, subs,
    entry_of, slab, nbrs, w_lift, w_coarse, w_back, w_up, w_down, wm,
    q, g, sx, sy, sz, hidden, slope, pooled, pool_slope, grad_merged,
    fine_out, w_lift_grad, w_coarse_grad, w_back_grad, parts, inner, border, send,
    m0, mx, my, mz, wide, flat, stage, taps, backs, coarse_sum, sem,
):
    nodes = groups * subs
    me = lax.axis_index("grp") * subs + lax.axis_index("sub")
    wide_slab = flat
    for s in range(subs):
        wide_slab[s * groups * 4 : (s + 1) * groups * 4, :] = slab[s].astype(F32)
    pieces = [wide_slab[pl.ds(k, nodes, stride=4), :] for k in range(4)]
    rows = lax.broadcasted_iota(jnp.int32, (nodes, nodes), 0)
    cols = lax.broadcasted_iota(jnp.int32, (nodes, nodes), 1)
    order = (lax.rem(rows, subs) * groups + rows // subs == cols).astype(F32).astype(BF16)
    gathered = dot(order, jnp.concatenate(pieces, axis=1).astype(BF16)).astype(BF16)
    node_mean, node_grad = gathered[:, :256], gathered[:, 256:]
    coarse_in = dot(node_mean, w_lift[...]).astype(BF16)
    picks = []
    taps[:, 0:512] = coarse_in
    for d in range(6):
        pick = (nbrs[:, d : d + 1] == cols).astype(F32).astype(BF16)
        picks.append(pick)
        taps[:, (d + 1) * 512 : (d + 2) * 512] = dot(pick, coarse_in).astype(BF16)
    coarse_pre = jnp.zeros((nodes, 512), F32)
    for t in range(7):
        coarse_pre = coarse_pre + dot(taps[:, t * 512 : (t + 1) * 512], w_coarse[t])
    s = sigmoid(coarse_pre)
    coarse_out = (coarse_pre * s).astype(BF16)
    coarse_slope = s * (1.0 + coarse_pre * (1.0 - s))
    mine = (lax.broadcasted_iota(jnp.int32, (16, nodes), 1) == me).astype(F32).astype(BF16)
    back = dot(dot(mine, coarse_out).astype(BF16), w_back[...])[0:1]
    w_back_grad[...] = dot_tn(coarse_out, node_grad)
    dpre = (dot_nt(node_grad, w_back[...]) * coarse_slope).astype(BF16)
    in_grad = dot_nt(dpre, w_coarse[0])
    for d in range(6):
        moved = dot_tn(picks[d], dpre).astype(BF16)
        in_grad = in_grad + dot_nt(moved, w_coarse[d + 1])
    in_grad = in_grad.astype(BF16)
    copies = []
    for t in range(7):
        coarse_sum[t] = dot_tn(taps[:, t * 512 : (t + 1) * 512], dpre)
        copy = pltpu.make_async_copy(coarse_sum.at[t], w_coarse_grad.at[t], sem.at[t])
        copy.start()
        copies.append(copy)
    w_lift_grad[...] = dot_tn(node_mean, in_grad)
    mean_grad = dot_nt(dot(mine, in_grad).astype(BF16), w_lift[...])[0:1] * (1.0 / 512.0)

    build_mats(wm, m0, mx, my, mz)
    merged = (pooled[...].astype(F32) + back).astype(BF16)
    out = q[...].astype(F32) + hidden[...].astype(F32) + dot(merged, w_up[...])
    fine_out[...] = natural_rows(out.astype(BF16), perm_from())
    up_part = dot_tn(merged, g[...])
    pool_dpre = ((grad_merged[...] + mean_grad) * pool_slope[...]).astype(BF16)
    down_part = dot_tn(hidden[...], pool_dpre)
    conv_dpre = ((g[...].astype(F32) + dot_nt(pool_dpre, w_down[...])) * slope[...]).astype(BF16)

    up_rows, down_rows, fine_rows = 256 // subs, 512 // subs, 256 // subs
    for i in range(subs):
        for k in range(4):
            parts[i, k * up_rows : (k + 1) * up_rows, :] = up_part[
                i * up_rows : (i + 1) * up_rows, k * 128 : (k + 1) * 128
            ].astype(BF16)
        at = 4 * up_rows
        for k in range(2):
            parts[i, at + k * down_rows : at + (k + 1) * down_rows, :] = down_part[
                i * down_rows : (i + 1) * down_rows, k * 128 : (k + 1) * 128
            ].astype(BF16)

    def block(value, i, j):
        return value[i * 128 : (i + 1) * 128, j * 128 : (j + 1) * 128]

    def fold(value):
        return value[:64] + pltpu.roll(value[64:], 64, 1)

    centre = dot_tn(q[...], conv_dpre)
    gx0 = dot_tn(sx[:, 0:256], conv_dpre[:, 256:512])
    gx1 = dot_tn(sx[:, 256:512], conv_dpre[:, 0:256])
    gy = [dot_tn(sy[:, a * 256 : a * 256 + 256], conv_dpre[:, a * 256 : a * 256 + 256]) for a in range(2)]
    gz = [dot_tn(sz[:, a * 256 : a * 256 + 256], conv_dpre[:, a * 256 : a * 256 + 256]) for a in range(2)]
    middle = sum(block(centre, i, i) for i in range(4))
    x_up = block(centre, 2, 0) + block(centre, 3, 1) + block(gx0, 0, 0) + block(gx0, 1, 1)
    x_down = block(centre, 0, 2) + block(centre, 1, 3) + block(gx1, 0, 0) + block(gx1, 1, 1)
    y_up = block(centre, 1, 0) + block(centre, 3, 2) + block(gy[0], 0, 1) + block(gy[1], 0, 1)
    y_down = block(centre, 0, 1) + block(centre, 2, 3) + block(gy[0], 1, 0) + block(gy[1], 1, 0)
    between = sum(block(value, i, i) for value in gz for i in range(2))
    z_up = middle[64:] + pltpu.roll(between[:64], 64, 1)
    z_down = pltpu.roll(middle[:64], 64, 1) + between[64:]
    tap_sums = [fold(middle), fold(x_up), fold(x_down), fold(y_up), fold(y_down), z_up, z_down]
    tap_sums.append(jnp.zeros((64, 128), F32))
    low = low_lanes(64)
    for pair in range(4):
        both = jnp.where(low, tap_sums[2 * pair], pltpu.roll(tap_sums[2 * pair + 1], 64, 1))
        for i in range(64 // fine_rows):
            at = 4 * up_rows + 2 * down_rows
            parts[pair * (64 // fine_rows) + i, at : at + fine_rows, :] = both[
                i * fine_rows : (i + 1) * fine_rows
            ].astype(BF16)

    inner[...] = g[...].astype(F32) + dot_nt(conv_dpre, m0[...])

    def take(d):
        axis, place, parity = BEYOND[d]
        brick_faces(layer(wide, axis, place, parity), stage, border, d)

    wide[:, 0:256] = dot_nt(conv_dpre[:, 256:512], mx[0])
    wide[:, 256:512] = dot_nt(conv_dpre[:, 0:256], mx[1])
    for z in range(4):
        at = z * 128
        inner[at + 32 : at + 128, 0:256] += wide[at : at + 96, 0:256]
        inner[at : at + 96, 256:512] += wide[at + 32 : at + 128, 256:512]
    take(0)
    take(1)
    for a in range(2):
        wide[:, a * 256 : a * 256 + 256] = dot_nt(conv_dpre[:, a * 256 : a * 256 + 256], my[...])
    for zu in range(16):
        at = zu * 32
        for a in range(2):
            first, second = slice(a * 256, a * 256 + 128), slice(a * 256 + 128, a * 256 + 256)
            inner[at + 8 : at + 32, first] += wide[at : at + 24, first]
            inner[at : at + 24, second] += wide[at + 8 : at + 32, second]
    take(2)
    take(3)
    for a in range(2):
        wide[:, a * 256 : a * 256 + 256] = dot_nt(conv_dpre[:, a * 256 : a * 256 + 256], mz[...])
    low = low_lanes(384)
    for i in range(4):
        lanes = slice(i * 128, i * 128 + 128)
        inner[128:512, lanes] += jnp.where(low, wide[0:384, lanes], 0.0)
        inner[0:384, lanes] += jnp.where(low, 0.0, wide[128:512, lanes])
    take(4)
    take(5)
    border[ENTRIES] = jnp.zeros((16, 256), BF16)
    for p in range(4):
        for slot in range(SLOTS):
            send[p, slot] = border[entry_of[p, slot]]
    for copy in copies:
        copy.wait()


def exchange_kernel(groups, subs, parts, send, total, slabs, part_in, mine, second, second_in, sems_a, sems_b, sems_c, sems_d, sems_e):
    g, s = lax.axis_index("grp"), lax.axis_index("sub")
    near = [coords(groups, subs, off) for off in OFFSETS]
    over_grp = [(lax.rem(g + k, groups), s) for k in range(1, groups)]
    over_sub = [(g, lax.rem(s + k, subs)) for k in range(1, subs)]
    barrier = pltpu.get_barrier_semaphore()
    everyone = near + over_grp + over_sub
    for peer in everyone:
        pl.semaphore_signal(barrier, inc=1, device_id=peer, device_id_type=MESH)
    pl.semaphore_wait(barrier, len(everyone))
    chunk = parts.shape[1]
    fine_rows = 256 // subs
    wide_rows = chunk - fine_rows
    share = wide_rows // groups

    copies = []
    for k, peer in enumerate(over_sub):
        copy = pltpu.make_async_remote_copy(
            src_ref=parts.at[peer[1]],
            dst_ref=part_in.at[k],
            send_sem=sems_a.at[0, k],
            recv_sem=sems_a.at[1, k],
            device_id=peer,
            device_id_type=MESH,
        )
        copy.start()
        copies.append(copy)
    slab_copies = []
    for p in range(4):
        copy = pltpu.make_async_remote_copy(
            src_ref=send.at[p],
            dst_ref=slabs.at[3 - p],
            send_sem=sems_e.at[0, p],
            recv_sem=sems_e.at[1, 3 - p],
            device_id=near[p],
            device_id_type=MESH,
        )
        copy.start()
        slab_copies.append(copy)
    value = parts[s].astype(F32)
    for k, copy in enumerate(copies):
        copy.wait()
        value = value + part_in[k].astype(F32)
    for i in range(groups):
        second[i, 0:share, :] = value[i * share : (i + 1) * share].astype(BF16)
        second[i, share : share + fine_rows, :] = value[wide_rows:].astype(BF16)
    copies = []
    for k, peer in enumerate(over_grp):
        copy = pltpu.make_async_remote_copy(
            src_ref=second.at[peer[0]],
            dst_ref=second_in.at[k],
            send_sem=sems_b.at[0, k],
            recv_sem=sems_b.at[1, k],
            device_id=peer,
            device_id_type=MESH,
        )
        copy.start()
        copies.append(copy)
    value = second[g].astype(F32)
    for k, copy in enumerate(copies):
        copy.wait()
        value = value + second_in[k].astype(F32)
    mine[...] = value[0:share].astype(BF16)
    total[s, pl.ds(pl.multiple_of(g * share, share), share), :] = value[0:share].astype(BF16)
    total[s, wide_rows:chunk, :] = value[share:].astype(BF16)
    copies = []
    for k, peer in enumerate(over_grp):
        copy = pltpu.make_async_remote_copy(
            src_ref=mine,
            dst_ref=total.at[s, pl.ds(pl.multiple_of(g * share, share), share), :],
            send_sem=sems_c.at[0, k],
            recv_sem=sems_c.at[1, k],
            device_id=peer,
            device_id_type=MESH,
        )
        copy.start()
        copies.append(copy)
    for copy in copies:
        copy.wait()
    copies = []
    for k, peer in enumerate(over_sub):
        copy = pltpu.make_async_remote_copy(
            src_ref=total.at[s],
            dst_ref=total.at[s],
            send_sem=sems_d.at[0, k],
            recv_sem=sems_d.at[1, k],
            device_id=peer,
            device_id_type=MESH,
        )
        copy.start()
        copies.append(copy)
    for copy in copies:
        copy.wait()
    for copy in slab_copies:
        copy.wait()


def finish_kernel(subs, rows_of, asked, total, slabs, inner, border, feats_grad, w_fine_grad, w_down_grad, w_up_grad, faces, wide, stage):
    faces[...] = jnp.zeros_like(faces)

    def local(entry, carry):
        row = rows_of[entry]

        @pl.when(row < ENTRIES)
        def _():
            faces[row] += border[entry].astype(F32)

        return carry

    lax.fori_loop(0, ENTRIES, local, 0)
    for p in range(4):
        for slot in range(SLOTS):
            row = asked[p, 0, slot]
            faces[row] += slabs[p, slot].astype(F32)
    wide[...] = inner[...]
    for f, (axis, place, parity) in enumerate(FACES):
        for b in range(8):
            face = faces[b * 6 + f]
            stage[0, pl.ds(b, 16, stride=8), :] = face[:, 0:128]
            stage[1, pl.ds(b, 16, stride=8), :] = face[:, 128:256]
        add_layer(wide, axis, place, parity, jnp.concatenate([stage[0], stage[1]], axis=1))
    feats_grad[...] = natural_rows(wide[...].astype(BF16), perm_from())
    up_rows, down_rows, fine_rows = 256 // subs, 512 // subs, 256 // subs
    at = 4 * up_rows
    for i in range(subs):
        for k in range(4):
            w_up_grad[i * up_rows : (i + 1) * up_rows, k * 128 : (k + 1) * 128] = total[
                i, k * up_rows : (k + 1) * up_rows, :
            ].astype(F32)
        for k in range(2):
            w_down_grad[i * down_rows : (i + 1) * down_rows, k * 128 : (k + 1) * 128] = total[
                i, at + k * down_rows : at + (k + 1) * down_rows, :
            ].astype(F32)
    at = 4 * up_rows + 2 * down_rows
    for pair in range(4):
        both = jnp.concatenate(
            [total[pair * (64 // fine_rows) + i, at : at + fine_rows, :] for i in range(64 // fine_rows)], axis=0
        ).astype(F32)
        w_fine_grad[2 * pair] = both[:, 0:64]
        if pair < 3:
            w_fine_grad[2 * pair + 1] = pltpu.roll(both, 64, 1)[:, 0:64]


def spec(space=pltpu.VMEM):
    return pl.BlockSpec(memory_space=space)


def shape(dims, dtype):
    return jax.ShapeDtypeStruct(dims, dtype)


def body(groups, subs, feats, neighbours, w_fine, w_down, w_lift, coarse_nbrs, w_coarse, w_back, w_up, grad_out):
    nodes = groups * subs
    plain = pltpu.CompilerParams(vmem_limit_bytes=VMEM_LIMIT)

    def talks(number):
        return pltpu.CompilerParams(collective_id=number, has_side_effects=True, vmem_limit_bytes=VMEM_LIMIT)

    smem = spec(pltpu.SMEM)
    vmem = spec()
    pair = jnp.zeros((64, 64), BF16)
    doubled = [
        jnp.concatenate(
            [jnp.concatenate([w_fine[t], pair], axis=1), jnp.concatenate([pair, w_fine[t]], axis=1)], axis=0
        )
        for t in range(1, 5)
    ]
    middle = jnp.concatenate(
        [
            jnp.concatenate([w_fine[0], w_fine[6]], axis=1),
            jnp.concatenate([w_fine[5], w_fine[0]], axis=1),
        ],
        axis=0,
    )
    between = jnp.concatenate(
        [jnp.concatenate([pair, w_fine[5]], axis=1), jnp.concatenate([w_fine[6], pair], axis=1)], axis=0
    )
    wm = jnp.stack([middle] + doubled + [between])

    sq16, sq32 = shape((512, 512), BF16), shape((512, 512), F32)
    q, g, faces, rows_of, wanted, entry_of = pl.pallas_call(
        functools.partial(prepare_kernel, nodes),
        out_shape=(
            sq16,
            sq16,
            shape((ENTRIES, 16, 256), BF16),
            shape((ENTRIES,), jnp.int32),
            shape((4, 8, 128), jnp.int32),
            shape((4, 8), jnp.int32),
        ),
        in_specs=[vmem, vmem, smem],
        out_specs=(vmem, vmem, vmem, smem, smem, smem),
        scratch_shapes=[pltpu.VMEM((512, 512), F32), pltpu.VMEM((2, 128, 128), F32)],
        compiler_params=plain,
        name="prepare",
    )(feats.reshape(64, 8, 512), grad_out.reshape(64, 8, 512), neighbours)

    table, asked = pl.pallas_call(
        functools.partial(halo_kernel, groups, subs),
        out_shape=(shape((TABLE, 16, 256), BF16), shape((4, 8, 128), jnp.int32)),
        in_specs=[vmem, vmem],
        out_specs=(vmem, vmem),
        scratch_shapes=[
            pltpu.SMEM((4, 8, 128), jnp.int32),
            pltpu.VMEM((4, SLOTS, 16, 256), BF16),
            pltpu.SemaphoreType.DMA((2, 4)),
            pltpu.SemaphoreType.DMA((2, 4)),
            pltpu.SemaphoreType.DMA,
        ],
        compiler_params=talks(1),
        name="halo",
    )(faces, wanted)

    mats = [
        pltpu.VMEM((512, 512), BF16),
        pltpu.VMEM((2, 256, 256), BF16),
        pltpu.VMEM((256, 256), BF16),
        pltpu.VMEM((256, 256), BF16),
    ]
    sx, sy, sz, hidden, slope, pooled, pool_slope, grad_merged, node = pl.pallas_call(
        forward_kernel,
        out_shape=(
            sq16, sq16, sq16, sq16, sq32,
            shape((512, 256), BF16), shape((512, 256), F32), shape((512, 256), F32), shape((4, 128), F32),
        ),
        in_specs=[smem] + [vmem] * 6,
        out_specs=(vmem,) * 9,
        scratch_shapes=[pltpu.VMEM((6, 2, 128, 128), F32)] + mats,
        compiler_params=plain,
        name="forward",
    )(rows_of, table, q, g, wm, w_down, w_up)

    slab = pl.pallas_call(
        functools.partial(gather_kernel, groups, subs),
        out_shape=shape((subs, groups * 4, 128), BF16),
        in_specs=[vmem],
        out_specs=vmem,
        scratch_shapes=[
            pltpu.VMEM((groups, 4, 128), F32),
            pltpu.VMEM((groups * 4, 128), F32),
            pltpu.SemaphoreType.DMA((2, groups - 1)),
            pltpu.SemaphoreType.DMA((2, subs - 1)),
        ],
        compiler_params=talks(2),
        name="gather",
    )(node)

    chunk = 2304 // subs
    fine_out, w_lift_grad, w_coarse_grad, w_back_grad, parts, inner, border, send = pl.pallas_call(
        functools.partial(backward_kernel, groups, subs),
        out_shape=(
            shape((64, 8, 512), BF16),
            shape((256, 512), F32),
            shape((7, 512, 512), F32),
            shape((512, 256), F32),
            shape((subs, chunk, 128), BF16),
            sq32,
            shape((ENTRIES + 1, 16, 256), BF16),
            shape((4, SLOTS, 16, 256), BF16),
        ),
        in_specs=[smem] + [vmem] * 18,
        out_specs=(vmem, vmem, spec(pl.ANY), vmem, vmem, vmem, vmem, vmem),
        scratch_shapes=mats
        + [
            pltpu.VMEM((512, 512), F32),
            pltpu.VMEM((nodes * 4, 128), F32),
            pltpu.VMEM((2, 128, 128), F32),
            pltpu.VMEM((nodes, 7 * 512), BF16),
            pltpu.VMEM((8, 128), F32),
            pltpu.VMEM((7, 512, 512), F32),
            pltpu.SemaphoreType.DMA((7,)),
        ],
        compiler_params=plain,
        name="backward",
    )(
        entry_of, slab, coarse_nbrs, w_lift, w_coarse, w_back, w_up, w_down, wm,
        q, g, sx, sy, sz, hidden, slope, pooled, pool_slope, grad_merged,
    )

    share = (2048 // subs) // groups
    total, slabs = pl.pallas_call(
        functools.partial(exchange_kernel, groups, subs),
        out_shape=(shape((subs, chunk, 128), BF16), shape((4, SLOTS, 16, 256), BF16)),
        in_specs=[vmem, vmem],
        out_specs=(vmem, vmem),
        scratch_shapes=[
            pltpu.VMEM((subs - 1, chunk, 128), BF16),
            pltpu.VMEM((share, 128), BF16),
            pltpu.VMEM((groups, share + 256 // subs, 128), BF16),
            pltpu.VMEM((groups - 1, share + 256 // subs, 128), BF16),
            pltpu.SemaphoreType.DMA((2, subs - 1)),
            pltpu.SemaphoreType.DMA((2, groups - 1)),
            pltpu.SemaphoreType.DMA((2, groups - 1)),
            pltpu.SemaphoreType.DMA((2, subs - 1)),
            pltpu.SemaphoreType.DMA((2, 4)),
        ],
        compiler_params=talks(3),
        name="exchange",
    )(parts, send)

    feats_grad, w_fine_grad, w_down_grad, w_up_grad = pl.pallas_call(
        functools.partial(finish_kernel, subs),
        out_shape=(
            shape((64, 8, 512), BF16),
            shape((7, 64, 64), F32),
            shape((512, 256), F32),
            shape((256, 512), F32),
        ),
        in_specs=[smem, smem] + [vmem] * 4,
        out_specs=(vmem,) * 4,
        scratch_shapes=[
            pltpu.VMEM((ENTRIES + 1, 16, 256), F32),
            pltpu.VMEM((512, 512), F32),
            pltpu.VMEM((2, 128, 128), F32),
        ],
        compiler_params=plain,
        name="finish",
    )(rows_of, asked, total, slabs, inner, border)

    return (
        fine_out.reshape(8, 8, 8, 512),
        feats_grad.reshape(8, 8, 8, 512),
        w_fine_grad,
        w_down_grad,
        w_lift_grad,
        w_coarse_grad,
        w_back_grad,
        w_up_grad,
    )


def solution(mesh):
    groups, subs = mesh.shape["grp"], mesh.shape["sub"]
    split4 = P(("grp", "sub"), None, None, None)
    return jax.shard_map(
        functools.partial(body, groups, subs),
        mesh=mesh,
        in_specs=(split4, P(("grp", "sub"), None)) + (P(),) * 7 + (split4,),
        out_specs=(split4, split4) + (P(),) * 6,
        check_vma=False,
    )
```

```python
import functools

import jax
import jax.numpy as jnp
from jax import lax
from jax.experimental import pallas as pl
from jax.experimental.pallas import tpu as pltpu
from jax.sharding import PartitionSpec as P

F32 = jnp.float32
BF16 = jnp.bfloat16
MESH = pl.DeviceIdType.MESH
OFFSETS = (-2, -1, 1, 2)
MEMORY = 58 << 20
ENTRIES = 48


def dot(x, y):
    return jnp.dot(x, y, preferred_element_type=F32)


def dot_nt(x, y):
    return lax.dot_general(x, y, (((1,), (1,)), ((), ())), preferred_element_type=F32)


def dot_tn(x, y):
    return lax.dot_general(x, y, (((0,), (0,)), ((), ())), preferred_element_type=F32)


def sigmoid(v):
    return 1.0 / (1.0 + jnp.exp(-v))


def perm_index(y):
    a, e = (y >> 8) & 1, (y >> 7) & 1
    u, w, b = (y >> 5) & 3, (y >> 3) & 3, y & 7
    return b * 64 + (2 * u + a) * 8 + 2 * w + e


def perm_to():
    rows = lax.broadcasted_iota(jnp.int32, (512, 512), 0)
    cols = lax.broadcasted_iota(jnp.int32, (512, 512), 1)
    return (perm_index(rows) == cols).astype(F32).astype(BF16)


def perm_from():
    rows = lax.broadcasted_iota(jnp.int32, (512, 512), 0)
    cols = lax.broadcasted_iota(jnp.int32, (512, 512), 1)
    return (perm_index(cols) == rows).astype(F32).astype(BF16)


def load_natural(ref):
    return ref[...].astype(F32).reshape(512, 512).astype(BF16)


def pooled_rows(x, perm, out_ref, wide_ref=None):
    y = dot(perm, x)
    for z in range(4):
        for ae in range(4):
            block = y[ae * 128 : (ae + 1) * 128, z * 128 : (z + 1) * 128]
            where = (pl.ds(z * 128, 128), pl.ds(ae * 128, 128))
            out_ref[where] = block.astype(BF16)
            if wide_ref is not None:
                wide_ref[where] = block


def natural_rows(q, perm_back):
    y = jnp.concatenate(
        [
            jnp.concatenate(
                [q[z * 128 : (z + 1) * 128, ae * 128 : (ae + 1) * 128] for z in range(4)], axis=1
            )
            for ae in range(4)
        ],
        axis=0,
    )
    return dot(perm_back, y).reshape(64, 8, 512).astype(BF16)


def low_lanes(rows):
    return lax.broadcasted_iota(jnp.int32, (rows, 128), 1) < 64


def layer(ref, axis, place, parity):
    if axis == 0:
        return jnp.concatenate(
            [
                ref[z * 128 + place * 32 : z * 128 + place * 32 + 32, parity * 256 : parity * 256 + 256]
                for z in range(4)
            ],
            axis=0,
        )
    if axis == 1:
        parts = []
        for a in range(2):
            lane = (a * 2 + parity) * 128
            parts.append(
                jnp.concatenate(
                    [ref[zu * 32 + place * 8 : zu * 32 + place * 8 + 8, lane : lane + 128] for zu in range(16)],
                    axis=0,
                )
            )
        return jnp.concatenate(parts, axis=1)
    parts = []
    for a in range(2):
        first = ref[place * 128 : place * 128 + 128, a * 256 : a * 256 + 128]
        second = ref[place * 128 : place * 128 + 128, a * 256 + 128 : a * 256 + 256]
        if parity == 0:
            second = pltpu.roll(second, 64, 1)
        else:
            first = pltpu.roll(first, 64, 1)
        parts.append(jnp.where(low_lanes(128), first, second))
    return jnp.concatenate(parts, axis=1)


def add_layer(ref, axis, place, parity, value):
    if axis == 0:
        for z in range(4):
            rows = pl.ds(z * 128 + place * 32, 32)
            ref[rows, parity * 256 : parity * 256 + 256] += value[z * 32 : z * 32 + 32]
    elif axis == 1:
        for a in range(2):
            lane = (a * 2 + parity) * 128
            for zu in range(16):
                rows = pl.ds(zu * 32 + place * 8, 8)
                ref[rows, lane : lane + 128] += value[zu * 8 : zu * 8 + 8, a * 128 : a * 128 + 128]
    else:
        low = low_lanes(128)
        rows = pl.ds(place * 128, 128)
        for a in range(2):
            part = value[:, a * 128 : a * 128 + 128]
            turned = pltpu.roll(part, 64, 1)
            first, second = (part, turned) if parity == 0 else (turned, part)
            keep = low if parity == 0 else ~low
            ref[rows, a * 256 : a * 256 + 128] += jnp.where(keep, first, 0.0)
            ref[rows, a * 256 + 128 : a * 256 + 256] += jnp.where(keep, second, 0.0)


FACES = ((0, 3, 1), (0, 0, 0), (1, 3, 1), (1, 0, 0), (2, 3, 1), (2, 0, 0))
BEYOND = ((0, 3, 0), (0, 0, 1), (1, 3, 0), (1, 0, 1), (2, 3, 0), (2, 0, 1))


def one_hot(mask):
    return mask.astype(F32).astype(BF16)


def iota(rows, cols, axis):
    return lax.broadcasted_iota(jnp.int32, (rows, cols), axis)


def entries(neighbours, me):
    nb = neighbours[...]
    n = jnp.concatenate([jnp.broadcast_to(nb[:, d : d + 1], (8, 128)) for d in range(6)], axis=0)
    lane = iota(ENTRIES, 128, 1)
    direction = iota(ENTRIES, 128, 0) >> 3
    offset = (n >> 3) - me
    face = (n >= 0) & ((n & 7) == (lane & 7)) & ((lane >> 3) == (direction ^ 1))
    local = face & (offset == 0)
    peer = lane >> 3
    peer_offset = jnp.where(peer < 2, peer - 2, peer - 1)
    far = (n >= 0) & (lane < 32) & (offset == peer_offset)
    before = one_hot(iota(ENTRIES, ENTRIES, 1) < iota(ENTRIES, ENTRIES, 0))
    count = dot(before, one_hot(far))
    slot = far & (count == (lane & 7).astype(F32))
    return one_hot(face), one_hot(local), one_hot(slot)


def rolled(x, by):
    return pltpu.roll(x.astype(F32), by, 1).astype(BF16)


def coords(groups, subs, offset):
    nodes = groups * subs
    at = lax.axis_index("grp") * subs + lax.axis_index("sub")
    to = lax.rem(at + offset + nodes, nodes)
    return (to // subs, lax.rem(to, subs))


def peers_of(groups, subs):
    g, s = lax.axis_index("grp"), lax.axis_index("sub")
    near = [coords(groups, subs, off) for off in OFFSETS]
    over_grp = [(lax.rem(g + k, groups), s) for k in range(1, groups)]
    over_sub = [(g, lax.rem(s + k, subs)) for k in range(1, subs)]
    return near, over_grp, over_sub


def greet(peers):
    barrier = pltpu.get_barrier_semaphore()
    for peer in peers:
        pl.semaphore_signal(barrier, inc=1, device_id=peer, device_id_type=MESH)
    return lambda: pl.semaphore_wait(barrier, len(peers))


def send_all(peers, sems, src_of, dst_of):
    copies = []
    for k, peer in enumerate(peers):
        copy = pltpu.make_async_remote_copy(
            src_ref=src_of(k, peer),
            dst_ref=dst_of(k, peer),
            send_sem=sems.at[0, k],
            recv_sem=sems.at[1, k],
            device_id=peer,
            device_id_type=MESH,
        )
        copy.start()
        copies.append(copy)
    return copies


def send_near(near, sems, src, dst):
    copies = []
    for p in range(4):
        copy = pltpu.make_async_remote_copy(
            src_ref=src.at[p],
            dst_ref=dst.at[3 - p],
            send_sem=sems.at[0, p],
            recv_sem=sems.at[1, 3 - p],
            device_id=near[p],
            device_id_type=MESH,
        )
        copy.start()
        copies.append(copy)
    return copies


def wait_all(copies):
    for copy in copies:
        copy.wait()


def by_place(layers):
    return jnp.concatenate([x.reshape(16, 8, 256) for x in layers], axis=1).astype(BF16)


def pack_slots(pick, table, wide, out):
    for place in range(16):
        wide[place, 0:32, :] = dot(pick, table[place])
    for p in range(4):
        out[p] = wide[:, p * 8 : p * 8 + 8, :].reshape(128, 256).astype(BF16)


def unpack_slots(slots, table):
    table[:, ENTRIES : ENTRIES + 32, :] = by_place([slots[p].astype(F32) for p in range(4)])


def build_mats(w_fine, m0, mx, my, mz):
    zero = jnp.zeros((128, 128), BF16)
    none = jnp.zeros((64, 64), BF16)

    def put(ref, i, j, value):
        ref[i * 128 : (i + 1) * 128, j * 128 : (j + 1) * 128] = value

    def quad(a, b, c, d):
        return jnp.concatenate(
            [jnp.concatenate([a, b], axis=1), jnp.concatenate([c, d], axis=1)], axis=0
        )

    w = [w_fine[t] for t in range(7)]
    c = quad(w[0], w[6], w[5], w[0])
    d1, d2, d3, d4 = (quad(w[t], none, none, w[t]) for t in range(1, 5))
    ez = quad(none, w[5], w[6], none)
    for a in range(2):
        for e in range(2):
            i = a * 2 + e
            put(m0, i, i, c)
            put(m0, i, (1 - a) * 2 + e, d1 if a == 1 else d2)
            put(m0, i, a * 2 + (1 - e), d3 if e == 1 else d4)
            put(m0, i, 3 - i, zero)
    for i in range(2):
        for j in range(2):
            put(mx.at[0], i, j, d1 if i == j else zero)
            put(mx.at[1], i, j, d2 if i == j else zero)
            put(mz, i, j, ez if i == j else zero)
    put(my, 0, 0, zero)
    put(my, 1, 1, zero)
    put(my, 0, 1, d3)
    put(my, 1, 0, d4)


def block_kernel(
    groups, subs,
    feats, grad, neighbours, w_fine, w_down, w_up, nbrs, w_lift, w_coarse_hbm, w_back,
    fine_out, feats_grad, up_all, down_all, fine_all, taps, out_mean, out_grad, out_coarse, out_dpre, out_in,
    q, g, sx, sy, sz, hidden, slope, pooled, pool_slope, grad_merged, slab, back_send, back_add,
    wide, table, slot_wide, rim, asked, wanted, send, recv, send_2, recv_2, m0, mx, my, mz, base, node, first, pack,
    flat, w_coarse, inner, merged, dpre, stage,
    up_parts, up_in, up_slots, down_parts, down_in, down_slots, fine_parts, fine_in, fine_slots,
    sem, sems_a, sems_b, sems_c, sems_d, sems_n, up_a, up_b, up_c, down_a, down_b, down_c, fine_a, fine_b, fine_c,
):
    gi, si = lax.axis_index("grp"), lax.axis_index("sub")
    near, over_grp, over_sub = peers_of(groups, subs)
    greeted = greet(near + over_grp + over_sub)
    weight_copy = pltpu.make_async_copy(w_coarse_hbm, w_coarse, sem)
    weight_copy.start()
    face, local, slot = entries(neighbours, gi * subs + si)
    wanted[...] = dot_tn(slot, face)[0:32].reshape(4, 8, 128)
    greeted()
    asking = send_near(near, sems_a, wanted, asked)

    perm = perm_to()
    pooled_rows(load_natural(feats), perm, q, wide)
    table[:, ENTRIES:128, :] = jnp.zeros((16, 128 - ENTRIES, 256), BF16)
    table[:, 0:ENTRIES, :] = by_place([layer(wide, *where) for where in FACES])
    eye = one_hot(iota(ENTRIES, 128, 0) == iota(ENTRIES, 128, 1))
    back_send[...] = dot_tn(slot, eye)[0:32].astype(BF16)
    local_back = dot_tn(local, eye)[0:ENTRIES].astype(BF16)
    wait_all(asking)
    given = asked[...].reshape(32, 128).astype(BF16)
    pack_slots(given, table, slot_wide, send)
    sending = send_near(near, sems_b, send, recv)

    given_back = dot_tn(given, eye[0:32])[0:ENTRIES].astype(BF16)
    back_add[...] = local_back + rolled(given_back, ENTRIES)
    pooled_rows(load_natural(grad), perm, g)
    build_mats(w_fine, m0, mx, my, mz)
    base[...] = dot(q[...], m0[...])
    merged_grad = dot_nt(g[...], w_up[...])
    grad_merged[...] = merged_grad
    total = jnp.sum(merged_grad, axis=0, keepdims=True).astype(BF16).astype(F32)
    low = low_lanes(512)
    for z in range(4):
        at = z * 128
        sx[at : at + 96, 0:256] = q[at + 32 : at + 128, 0:256]
        sx[at + 32 : at + 128, 256:512] = q[at : at + 96, 256:512]
    pick = local + rolled(slot, ENTRIES)

    wait_all(sending)
    unpack_slots(recv, table)
    for place in range(16):
        slot_wide[place] = dot(pick, table[place])
    for d in range(6):
        rim[d] = slot_wide[:, d * 8 : d * 8 + 8, :].reshape(128, 256)
    for z in range(4):
        at = z * 128
        sx[at + 96 : at + 128, 0:256] = rim[0, z * 32 : z * 32 + 32, :].astype(BF16)
        sx[at : at + 32, 256:512] = rim[1, z * 32 : z * 32 + 32, :].astype(BF16)
    for a in range(2):
        half = slice(a * 128, a * 128 + 128)
        lanes = slice(a * 256, a * 256 + 128)
        part = wide[:, lanes].reshape(16, 32, 128)
        edge = rim[2, :, half].reshape(16, 8, 128)
        sy[:, lanes] = jnp.concatenate([part[:, 8:], edge], axis=1).reshape(512, 128).astype(BF16)
        lanes = slice(a * 256 + 128, a * 256 + 256)
        part = wide[:, lanes].reshape(16, 32, 128)
        edge = rim[3, :, half].reshape(16, 8, 128)
        sy[:, lanes] = jnp.concatenate([edge, part[:, :24]], axis=1).reshape(512, 128).astype(BF16)
        above, below = rim[4, :, half], rim[5, :, half]
        for e in range(2):
            lanes = slice((a * 2 + e) * 128, (a * 2 + e) * 128 + 128)
            part = wide[:, lanes]
            edge_up = above if e == 0 else pltpu.roll(above, 64, 1)
            edge_down = pltpu.roll(below, 64, 1) if e == 0 else below
            up = jnp.concatenate([part[128:], edge_up], axis=0)
            down = jnp.concatenate([edge_down, part[:384]], axis=0)
            sz[:, lanes] = jnp.where(low, up, down).astype(BF16)
    for a in range(2):
        lanes = slice(a * 256, a * 256 + 256)
        other = slice(256 - a * 256, 512 - a * 256)
        pre = (
            base[:, lanes]
            + dot(sx[:, other], mx[1 - a])
            + dot(sy[:, lanes], my[...])
            + dot(sz[:, lanes], mz[...])
        )
        s = sigmoid(pre)
        hidden[:, lanes] = (pre * s).astype(BF16)
        slope[:, lanes] = s * (1.0 + pre * (1.0 - s))
    pre = dot(hidden[...], w_down[...])
    s = sigmoid(pre)
    value = (pre * s).astype(BF16)
    mean = jnp.sum(value.astype(F32), axis=0, keepdims=True) * (1.0 / 512.0)
    mean = mean.astype(BF16).astype(F32)
    for half in range(2):
        node[half : half + 1, :] = mean[:, half * 128 : half * 128 + 128]
        node[2 + half : 3 + half, :] = total[:, half * 128 : half * 128 + 128]
    sending = send_all(over_grp, sems_c, lambda k, peer: node, lambda k, peer: first.at[gi])
    pooled[...] = value
    pool_slope[...] = s * (1.0 + pre * (1.0 - s))
    first[gi] = node[...]
    wait_all(sending)
    for i in range(groups):
        pack[4 * i : 4 * i + 4, :] = first[i]
    slab[si] = pack[...].astype(BF16)
    wait_all(send_all(over_sub, sems_d, lambda k, peer: slab.at[si], lambda k, peer: slab.at[si]))

    nodes = groups * subs
    me = gi * subs + si
    for s in range(subs):
        flat[s * groups * 4 : (s + 1) * groups * 4, :] = slab[s].astype(F32)
    pieces = [flat[pl.ds(k, nodes, stride=4), :] for k in range(4)]
    rows, cols = iota(nodes, nodes, 0), iota(nodes, nodes, 1)
    order = one_hot(lax.rem(rows, subs) * groups + rows // subs == cols)
    gathered = dot(order, jnp.concatenate(pieces, axis=1).astype(BF16)).astype(BF16)
    node_mean, node_grad = gathered[:, :256], gathered[:, 256:]
    coarse_in = dot(node_mean, w_lift[...]).astype(BF16)
    picks = [one_hot(nbrs[d : d + 1, :] == rows) for d in range(6)]
    taps[:, 0:512] = coarse_in
    for d in range(6):
        taps[:, (d + 1) * 512 : (d + 2) * 512] = dot_tn(picks[d], coarse_in).astype(BF16)
    weight_copy.wait()
    coarse_pre = jnp.zeros((nodes, 512), F32)
    for t in range(7):
        coarse_pre = coarse_pre + dot(taps[:, t * 512 : (t + 1) * 512], w_coarse[t])
    s = sigmoid(coarse_pre)
    coarse_out = (coarse_pre * s).astype(BF16)
    coarse_slope = s * (1.0 + coarse_pre * (1.0 - s))
    coarse_dpre = (dot_nt(node_grad, w_back[...]) * coarse_slope).astype(BF16)
    in_grad = dot_nt(coarse_dpre, w_coarse[0])
    for d in range(6):
        moved = dot(picks[d], coarse_dpre).astype(BF16)
        in_grad = in_grad + dot_nt(moved, w_coarse[d + 1])
    in_grad = in_grad.astype(BF16)
    mine = one_hot(iota(16, nodes, 1) == me)
    back = dot(dot(mine, coarse_out).astype(BF16), w_back[...])[0:1]
    mean_grad = dot_nt(dot(mine, in_grad).astype(BF16), w_lift[...])[0:1] * (1.0 / 512.0)
    for ref, value in (
        (out_mean, node_mean), (out_grad, node_grad), (out_coarse, coarse_out),
        (out_dpre, coarse_dpre), (out_in, in_grad),
    ):
        ref[...] = value

    up_rows, down_rows, fine_rows = 256 // subs, 512 // groups, 256 // subs

    merged[...] = (pooled[...].astype(F32) + back).astype(BF16)
    part = dot_tn(merged[...], g[...])
    for i in range(subs):
        for k in range(4):
            up_parts[i, k * up_rows : (k + 1) * up_rows, :] = part[
                i * up_rows : (i + 1) * up_rows, k * 128 : (k + 1) * 128
            ].astype(BF16)
    up_sent = send_all(over_sub, up_a, lambda k, peer: up_parts.at[peer[1]], lambda k, peer: up_in.at[k])

    pool_dpre = ((grad_merged[...] + mean_grad) * pool_slope[...]).astype(BF16)
    part = dot_tn(hidden[...], pool_dpre)
    for i in range(groups):
        for k in range(2):
            down_parts[i, k * down_rows : (k + 1) * down_rows, :] = part[
                i * down_rows : (i + 1) * down_rows, k * 128 : (k + 1) * 128
            ].astype(BF16)
    down_sent = send_all(over_grp, down_a, lambda k, peer: down_parts.at[peer[0]], lambda k, peer: down_in.at[k])

    dpre[...] = ((g[...].astype(F32) + dot_nt(pool_dpre, w_down[...])) * slope[...]).astype(BF16)

    def block(value, i, j):
        return value[i * 128 : (i + 1) * 128, j * 128 : (j + 1) * 128]

    def fold(value):
        return value[:64] + pltpu.roll(value[64:], 64, 1)

    centre = dot_tn(q[...], dpre[...])
    gx0 = dot_tn(sx[:, 0:256], dpre[:, 256:512])
    gx1 = dot_tn(sx[:, 256:512], dpre[:, 0:256])
    gy = [dot_tn(sy[:, a * 256 : a * 256 + 256], dpre[:, a * 256 : a * 256 + 256]) for a in range(2)]
    gz = [dot_tn(sz[:, a * 256 : a * 256 + 256], dpre[:, a * 256 : a * 256 + 256]) for a in range(2)]
    middle = sum(block(centre, i, i) for i in range(4))
    x_up = block(centre, 2, 0) + block(centre, 3, 1) + block(gx0, 0, 0) + block(gx0, 1, 1)
    x_down = block(centre, 0, 2) + block(centre, 1, 3) + block(gx1, 0, 0) + block(gx1, 1, 1)
    y_up = block(centre, 1, 0) + block(centre, 3, 2) + block(gy[0], 0, 1) + block(gy[1], 0, 1)
    y_down = block(centre, 0, 1) + block(centre, 2, 3) + block(gy[0], 1, 0) + block(gy[1], 1, 0)
    between = sum(block(value, i, i) for value in gz for i in range(2))
    z_up = middle[64:] + pltpu.roll(between[:64], 64, 1)
    z_down = pltpu.roll(middle[:64], 64, 1) + between[64:]
    tap_sums = [fold(middle), fold(x_up), fold(x_down), fold(y_up), fold(y_down), z_up, z_down]
    tap_sums.append(jnp.zeros((64, 128), F32))
    low = low_lanes(64)
    for pair in range(4):
        both = jnp.where(low, tap_sums[2 * pair], pltpu.roll(tap_sums[2 * pair + 1], 64, 1))
        for i in range(64 // fine_rows):
            fine_parts[pair * (64 // fine_rows) + i] = both[i * fine_rows : (i + 1) * fine_rows].astype(BF16)
    fine_sent = send_all(over_sub, fine_a, lambda k, peer: fine_parts.at[peer[1]], lambda k, peer: fine_in.at[k])

    inner[...] = g[...].astype(F32) + dot_nt(dpre[...], m0[...])
    wide[:, 0:256] = dot_nt(dpre[:, 256:512], mx[0])
    wide[:, 256:512] = dot_nt(dpre[:, 0:256], mx[1])
    for z in range(4):
        at = z * 128
        inner[at + 32 : at + 128, 0:256] += wide[at : at + 96, 0:256]
        inner[at : at + 96, 256:512] += wide[at + 32 : at + 128, 256:512]
    for d in (0, 1):
        stage[d] = layer(wide, *BEYOND[d])
    for a in range(2):
        wide[:, a * 256 : a * 256 + 256] = dot_nt(dpre[:, a * 256 : a * 256 + 256], my[...])
    for zu in range(16):
        at = zu * 32
        for a in range(2):
            first, second = slice(a * 256, a * 256 + 128), slice(a * 256 + 128, a * 256 + 256)
            inner[at + 8 : at + 32, first] += wide[at : at + 24, first]
            inner[at : at + 24, second] += wide[at + 8 : at + 32, second]
    for d in (2, 3):
        stage[d] = layer(wide, *BEYOND[d])
    for a in range(2):
        wide[:, a * 256 : a * 256 + 256] = dot_nt(dpre[:, a * 256 : a * 256 + 256], mz[...])
    for d in (4, 5):
        stage[d] = layer(wide, *BEYOND[d])
    table[:, ENTRIES : ENTRIES + 32, :] = jnp.zeros((16, 32, 256), BF16)
    table[:, 0:ENTRIES, :] = by_place([stage[d] for d in range(6)])
    pack_slots(back_send[...], table, slot_wide, send_2)
    slots_sent = send_near(near, sems_n, send_2, recv_2)
    low = low_lanes(384)
    for i in range(4):
        lanes = slice(i * 128, i * 128 + 128)
        inner[128:512, lanes] += jnp.where(low, wide[0:384, lanes], 0.0)
        inner[0:384, lanes] += jnp.where(low, 0.0, wide[128:512, lanes])

    def reduce(own, incoming, copies):
        wait_all(copies)
        value = own.astype(F32)
        for k in range(len(copies)):
            value = value + incoming[k].astype(F32)
        return value.astype(BF16)

    def join(slots, copies, count):
        wait_all(copies)
        value = slots[0].astype(F32)
        for k in range(1, count):
            value = value + slots[k].astype(F32)
        return value.astype(BF16)

    up_slots[gi] = reduce(up_parts[si], up_in, up_sent)
    up_sent = send_all(over_grp, up_b, lambda k, peer: up_slots.at[gi], lambda k, peer: up_slots.at[gi])
    down_slots[si] = reduce(down_parts[gi], down_in, down_sent)
    down_sent = send_all(over_sub, down_b, lambda k, peer: down_slots.at[si], lambda k, peer: down_slots.at[si])
    fine_slots[gi] = reduce(fine_parts[si], fine_in, fine_sent)
    fine_sent = send_all(over_grp, fine_b, lambda k, peer: fine_slots.at[gi], lambda k, peer: fine_slots.at[gi])

    back_perm = perm_from()
    out = q[...].astype(F32) + hidden[...].astype(F32) + dot(merged[...], w_up[...])
    fine_out[...] = natural_rows(out.astype(BF16), back_perm)

    up_all[si] = join(up_slots, up_sent, groups)
    up_sent = send_all(over_sub, up_c, lambda k, peer: up_all.at[si], lambda k, peer: up_all.at[si])
    fine_all[si] = join(fine_slots, fine_sent, groups)
    fine_sent = send_all(over_sub, fine_c, lambda k, peer: fine_all.at[si], lambda k, peer: fine_all.at[si])
    down_all[gi] = join(down_slots, down_sent, subs)
    down_sent = send_all(over_grp, down_c, lambda k, peer: down_all.at[gi], lambda k, peer: down_all.at[gi])

    wait_all(slots_sent)
    unpack_slots(recv_2, table)
    for place in range(16):
        slot_wide[place] = dot(back_add[...], table[place])
    for f in range(6):
        add_layer(inner, *FACES[f], slot_wide[:, f * 8 : f * 8 + 8, :].reshape(128, 256))
    feats_grad[...] = natural_rows(inner[...].astype(BF16), back_perm)
    wait_all(up_sent)
    wait_all(down_sent)
    wait_all(fine_sent)


def finish_kernel(
    groups, subs, fine_in, feats_in, up_all, down_all, fine_all, taps, node_mean, node_grad, coarse_out, dpre, in_grad,
    fine_out, feats_grad, w_fine_grad, w_down_grad, w_lift_grad, w_coarse_grad, w_back_grad, w_up_grad,
    coarse_sum, sems,
):
    copies = []
    for t in range(7):
        coarse_sum[t] = dot_tn(taps[:, t * 512 : (t + 1) * 512], dpre[...])
        copy = pltpu.make_async_copy(coarse_sum.at[t], w_coarse_grad.at[t], sems.at[t])
        copy.start()
        copies.append(copy)
    w_back_grad[...] = dot_tn(coarse_out[...], node_grad[...])
    w_lift_grad[...] = dot_tn(node_mean[...], in_grad[...])
    fine_out[...] = fine_in[...]
    feats_grad[...] = feats_in[...]
    up_rows, down_rows, fine_rows = 256 // subs, 512 // groups, 256 // subs
    for i in range(subs):
        for k in range(4):
            w_up_grad[i * up_rows : (i + 1) * up_rows, k * 128 : (k + 1) * 128] = up_all[
                i, k * up_rows : (k + 1) * up_rows, :
            ].astype(F32)
    for i in range(groups):
        for k in range(2):
            w_down_grad[i * down_rows : (i + 1) * down_rows, k * 128 : (k + 1) * 128] = down_all[
                i, k * down_rows : (k + 1) * down_rows, :
            ].astype(F32)
    each = 64 // fine_rows
    for pair in range(4):
        both = jnp.concatenate([fine_all[pair * each + i] for i in range(each)], axis=0).astype(F32)
        w_fine_grad[2 * pair] = both[:, 0:64]
        if pair < 3:
            w_fine_grad[2 * pair + 1] = pltpu.roll(both, 64, 1)[:, 0:64]
    wait_all(copies)


def spec(space=pltpu.VMEM):
    return pl.BlockSpec(memory_space=space)


def shape(dims, dtype):
    return jax.ShapeDtypeStruct(dims, dtype)


def buf(dims, dtype=BF16):
    return pltpu.VMEM(dims, dtype)


def pairs(count):
    return pltpu.SemaphoreType.DMA((2, count))


def body(groups, subs, feats, neighbours, w_fine, w_down, w_lift, coarse_nbrs, w_coarse, w_back, w_up, grad_out):
    nodes = groups * subs
    up_rows, down_rows, fine_rows = 256 // subs, 512 // groups, 256 // subs
    vmem, anywhere = spec(), spec(pl.ANY)
    sq16, sq32 = buf((512, 512)), buf((512, 512), F32)
    up_shape, down_shape, fine_shape = (4 * up_rows, 128), (2 * down_rows, 128), (fine_rows, 128)
    slots = buf((4, 128, 256))

    results = pl.pallas_call(
        functools.partial(block_kernel, groups, subs),
        out_shape=(
            shape((64, 8, 512), BF16),
            shape((64, 8, 512), BF16),
            shape((subs,) + up_shape, BF16),
            shape((groups,) + down_shape, BF16),
            shape((subs,) + fine_shape, BF16),
            shape((nodes, 7 * 512), BF16),
            shape((nodes, 256), BF16),
            shape((nodes, 256), BF16),
            shape((nodes, 512), BF16),
            shape((nodes, 512), BF16),
            shape((nodes, 512), BF16),
        ),
        in_specs=[vmem] * 8 + [anywhere, vmem],
        out_specs=(vmem,) * 11,
        scratch_shapes=[sq16] * 6
        + [sq32, buf((512, 256)), buf((512, 256), F32), buf((512, 256), F32)]
        + [buf((subs, groups * 4, 128)), buf((32, 128)), buf((ENTRIES, 128))]
        + [sq32, buf((16, 128, 256)), buf((16, ENTRIES, 256), F32), buf((6, 128, 256), F32)]
        + [buf((4, 8, 128), F32), buf((4, 8, 128), F32), slots, slots, slots, slots]
        + [sq16, buf((2, 256, 256)), buf((256, 256)), buf((256, 256))]
        + [sq32, buf((4, 128), F32), buf((groups, 4, 128), F32), buf((groups * 4, 128), F32)]
        + [buf((nodes * 4, 128), F32), buf((7, 512, 512)), sq32, buf((512, 256)), sq16, buf((6, 128, 256), F32)]
        + [buf((subs,) + up_shape), buf((subs - 1,) + up_shape), buf((groups,) + up_shape)]
        + [buf((groups,) + down_shape), buf((groups - 1,) + down_shape), buf((subs,) + down_shape)]
        + [buf((subs,) + fine_shape), buf((subs - 1,) + fine_shape), buf((groups,) + fine_shape)]
        + [pltpu.SemaphoreType.DMA, pairs(4), pairs(4), pairs(groups - 1), pairs(subs - 1), pairs(4)]
        + [pairs(subs - 1), pairs(groups - 1), pairs(subs - 1)]
        + [pairs(groups - 1), pairs(subs - 1), pairs(groups - 1)]
        + [pairs(subs - 1), pairs(groups - 1), pairs(subs - 1)],
        compiler_params=pltpu.CompilerParams(collective_id=1, has_side_effects=True, vmem_limit_bytes=MEMORY),
        name="block",
    )(
        feats.reshape(64, 8, 512), grad_out.reshape(64, 8, 512), neighbours,
        w_fine, w_down, w_up, coarse_nbrs.T, w_lift, w_coarse, w_back,
    )

    outs = pl.pallas_call(
        functools.partial(finish_kernel, groups, subs),
        out_shape=(
            shape((64, 8, 512), BF16),
            shape((64, 8, 512), BF16),
            shape((7, 64, 64), F32),
            shape((512, 256), F32),
            shape((256, 512), F32),
            shape((7, 512, 512), F32),
            shape((512, 256), F32),
            shape((256, 512), F32),
        ),
        in_specs=[vmem] * 11,
        out_specs=(vmem,) * 5 + (anywhere, vmem, vmem),
        scratch_shapes=[buf((7, 512, 512), F32), pltpu.SemaphoreType.DMA((7,))],
        compiler_params=pltpu.CompilerParams(vmem_limit_bytes=MEMORY),
        name="finish",
    )(*results)
    return (outs[0].reshape(8, 8, 8, 512), outs[1].reshape(8, 8, 8, 512)) + tuple(outs[2:])


def solution(mesh):
    groups, subs = mesh.shape["grp"], mesh.shape["sub"]
    split4 = P(("grp", "sub"), None, None, None)
    return jax.shard_map(
        functools.partial(body, groups, subs),
        mesh=mesh,
        in_specs=(split4, P(("grp", "sub"), None)) + (P(),) * 7 + (split4,),
        out_specs=(split4, split4) + (P(),) * 6,
        check_vma=False,
    )
```

```python
import functools

import jax
import jax.numpy as jnp
from jax import lax
from jax.experimental import pallas as pl
from jax.experimental.pallas import tpu as pltpu
from jax.sharding import PartitionSpec as P

F32 = jnp.float32
BF16 = jnp.bfloat16
I32 = jnp.int32
MESH = pl.DeviceIdType.MESH
OFFSETS = (-2, -1, 1, 2)
MEMORY = 58 << 20
ENTRIES = 48
SOURCES = ENTRIES + 32
SLOTS = 6


def dot(x, y):
    return jnp.dot(x, y, preferred_element_type=F32)


def dot_nt(x, y):
    return lax.dot_general(x, y, (((1,), (1,)), ((), ())), preferred_element_type=F32)


def dot_tn(x, y):
    return lax.dot_general(x, y, (((0,), (0,)), ((), ())), preferred_element_type=F32)


def sigmoid(v):
    return 1.0 / (1.0 + jnp.exp(-v))


def perm_index(y):
    a, e = (y >> 8) & 1, (y >> 7) & 1
    u, w, b = (y >> 5) & 3, (y >> 3) & 3, y & 7
    return b * 64 + (2 * u + a) * 8 + 2 * w + e


def perm_to():
    rows = lax.broadcasted_iota(jnp.int32, (512, 512), 0)
    cols = lax.broadcasted_iota(jnp.int32, (512, 512), 1)
    return (perm_index(rows) == cols).astype(F32).astype(BF16)


def perm_from():
    rows = lax.broadcasted_iota(jnp.int32, (512, 512), 0)
    cols = lax.broadcasted_iota(jnp.int32, (512, 512), 1)
    return (perm_index(cols) == rows).astype(F32).astype(BF16)


def load_natural(ref):
    return ref[...].astype(F32).reshape(512, 512).astype(BF16)


def pooled_rows(x, perm, out_ref, wide_ref=None):
    y = dot(perm, x)
    for z in range(4):
        for ae in range(4):
            block = y[ae * 128 : (ae + 1) * 128, z * 128 : (z + 1) * 128]
            where = (pl.ds(z * 128, 128), pl.ds(ae * 128, 128))
            out_ref[where] = block.astype(BF16)
            if wide_ref is not None:
                wide_ref[where] = block


def natural_rows(q, perm_back):
    y = jnp.concatenate(
        [
            jnp.concatenate(
                [q[z * 128 : (z + 1) * 128, ae * 128 : (ae + 1) * 128] for z in range(4)], axis=1
            )
            for ae in range(4)
        ],
        axis=0,
    )
    return dot(perm_back, y).reshape(64, 8, 512).astype(BF16)


def low_lanes(rows):
    return lax.broadcasted_iota(jnp.int32, (rows, 128), 1) < 64


def layer(ref, axis, place, parity):
    if axis == 0:
        return jnp.concatenate(
            [
                ref[z * 128 + place * 32 : z * 128 + place * 32 + 32, parity * 256 : parity * 256 + 256]
                for z in range(4)
            ],
            axis=0,
        )
    if axis == 1:
        parts = []
        for a in range(2):
            lane = (a * 2 + parity) * 128
            parts.append(
                jnp.concatenate(
                    [ref[zu * 32 + place * 8 : zu * 32 + place * 8 + 8, lane : lane + 128] for zu in range(16)],
                    axis=0,
                )
            )
        return jnp.concatenate(parts, axis=1)
    parts = []
    for a in range(2):
        first = ref[place * 128 : place * 128 + 128, a * 256 : a * 256 + 128]
        second = ref[place * 128 : place * 128 + 128, a * 256 + 128 : a * 256 + 256]
        if parity == 0:
            second = pltpu.roll(second, 64, 1)
        else:
            first = pltpu.roll(first, 64, 1)
        parts.append(jnp.where(low_lanes(128), first, second))
    return jnp.concatenate(parts, axis=1)


def add_layer(ref, axis, place, parity, value):
    if axis == 0:
        for z in range(4):
            rows = pl.ds(z * 128 + place * 32, 32)
            ref[rows, parity * 256 : parity * 256 + 256] += value[z * 32 : z * 32 + 32]
    elif axis == 1:
        for a in range(2):
            lane = (a * 2 + parity) * 128
            for zu in range(16):
                rows = pl.ds(zu * 32 + place * 8, 8)
                ref[rows, lane : lane + 128] += value[zu * 8 : zu * 8 + 8, a * 128 : a * 128 + 128]
    else:
        low = low_lanes(128)
        rows = pl.ds(place * 128, 128)
        for a in range(2):
            part = value[:, a * 128 : a * 128 + 128]
            turned = pltpu.roll(part, 64, 1)
            first, second = (part, turned) if parity == 0 else (turned, part)
            keep = low if parity == 0 else ~low
            ref[rows, a * 256 : a * 256 + 128] += jnp.where(keep, first, 0.0)
            ref[rows, a * 256 + 128 : a * 256 + 256] += jnp.where(keep, second, 0.0)


FACES = ((0, 3, 1), (0, 0, 0), (1, 3, 1), (1, 0, 0), (2, 3, 1), (2, 0, 0))
BEYOND = ((0, 3, 0), (0, 0, 1), (1, 3, 0), (1, 0, 1), (2, 3, 0), (2, 0, 1))


def one_hot(mask):
    return mask.astype(F32).astype(BF16)


def iota(rows, cols, axis):
    return lax.broadcasted_iota(jnp.int32, (rows, cols), axis)


def entries(neighbours, me):
    nb = neighbours[...]
    n = jnp.concatenate([jnp.broadcast_to(nb[:, d : d + 1], (8, 128)) for d in range(6)], axis=0)
    lane = iota(ENTRIES, 128, 1)
    direction = iota(ENTRIES, 128, 0) >> 3
    offset = (n >> 3) - me
    number = (direction ^ 1) * 8 + (n & 7)
    local = (n >= 0) & (offset == 0)
    peer = lane >> 3
    peer_offset = jnp.where(peer < 2, peer - 2, peer - 1)
    far = (n >= 0) & (lane < 32) & (offset == peer_offset)
    before = one_hot(iota(ENTRIES, ENTRIES, 1) < iota(ENTRIES, ENTRIES, 0))
    count = dot(before, one_hot(far))
    slot = far & (count == (lane & 7).astype(F32))
    place = jnp.sum(jnp.where(slot, lane + 1, 0), axis=1, keepdims=True)
    source = jnp.where(local, number, jnp.where(place > 0, ENTRIES - 1 + place, SOURCES))
    return one_hot(local & (lane == number)), one_hot(slot), number, source


def rolled(x, by):
    return pltpu.roll(x.astype(F32), by, 1).astype(BF16)


def coords(groups, subs, offset):
    nodes = groups * subs
    at = lax.axis_index("grp") * subs + lax.axis_index("sub")
    to = lax.rem(at + offset + nodes, nodes)
    return (to // subs, lax.rem(to, subs))


def ring(a, b, size):
    return min((a - b) % size, (b - a) % size)


def peers_of(groups, subs):
    g, s = lax.axis_index("grp"), lax.axis_index("sub")
    near = [coords(groups, subs, off) for off in OFFSETS]
    y, core = g // 2, lax.rem(g, 2)
    steps = [(dy, dc) for dy in range(groups // 2) for dc in range(2) if dy or dc]
    steps.sort(key=lambda d: -4 * ring(d[0], 0, groups // 2) - d[1])
    over_grp = [(lax.rem(y + dy, groups // 2) * 2 + lax.rem(core + dc, 2), s) for dy, dc in steps]
    wide = min(4, subs)
    deep = subs // wide
    z, x = s // wide, lax.rem(s, wide)
    steps = [(dz, dx) for dz in range(deep) for dx in range(wide) if dz or dx]
    steps.sort(key=lambda d: -ring(d[0], 0, deep) - ring(d[1], 0, wide))
    over_sub = [(g, lax.rem(z + dz, deep) * wide + lax.rem(x + dx, wide)) for dz, dx in steps]
    heard = [lax.rem(z + deep - dz, deep) * wide + lax.rem(x + wide - dx, wide) for dz, dx in steps]
    return near, over_grp, over_sub, heard


def greet(peers):
    barrier = pltpu.get_barrier_semaphore()
    for peer in peers:
        pl.semaphore_signal(barrier, inc=1, device_id=peer, device_id_type=MESH)
    return lambda: pl.semaphore_wait(barrier, len(peers))


def send_all(peers, sems, src_of, dst_of):
    copies = []
    for k, peer in enumerate(peers):
        copy = pltpu.make_async_remote_copy(
            src_ref=src_of(k, peer),
            dst_ref=dst_of(k, peer),
            send_sem=sems.at[0, k],
            recv_sem=sems.at[1, k],
            device_id=peer,
            device_id_type=MESH,
        )
        copy.start()
        copies.append(copy)
    return copies


def send_near(near, sems, src, dst):
    copies = []
    for p in (0, 3, 1, 2):
        copy = pltpu.make_async_remote_copy(
            src_ref=src.at[p],
            dst_ref=dst.at[3 - p],
            send_sem=sems.at[0, p],
            recv_sem=sems.at[1, 3 - p],
            device_id=near[p],
            device_id_type=MESH,
        )
        copy.start()
        copies.append(copy)
    return copies


def copy_all(pairs, sems, first):
    copies = []
    for k, (src, dst) in enumerate(pairs):
        copy = pltpu.make_async_copy(src, dst, sems.at[first + k])
        copy.start()
        copies.append(copy)
    return copies


def wait_all(copies):
    for copy in copies:
        copy.wait()


def by_place(layers):
    return jnp.concatenate([x.reshape(16, 8, 256) for x in layers], axis=1).astype(BF16)


def by_brick(layers, stage, out):
    for which, value in enumerate(layers):
        for half in range(2):
            lanes = slice(half * 128, half * 128 + 128)
            stage[which, half] = value[:, lanes]
            for b in range(8):
                out[which * 8 + b, :, lanes] = stage[which, half, pl.ds(b, 16, stride=8), :].astype(BF16)


def pick_slots(numbers, faces, out):
    for p in range(4):
        for i in range(SLOTS):
            row = jnp.clip(numbers[p * 8 + i, 0] - 1, 0, ENTRIES - 1)
            out[p, i] = faces[row]


def unpack_slots(slots, spread, table):
    for p in range(4):
        for i in range(SLOTS):
            face = slots[p, i].astype(F32)
            for half in range(2):
                spread[half, pl.ds(p * 8 + i, 16, stride=32), :] = face[:, half * 128 : half * 128 + 128]
    for half in range(2):
        table[:, ENTRIES:SOURCES, half * 128 : half * 128 + 128] = (
            spread[half].reshape(16, 32, 128).astype(BF16)
        )


def build_mats(w_fine, m0, mx, my, mz):
    zero = jnp.zeros((128, 128), BF16)
    none = jnp.zeros((64, 64), BF16)

    def put(ref, i, j, value):
        ref[i * 128 : (i + 1) * 128, j * 128 : (j + 1) * 128] = value

    def quad(a, b, c, d):
        return jnp.concatenate(
            [jnp.concatenate([a, b], axis=1), jnp.concatenate([c, d], axis=1)], axis=0
        )

    w = [w_fine[t] for t in range(7)]
    c = quad(w[0], w[6], w[5], w[0])
    d1, d2, d3, d4 = (quad(w[t], none, none, w[t]) for t in range(1, 5))
    ez = quad(none, w[5], w[6], none)
    for a in range(2):
        for e in range(2):
            i = a * 2 + e
            put(m0, i, i, c)
            put(m0, i, (1 - a) * 2 + e, d1 if a == 1 else d2)
            put(m0, i, a * 2 + (1 - e), d3 if e == 1 else d4)
            put(m0, i, 3 - i, zero)
    for i in range(2):
        for j in range(2):
            put(mx.at[0], i, j, d1 if i == j else zero)
            put(mx.at[1], i, j, d2 if i == j else zero)
            put(mz, i, j, ez if i == j else zero)
    put(my, 0, 0, zero)
    put(my, 1, 1, zero)
    put(my, 0, 1, d3)
    put(my, 1, 0, d4)


def block_kernel(
    groups, subs,
    feats_in, grad_in, neighbours, w_fine, w_down_in, w_up_in, nbrs, w_lift_in, w_coarse_in, w_back_in,
    fine_to, feats_grad, up_all, down_all, fine_all, taps_to, mean_to, grad_to, coarse_to, dpre_to, in_to, back_to, sum_to,
    feats, grad, w_down, w_up, w_lift, w_coarse, w_back,
    fine_out, taps_out, out_mean, out_grad, out_coarse, out_dpre, out_in, out_back, out_sum,
    q, g, sx, sy, sz, hidden, slope, pooled, pool_slope, grad_merged, slab, back_add,
    wide, faces, border, table, slot_wide, spread_out, rim, asked, wanted, source_of, entry_of,
    asked_at, source_at, entry_at, send, send_2, recv_2, m0, mx, my, mz, base, node, first, pack,
    flat, taps, inner, merged, dpre, x_back, y_back, z_back,
    up_parts, up_core, up_mid, up_in, up_slots, down_parts, down_core, down_mid, down_in, down_slots,
    fine_parts, fine_in, fine_slots,
    sems_in, sems_out, sems_s, sems_a, sems_b, sems_c, sems_d, sems_n,
    up_a, up_b, up_c, up_d, up_e, down_a, down_b, down_c, down_d, down_e, fine_a, fine_b, fine_c,
):
    gi, si = lax.axis_index("grp"), lax.axis_index("sub")
    near, over_grp, over_sub, heard = peers_of(groups, subs)
    ys = groups // 2
    yi, ci = gi // 2, lax.rem(gi, 2)
    twin = [(2 * yi + 1 - ci, si)]
    over_y = [(2 * lax.rem(yi + k, ys) + ci, si) for k in range(1, ys)]
    greeted = greet(near + over_grp + over_sub)
    up_rows, down_rows, fine_rows = 256 // subs, 512 // subs, 256 // groups

    def add(own, incoming, copies):
        wait_all(copies)
        value = own.astype(F32)
        for k in range(len(copies)):
            value = value + incoming[k].astype(F32)
        return value.astype(BF16)

    def join(slots, copies, count):
        wait_all(copies)
        value = slots[0].astype(F32)
        for k in range(1, count):
            value = value + slots[k].astype(F32)
        return value.astype(BF16)

    def to_twin(parts, core_in, sems):
        return send_all(twin, sems, lambda k, peer: parts.at[1 - ci], lambda k, peer: core_in)

    def over_chips(parts, core_in, mid, incoming, copies, sems):
        wait_all(copies)
        mid[...] = (parts[ci].astype(F32) + core_in[...].astype(F32)).astype(BF16)
        return send_all(over_sub, sems, lambda k, peer: mid.at[peer[1]], lambda k, peer: incoming.at[k])

    def along_y(mid, incoming, slots, copies, sems):
        slots[yi] = add(mid[si], incoming, copies)
        return send_all(over_y, sems, lambda k, peer: slots.at[yi], lambda k, peer: slots.at[yi])

    def spread(slots, everything, copies, sems):
        everything[ci, si] = join(slots, copies, ys)
        return send_all(
            over_sub, sems, lambda k, peer: everything.at[ci, si], lambda k, peer: everything.at[ci, si]
        )

    def share(everything, copies, sems):
        sent = []
        for k in range(subs):
            if k > 0:
                copies[k - 1].wait_recv()
            part = everything.at[ci, si if k == 0 else heard[k - 1]]
            copy = pltpu.make_async_remote_copy(
                src_ref=part,
                dst_ref=part,
                send_sem=sems.at[0, k],
                recv_sem=sems.at[1, k],
                device_id=twin[0],
                device_id_type=MESH,
            )
            copy.start()
            sent.append(copy)
        for copy in copies:
            copy.wait_send()
        return sent

    loads = copy_all(
        ((feats_in, feats), (grad_in, grad), (w_up_in, w_up), (w_down_in, w_down)), sems_in, 0
    )
    local, slot, number, source = entries(neighbours, gi * subs + si)
    wanted[...] = dot_tn(slot, (number + 1).astype(F32).astype(BF16))[0:32].reshape(4, 8, 128).astype(jnp.int32)
    greeted()
    asking = send_near(near, sems_a, wanted, asked)
    entry = (iota(ENTRIES, 128, 0) + 1).astype(F32).astype(BF16)
    entry_of[...] = dot_tn(slot, entry)[0:32].astype(jnp.int32)
    source_of[...] = source
    numbers = copy_all(((source_of, source_at), (entry_of, entry_at)), sems_s, 0)
    loads += copy_all(
        ((w_lift_in, w_lift), (w_coarse_in, w_coarse), (w_back_in, w_back)), sems_in, len(loads)
    )

    perm = perm_to()
    loads[0].wait()
    pooled_rows(load_natural(feats), perm, q, wide)
    by_brick([layer(wide, *where) for where in FACES], rim, border)
    faces[SOURCES] = jnp.zeros((16, 256), BF16)
    wait_all(asking)
    asked_copy = copy_all(((asked, asked_at),), sems_s, 2)
    eye = one_hot(iota(ENTRIES, 128, 0) == iota(ENTRIES, 128, 1))
    given = one_hot(asked[...].reshape(32, 128) - 1 == iota(32, 128, 1))
    wait_all(asked_copy)
    for p in range(4):
        for i in range(SLOTS):
            row = jnp.clip(asked_at[p, i, 0] - 1, 0, ENTRIES - 1)
            send[p, i] = border[row]
    sending = []
    for p in (0, 3, 1, 2):
        copy = pltpu.make_async_remote_copy(
            src_ref=send.at[p],
            dst_ref=faces.at[pl.ds(ENTRIES + (3 - p) * 8, SLOTS)],
            send_sem=sems_b.at[0, p],
            recv_sem=sems_b.at[1, 3 - p],
            device_id=near[p],
            device_id_type=MESH,
        )
        copy.start()
        sending.append(copy)

    local_back = dot_tn(local, eye)[0:ENTRIES].astype(BF16)
    given_back = dot_tn(given, eye[0:32])[0:ENTRIES].astype(BF16)
    back_add[...] = local_back + rolled(given_back, ENTRIES)
    spread_out[...] = jnp.zeros_like(spread_out)
    faces[0:ENTRIES] = border[...]
    loads[1].wait()
    pooled_rows(load_natural(grad), perm, g)
    build_mats(w_fine, m0, mx, my, mz)
    base[...] = dot(q[...], m0[...])
    loads[2].wait()
    merged_grad = dot_nt(g[...], w_up[...])
    grad_merged[...] = merged_grad
    total = jnp.sum(g[...].astype(F32), axis=0, keepdims=True).astype(BF16).astype(F32)
    low = low_lanes(512)
    for z in range(4):
        at = z * 128
        sx[at : at + 96, 0:256] = q[at + 32 : at + 128, 0:256]
        sx[at + 32 : at + 128, 256:512] = q[at : at + 96, 256:512]
    wait_all(numbers)
    loads[3].wait()

    wait_all(sending)
    for d in range(6):
        for b in range(8):
            row = jnp.clip(source_at[d * 8 + b, 0], 0, SOURCES)
            face = faces[row].astype(F32)
            for half in range(2):
                rim[d, half, pl.ds(b, 16, stride=8), :] = face[:, half * 128 : half * 128 + 128]
    for z in range(4):
        at = z * 128
        for half in range(2):
            first_lanes, last_lanes = slice(half * 128, half * 128 + 128), slice(half * 128 + 256, half * 128 + 384)
            sx[at + 96 : at + 128, first_lanes] = rim[0, half, z * 32 : z * 32 + 32, :].astype(BF16)
            sx[at : at + 32, last_lanes] = rim[1, half, z * 32 : z * 32 + 32, :].astype(BF16)
    for a in range(2):
        lanes = slice(a * 256, a * 256 + 128)
        part = wide[:, lanes].reshape(16, 32, 128)
        edge = rim[2, a].reshape(16, 8, 128)
        sy[:, lanes] = jnp.concatenate([part[:, 8:], edge], axis=1).reshape(512, 128).astype(BF16)
        lanes = slice(a * 256 + 128, a * 256 + 256)
        part = wide[:, lanes].reshape(16, 32, 128)
        edge = rim[3, a].reshape(16, 8, 128)
        sy[:, lanes] = jnp.concatenate([edge, part[:, :24]], axis=1).reshape(512, 128).astype(BF16)
        above, below = rim[4, a], rim[5, a]
        for e in range(2):
            lanes = slice((a * 2 + e) * 128, (a * 2 + e) * 128 + 128)
            part = wide[:, lanes]
            edge_up = above if e == 0 else pltpu.roll(above, 64, 1)
            edge_down = pltpu.roll(below, 64, 1) if e == 0 else below
            up = jnp.concatenate([part[128:], edge_up], axis=0)
            down = jnp.concatenate([edge_down, part[:384]], axis=0)
            sz[:, lanes] = jnp.where(low, up, down).astype(BF16)
    for a in range(2):
        lanes = slice(a * 256, a * 256 + 256)
        other = slice(256 - a * 256, 512 - a * 256)
        pre = (
            base[:, lanes]
            + dot(sx[:, other], mx[1 - a])
            + dot(sy[:, lanes], my[...])
            + dot(sz[:, lanes], mz[...])
        )
        s = sigmoid(pre)
        hidden[:, lanes] = (pre * s).astype(BF16)
        slope[:, lanes] = s * (1.0 + pre * (1.0 - s))
    pre = dot(hidden[...], w_down[...])
    s = sigmoid(pre)
    value = (pre * s).astype(BF16)
    mean = jnp.sum(value.astype(F32), axis=0, keepdims=True) * (1.0 / 512.0)
    mean = mean.astype(BF16).astype(F32)
    for k in range(2):
        node[k : k + 1, :] = mean[:, k * 128 : k * 128 + 128]
    for k in range(4):
        node[2 + k : 3 + k, :] = total[:, k * 128 : k * 128 + 128]
    sending = send_all(over_grp, sems_c, lambda k, peer: node, lambda k, peer: first.at[gi])
    pooled[...] = value
    pool_slope[...] = s * (1.0 + pre * (1.0 - s))
    first[gi] = node[...]
    part = dot_tn(value, g[...])
    for c in range(2):
        for i in range(subs):
            for k in range(2):
                up_parts[c, i, k * up_rows : (k + 1) * up_rows, :] = part[
                    i * up_rows : (i + 1) * up_rows, c * 256 + k * 128 : c * 256 + (k + 1) * 128
                ].astype(BF16)
    up_sent = to_twin(up_parts, up_core, up_a)
    wait_all(sending)
    for i in range(groups):
        pack[6 * i : 6 * i + 6, :] = first[i]
    slab[si] = pack[...].astype(BF16)
    sending = send_all(over_sub, sems_d, lambda k, peer: slab.at[si], lambda k, peer: slab.at[si])
    up_sent = over_chips(up_parts, up_core, up_mid, up_in, up_sent, up_b)
    wait_all(sending)

    nodes = groups * subs
    me = gi * subs + si
    for s in range(subs):
        flat[s * groups * 6 : (s + 1) * groups * 6, :] = slab[s].astype(F32)
    pieces = [flat[pl.ds(k, nodes, stride=6), :] for k in range(6)]
    rows, cols = iota(nodes, nodes, 0), iota(nodes, nodes, 1)
    order = one_hot(lax.rem(rows, subs) * groups + rows // subs == cols)
    gathered = dot(order, jnp.concatenate(pieces, axis=1).astype(BF16)).astype(BF16)
    node_mean, grad_sum = gathered[:, :256], gathered[:, 256:]
    node_grad = dot_nt(grad_sum, w_up[...]).astype(BF16)
    wait_all(loads[4:])
    coarse_in = dot(node_mean, w_lift[...]).astype(BF16)
    picks = [one_hot(nbrs[d : d + 1, :] == rows) for d in range(6)]
    taps[:, 0:512] = coarse_in
    for d in range(6):
        taps[:, (d + 1) * 512 : (d + 2) * 512] = dot_tn(picks[d], coarse_in).astype(BF16)
    coarse_pre = jnp.zeros((nodes, 512), F32)
    for t in range(7):
        coarse_pre = coarse_pre + dot(taps[:, t * 512 : (t + 1) * 512], w_coarse[t])
    s = sigmoid(coarse_pre)
    coarse_out = (coarse_pre * s).astype(BF16)
    coarse_slope = s * (1.0 + coarse_pre * (1.0 - s))
    coarse_dpre = (dot_nt(node_grad, w_back[...]) * coarse_slope).astype(BF16)
    in_grad = dot_nt(coarse_dpre, w_coarse[0])
    for d in range(6):
        moved = dot(picks[d], coarse_dpre).astype(BF16)
        in_grad = in_grad + dot_nt(moved, w_coarse[d + 1])
    in_grad = in_grad.astype(BF16)
    mine = one_hot(iota(16, nodes, 1) == me)
    mean_grad = dot_nt(dot(mine, in_grad).astype(BF16), w_lift[...])[0:1] * (1.0 / 512.0)


    pool_dpre = ((grad_merged[...] + mean_grad) * pool_slope[...]).astype(BF16)
    part = dot_tn(hidden[...], pool_dpre)
    for c in range(2):
        down_parts[c] = part[:, c * 128 : (c + 1) * 128].reshape(subs, down_rows, 128).astype(BF16)
    down_sent = to_twin(down_parts, down_core, down_a)
    up_sent = along_y(up_mid, up_in, up_slots, up_sent, up_c)
    dpre[...] = ((g[...].astype(F32) + dot_nt(pool_dpre, w_down[...])) * slope[...]).astype(BF16)

    def block(value, i, j):
        return value[i * 128 : (i + 1) * 128, j * 128 : (j + 1) * 128]

    def fold(value):
        return value[:64] + pltpu.roll(value[64:], 64, 1)

    down_sent = over_chips(down_parts, down_core, down_mid, down_in, down_sent, down_b)
    centre = dot_tn(q[...], dpre[...])
    gx0 = dot_tn(sx[:, 0:256], dpre[:, 256:512])
    gx1 = dot_tn(sx[:, 256:512], dpre[:, 0:256])
    gy = [dot_tn(sy[:, a * 256 : a * 256 + 256], dpre[:, a * 256 : a * 256 + 256]) for a in range(2)]
    gz = [dot_tn(sz[:, a * 256 : a * 256 + 256], dpre[:, a * 256 : a * 256 + 256]) for a in range(2)]
    middle = sum(block(centre, i, i) for i in range(4))
    x_up = block(centre, 2, 0) + block(centre, 3, 1) + block(gx0, 0, 0) + block(gx0, 1, 1)
    x_down = block(centre, 0, 2) + block(centre, 1, 3) + block(gx1, 0, 0) + block(gx1, 1, 1)
    y_up = block(centre, 1, 0) + block(centre, 3, 2) + block(gy[0], 0, 1) + block(gy[1], 0, 1)
    y_down = block(centre, 0, 1) + block(centre, 2, 3) + block(gy[0], 1, 0) + block(gy[1], 1, 0)
    between = sum(block(value, i, i) for value in gz for i in range(2))
    z_up = middle[64:] + pltpu.roll(between[:64], 64, 1)
    z_down = pltpu.roll(middle[:64], 64, 1) + between[64:]
    tap_sums = [fold(middle), fold(x_up), fold(x_down), fold(y_up), fold(y_down), z_up, z_down]
    tap_sums.append(jnp.zeros((64, 128), F32))
    low = low_lanes(64)
    for pair in range(4):
        both = jnp.where(low, tap_sums[2 * pair], pltpu.roll(tap_sums[2 * pair + 1], 64, 1))
        each = fine_rows if fine_rows < 64 else 64
        for i in range(64 // each):
            row = pair * 64 + i * each
            at = row % fine_rows
            fine_parts[row // fine_rows, at : at + each, :] = both[i * each : (i + 1) * each].astype(BF16)
    fine_sent = send_all(over_grp, fine_a, lambda k, peer: fine_parts.at[peer[0]], lambda k, peer: fine_in.at[k])

    up_sent = spread(up_slots, up_all, up_sent, up_d)
    x_back[:, 0:256] = dot_nt(dpre[:, 256:512], mx[0])
    x_back[:, 256:512] = dot_nt(dpre[:, 0:256], mx[1])
    for a in range(2):
        lanes = slice(a * 256, a * 256 + 256)
        y_back[:, lanes] = dot_nt(dpre[:, lanes], my[...])
        z_back[:, lanes] = dot_nt(dpre[:, lanes], mz[...])
    backs = (x_back, y_back, z_back)
    layers = [layer(backs[where[0]], *where) for where in BEYOND]
    by_brick(layers, rim, border)
    pick_slots(entry_at, border, send_2)
    fine_slots[si] = add(fine_parts[gi], fine_in, fine_sent)
    fine_sent = send_all(over_sub, fine_b, lambda k, peer: fine_slots.at[si], lambda k, peer: fine_slots.at[si])
    slots_sent = send_near(near, sems_n, send_2, recv_2)
    table[:, 0:ENTRIES, :] = by_place(layers)
    for ref, value in (
        (out_mean, node_mean), (out_grad, node_grad), (out_coarse, coarse_out),
        (out_dpre, coarse_dpre), (out_in, in_grad),
        (out_back, dot(coarse_out, w_back[...]).astype(BF16)), (out_sum, grad_sum),
    ):
        ref[...] = value
    stores = copy_all(
        (
            (out_dpre, dpre_to), (out_mean, mean_to), (out_grad, grad_to),
            (out_coarse, coarse_to), (out_in, in_to), (out_back, back_to), (out_sum, sum_to),
        ),
        sems_out,
        0,
    )

    down_sent = along_y(down_mid, down_in, down_slots, down_sent, down_c)
    turned = dot_tn(coarse_in, one_hot(rows == cols)).astype(BF16)
    taps_out[0:512, :] = turned
    for d in range(6):
        taps_out[(d + 1) * 512 : (d + 2) * 512, :] = dot(turned, picks[d]).astype(BF16)
    stores += copy_all(((taps_out, taps_to),), sems_out, len(stores))
    back = dot(dot(mine, coarse_out).astype(BF16), w_back[...])[0:1]
    merged[...] = (pooled[...].astype(F32) + back).astype(BF16)
    inner[...] = g[...].astype(F32) + dot_nt(dpre[...], m0[...])
    down_sent = spread(down_slots, down_all, down_sent, down_d)

    for z in range(4):
        at = z * 128
        inner[at + 32 : at + 128, 0:256] += x_back[at : at + 96, 0:256]
        inner[at : at + 96, 256:512] += x_back[at + 32 : at + 128, 256:512]
    for zu in range(16):
        at = zu * 32
        for a in range(2):
            low_half, high_half = slice(a * 256, a * 256 + 128), slice(a * 256 + 128, a * 256 + 256)
            inner[at + 8 : at + 32, low_half] += y_back[at : at + 24, low_half]
            inner[at : at + 24, high_half] += y_back[at + 8 : at + 32, high_half]
    low = low_lanes(384)
    for i in range(4):
        lanes = slice(i * 128, i * 128 + 128)
        inner[128:512, lanes] += jnp.where(low, z_back[0:384, lanes], 0.0)
        inner[0:384, lanes] += jnp.where(low, 0.0, z_back[128:512, lanes])
    back_perm = perm_from()
    out = q[...].astype(F32) + hidden[...].astype(F32) + dot(merged[...], w_up[...])
    fine_out[...] = natural_rows(out.astype(BF16), back_perm)
    stores += copy_all(((fine_out, fine_to),), sems_out, len(stores))

    fine_all[gi] = join(fine_slots, fine_sent, subs)
    fine_sent = send_all(over_grp, fine_c, lambda k, peer: fine_all.at[gi], lambda k, peer: fine_all.at[gi])
    up_sent = share(up_all, up_sent, up_e)
    wait_all(slots_sent)
    unpack_slots(recv_2, spread_out, table)
    for place in range(16):
        slot_wide[place] = dot(back_add[:, 0:SOURCES], table[place])
    for f in range(6):
        add_layer(inner, *FACES[f], slot_wide[:, f * 8 : f * 8 + 8, :].reshape(128, 256))
    feats_grad[...] = natural_rows(inner[...].astype(BF16), back_perm)
    down_sent = share(down_all, down_sent, down_e)
    wait_all(up_sent)
    wait_all(fine_sent)
    wait_all(down_sent)
    wait_all(stores)


def finish_kernel(
    groups, subs,
    fine_in, feats_in, up_in, down_in, fine_sum_in, taps_in, mean_in, grad_in, coarse_in, dpre_in, in_grad_in, back_in, sum_in,
    fine_to, feats_to, w_fine_to, w_down_to, w_lift_to, w_coarse_to, w_back_to, w_up_to,
    fine_out, feats_out, up_all, down_all, fine_all, taps, node_mean, node_grad, coarse_out, dpre, in_grad, back, grad_sum,
    w_fine_grad, w_down_grad, w_lift_grad, w_coarse_grad, w_back_grad, w_up_grad,
    sems_in, sems_out,
):
    first = copy_all(
        ((dpre_in, dpre),) + tuple((taps_in.at[pl.ds(t * 512, 512)], taps.at[pl.ds(t * 512, 512)]) for t in range(7)),
        sems_in,
        0,
    )
    rest = copy_all(
        (
            (back_in, back), (sum_in, grad_sum), (up_in, up_all), (down_in, down_all), (fine_sum_in, fine_all), (coarse_in, coarse_out),
            (grad_in, node_grad), (mean_in, node_mean), (in_grad_in, in_grad), (fine_in, fine_out), (feats_in, feats_out),
        ),
        sems_in,
        8,
    )
    stores = []

    def store(src, dst):
        stores.extend(copy_all(((src, dst),), sems_out, len(stores)))

    first[0].wait()
    for t in range(7):
        first[t + 1].wait()
        w_coarse_grad[t] = dot(taps[t * 512 : (t + 1) * 512, :], dpre[...])
        store(w_coarse_grad.at[t], w_coarse_to.at[t])
    up_rows, down_rows = 256 // subs, 512 // subs
    wait_all(rest[0:3])
    w_up_grad[...] = dot_tn(back[...], grad_sum[...])
    for c in range(2):
        for i in range(subs):
            for k in range(2):
                w_up_grad[i * up_rows : (i + 1) * up_rows, c * 256 + k * 128 : c * 256 + (k + 1) * 128] += up_all[
                    c, i, k * up_rows : (k + 1) * up_rows, :
                ].astype(F32)
    store(w_up_grad, w_up_to)
    rest[3].wait()
    for c in range(2):
        w_down_grad[:, c * 128 : (c + 1) * 128] = down_all[c].astype(F32).reshape(512, 128)
    store(w_down_grad, w_down_to)
    rest[4].wait()
    sums = fine_all[...].astype(F32).reshape(256, 128)
    for pair in range(4):
        both = sums[pair * 64 : (pair + 1) * 64]
        w_fine_grad[2 * pair] = both[:, 0:64]
        if pair < 3:
            w_fine_grad[2 * pair + 1] = pltpu.roll(both, 64, 1)[:, 0:64]
    store(w_fine_grad, w_fine_to)
    wait_all(rest[5:9])
    w_back_grad[...] = dot_tn(coarse_out[...], node_grad[...])
    store(w_back_grad, w_back_to)
    w_lift_grad[...] = dot_tn(node_mean[...], in_grad[...])
    store(w_lift_grad, w_lift_to)
    rest[9].wait()
    store(fine_out, fine_to)
    rest[10].wait()
    store(feats_out, feats_to)
    wait_all(stores)


def spec(space=pltpu.VMEM):
    return pl.BlockSpec(memory_space=space)


def shape(dims, dtype):
    return jax.ShapeDtypeStruct(dims, dtype)


def buf(dims, dtype=BF16):
    return pltpu.VMEM(dims, dtype)


def pairs(count):
    return pltpu.SemaphoreType.DMA((2, count))


def body(groups, subs, feats, neighbours, w_fine, w_down, w_lift, coarse_nbrs, w_coarse, w_back, w_up, grad_out):
    nodes = groups * subs
    vmem, anywhere = spec(), spec(pl.ANY)
    sq16, sq32 = buf((512, 512)), buf((512, 512), F32)
    natural = shape((64, 8, 512), BF16)
    chunk = (512 // subs, 128)
    fine_chunk = (256 // groups, 128)
    sums = (
        shape((2, subs) + chunk, BF16), shape((2, subs) + chunk, BF16), shape((groups,) + fine_chunk, BF16),
    )
    coarse = (
        shape((7 * 512, nodes), BF16), shape((nodes, 256), BF16), shape((nodes, 256), BF16),
        shape((nodes, 512), BF16), shape((nodes, 512), BF16), shape((nodes, 512), BF16),
        shape((nodes, 256), BF16), shape((nodes, 512), BF16),
    )
    slots = buf((4, SLOTS, 16, 256))
    reduction = [
        buf((2, subs) + chunk), buf((subs,) + chunk), buf((subs,) + chunk),
        buf((subs - 1,) + chunk), buf((groups // 2,) + chunk),
    ]
    reduction_sems = [pairs(1), pairs(subs - 1), pairs(groups // 2 - 1), pairs(subs - 1), pairs(subs)]

    def like(x):
        return buf(x.shape, x.dtype)

    results = pl.pallas_call(
        functools.partial(block_kernel, groups, subs),
        out_shape=(natural, natural) + sums + coarse,
        in_specs=[anywhere, anywhere, vmem, vmem, anywhere, anywhere, vmem, anywhere, anywhere, anywhere],
        out_specs=(anywhere,) + (vmem,) * 4 + (anywhere,) * 8,
        scratch_shapes=[like(natural), like(natural)]
        + [buf((512, 256)), buf((256, 512)), buf((256, 512)), buf((7, 512, 512)), buf((512, 256))]
        + [like(natural)]
        + [like(x) for x in coarse]
        + [sq16] * 6
        + [sq32, buf((512, 256)), buf((512, 256), F32), buf((512, 256), F32)]
        + [buf((subs, groups * 6, 128)), buf((ENTRIES, 128))]
        + [sq32, buf((SOURCES + 1, 16, 256)), buf((ENTRIES, 16, 256))]
        + [buf((16, SOURCES, 256)), buf((16, ENTRIES, 256), F32), buf((2, 512, 128), F32), buf((6, 2, 128, 128), F32)]
        + [buf((4, 8, 128), I32), buf((4, 8, 128), I32), buf((ENTRIES, 128), I32), buf((32, 128), I32)]
        + [pltpu.SMEM((4, 8, 128), I32), pltpu.SMEM((ENTRIES, 128), I32), pltpu.SMEM((32, 128), I32)]
        + [slots, slots, slots]
        + [sq16, buf((2, 256, 256)), buf((256, 256)), buf((256, 256))]
        + [sq32, buf((6, 128), F32), buf((groups, 6, 128), F32), buf((groups * 6, 128), F32)]
        + [buf((nodes * 6, 128), F32), buf((nodes, 7 * 512)), sq32, buf((512, 256)), sq16, sq32, sq32, sq32]
        + reduction
        + reduction
        + [buf((groups,) + fine_chunk), buf((groups - 1,) + fine_chunk), buf((subs,) + fine_chunk)]
        + [pltpu.SemaphoreType.DMA((7,)), pltpu.SemaphoreType.DMA((9,)), pltpu.SemaphoreType.DMA((3,))]
        + [pairs(4), pairs(4), pairs(groups - 1), pairs(subs - 1), pairs(4)]
        + reduction_sems
        + reduction_sems
        + [pairs(groups - 1), pairs(subs - 1), pairs(groups - 1)],
        compiler_params=pltpu.CompilerParams(collective_id=1, has_side_effects=True, vmem_limit_bytes=MEMORY),
        name="block",
    )(
        feats.reshape(64, 8, 512), grad_out.reshape(64, 8, 512), neighbours,
        w_fine, w_down, w_up, coarse_nbrs.T, w_lift, w_coarse, w_back,
    )

    grads = (
        shape((7, 64, 64), F32), shape((512, 256), F32), shape((256, 512), F32),
        shape((7, 512, 512), F32), shape((512, 256), F32), shape((256, 512), F32),
    )
    outs = pl.pallas_call(
        functools.partial(finish_kernel, groups, subs),
        out_shape=(natural, natural) + grads,
        in_specs=[anywhere] * 13,
        out_specs=(anywhere,) * 8,
        scratch_shapes=[like(natural), like(natural)]
        + [like(x) for x in sums + coarse + grads]
        + [pltpu.SemaphoreType.DMA((19,)), pltpu.SemaphoreType.DMA((14,))],
        compiler_params=pltpu.CompilerParams(vmem_limit_bytes=MEMORY),
        name="finish",
    )(*results)
    return (outs[0].reshape(8, 8, 8, 512), outs[1].reshape(8, 8, 8, 512)) + tuple(outs[2:])


def solution(mesh):
    groups, subs = mesh.shape["grp"], mesh.shape["sub"]
    split4 = P(("grp", "sub"), None, None, None)
    return jax.shard_map(
        functools.partial(body, groups, subs),
        mesh=mesh,
        in_specs=(split4, P(("grp", "sub"), None)) + (P(),) * 7 + (split4,),
        out_specs=(split4, split4) + (P(),) * 6,
        check_vma=False,
    )
```

```python
import functools

import jax
import jax.numpy as jnp
from jax import lax
from jax.experimental import pallas as pl
from jax.experimental.pallas import tpu as pltpu
from jax.sharding import PartitionSpec as P

F32 = jnp.float32
BF16 = jnp.bfloat16
I32 = jnp.int32
MESH = pl.DeviceIdType.MESH
OFFSETS = (-2, -1, 1, 2)
MEMORY = 58 << 20
ENTRIES = 48
SOURCES = ENTRIES + 32
SLOTS = 6


def dot(x, y):
    return jnp.dot(x, y, preferred_element_type=F32)


def dot_nt(x, y):
    return lax.dot_general(x, y, (((1,), (1,)), ((), ())), preferred_element_type=F32)


def dot_tn(x, y):
    return lax.dot_general(x, y, (((0,), (0,)), ((), ())), preferred_element_type=F32)


def sigmoid(v):
    return 1.0 / (1.0 + jnp.exp(-v))


def perm_index(y):
    a, e = (y >> 8) & 1, (y >> 7) & 1
    u, w, b = (y >> 5) & 3, (y >> 3) & 3, y & 7
    return b * 64 + (2 * u + a) * 8 + 2 * w + e


def perm_to():
    rows = lax.broadcasted_iota(jnp.int32, (512, 512), 0)
    cols = lax.broadcasted_iota(jnp.int32, (512, 512), 1)
    return (perm_index(rows) == cols).astype(F32).astype(BF16)


def perm_from():
    rows = lax.broadcasted_iota(jnp.int32, (512, 512), 0)
    cols = lax.broadcasted_iota(jnp.int32, (512, 512), 1)
    return (perm_index(cols) == rows).astype(F32).astype(BF16)


def load_natural(ref):
    return ref[...].astype(F32).reshape(512, 512).astype(BF16)


def pooled_rows(x, perm, out_ref, wide_ref=None):
    y = dot(perm, x)
    for z in range(4):
        for ae in range(4):
            block = y[ae * 128 : (ae + 1) * 128, z * 128 : (z + 1) * 128]
            where = (pl.ds(z * 128, 128), pl.ds(ae * 128, 128))
            out_ref[where] = block.astype(BF16)
            if wide_ref is not None:
                wide_ref[where] = block


def natural_rows(q, perm_back):
    y = jnp.concatenate(
        [
            jnp.concatenate(
                [q[z * 128 : (z + 1) * 128, ae * 128 : (ae + 1) * 128] for z in range(4)], axis=1
            )
            for ae in range(4)
        ],
        axis=0,
    )
    return dot(perm_back, y).reshape(64, 8, 512).astype(BF16)


def low_lanes(rows):
    return lax.broadcasted_iota(jnp.int32, (rows, 128), 1) < 64


def layer(ref, axis, place, parity):
    if axis == 0:
        return jnp.concatenate(
            [
                ref[z * 128 + place * 32 : z * 128 + place * 32 + 32, parity * 256 : parity * 256 + 256]
                for z in range(4)
            ],
            axis=0,
        )
    if axis == 1:
        parts = []
        for a in range(2):
            lane = (a * 2 + parity) * 128
            parts.append(
                jnp.concatenate(
                    [ref[zu * 32 + place * 8 : zu * 32 + place * 8 + 8, lane : lane + 128] for zu in range(16)],
                    axis=0,
                )
            )
        return jnp.concatenate(parts, axis=1)
    parts = []
    for a in range(2):
        first = ref[place * 128 : place * 128 + 128, a * 256 : a * 256 + 128]
        second = ref[place * 128 : place * 128 + 128, a * 256 + 128 : a * 256 + 256]
        if parity == 0:
            second = pltpu.roll(second, 64, 1)
        else:
            first = pltpu.roll(first, 64, 1)
        parts.append(jnp.where(low_lanes(128), first, second))
    return jnp.concatenate(parts, axis=1)


def add_layer(ref, axis, place, parity, value):
    if axis == 0:
        for z in range(4):
            rows = pl.ds(z * 128 + place * 32, 32)
            ref[rows, parity * 256 : parity * 256 + 256] += value[z * 32 : z * 32 + 32]
    elif axis == 1:
        for a in range(2):
            lane = (a * 2 + parity) * 128
            for zu in range(16):
                rows = pl.ds(zu * 32 + place * 8, 8)
                ref[rows, lane : lane + 128] += value[zu * 8 : zu * 8 + 8, a * 128 : a * 128 + 128]
    else:
        low = low_lanes(128)
        rows = pl.ds(place * 128, 128)
        for a in range(2):
            part = value[:, a * 128 : a * 128 + 128]
            turned = pltpu.roll(part, 64, 1)
            first, second = (part, turned) if parity == 0 else (turned, part)
            keep = low if parity == 0 else ~low
            ref[rows, a * 256 : a * 256 + 128] += jnp.where(keep, first, 0.0)
            ref[rows, a * 256 + 128 : a * 256 + 256] += jnp.where(keep, second, 0.0)


FACES = ((0, 3, 1), (0, 0, 0), (1, 3, 1), (1, 0, 0), (2, 3, 1), (2, 0, 0))
BEYOND = ((0, 3, 0), (0, 0, 1), (1, 3, 0), (1, 0, 1), (2, 3, 0), (2, 0, 1))


def one_hot(mask):
    return mask.astype(F32).astype(BF16)


def iota(rows, cols, axis):
    return lax.broadcasted_iota(jnp.int32, (rows, cols), axis)


def entries(neighbours, me):
    nb = neighbours[...]
    n = jnp.concatenate([jnp.broadcast_to(nb[:, d : d + 1], (8, 128)) for d in range(6)], axis=0)
    lane = iota(ENTRIES, 128, 1)
    direction = iota(ENTRIES, 128, 0) >> 3
    offset = (n >> 3) - me
    number = (direction ^ 1) * 8 + (n & 7)
    local = (n >= 0) & (offset == 0)
    peer = lane >> 3
    peer_offset = jnp.where(peer < 2, peer - 2, peer - 1)
    far = (n >= 0) & (lane < 32) & (offset == peer_offset)
    before = one_hot(iota(ENTRIES, ENTRIES, 1) < iota(ENTRIES, ENTRIES, 0))
    count = dot(before, one_hot(far))
    slot = far & (count == (lane & 7).astype(F32))
    place = jnp.sum(jnp.where(slot, lane + 1, 0), axis=1, keepdims=True)
    source = jnp.where(local, number, jnp.where(place > 0, ENTRIES - 1 + place, SOURCES))
    return one_hot(local & (lane == number)), one_hot(slot), number, source


def rolled(x, by):
    return pltpu.roll(x.astype(F32), by, 1).astype(BF16)


def coords(groups, subs, offset):
    nodes = groups * subs
    at = lax.axis_index("grp") * subs + lax.axis_index("sub")
    to = lax.rem(at + offset + nodes, nodes)
    return (to // subs, lax.rem(to, subs))


def ring(a, b, size):
    return min((a - b) % size, (b - a) % size)


def peers_of(groups, subs):
    g, s = lax.axis_index("grp"), lax.axis_index("sub")
    near = [coords(groups, subs, off) for off in OFFSETS]
    y, core = g // 2, lax.rem(g, 2)
    steps = [(dy, dc) for dy in range(groups // 2) for dc in range(2) if dy or dc]
    steps.sort(key=lambda d: -4 * ring(d[0], 0, groups // 2) - d[1])
    over_grp = [(lax.rem(y + dy, groups // 2) * 2 + lax.rem(core + dc, 2), s) for dy, dc in steps]
    wide = min(4, subs)
    deep = subs // wide
    z, x = s // wide, lax.rem(s, wide)
    steps = [(dz, dx) for dz in range(deep) for dx in range(wide) if dz or dx]
    steps.sort(key=lambda d: -ring(d[0], 0, deep) - ring(d[1], 0, wide))
    over_sub = [(g, lax.rem(z + dz, deep) * wide + lax.rem(x + dx, wide)) for dz, dx in steps]
    return near, over_grp, over_sub


def squares(groups, subs):
    g, s = lax.axis_index("grp"), lax.axis_index("sub")
    ys, deep = groups // 2, subs // 4
    y, core = g // 2, lax.rem(g, 2)
    z, x = s // 4, lax.rem(s, 4)
    low, high = (x ^ (x >> 1)) & 1, x >> 1
    steps = [(d, f) for d in range(ys) for f in range(2) if d or f]
    steps.sort(key=lambda d: -ring(d[0], 0, ys) - d[1])
    first = [(lax.rem(y + d, ys) * 2 + core, z * 4 + (x ^ f)) for d, f in steps]
    first_rank = [lax.rem(y + d, ys) * 2 + (low ^ f) for d, f in steps]
    heard_rank = [lax.rem(y + ys - d, ys) * 2 + (low ^ f) for d, f in steps]
    steps = [(d, f) for d in range(deep) for f in range(2) if d or f]
    steps.sort(key=lambda d: -ring(d[0], 0, deep) - d[1])
    second = [(g, lax.rem(z + d, deep) * 4 + (x ^ (3 * f))) for d, f in steps]
    return first, first_rank, heard_rank, y * 2 + low, second, z * 2 + high


def greet(peers):
    barrier = pltpu.get_barrier_semaphore()
    for peer in peers:
        pl.semaphore_signal(barrier, inc=1, device_id=peer, device_id_type=MESH)
    return lambda: pl.semaphore_wait(barrier, len(peers))


def send_all(peers, sems, src_of, dst_of):
    copies = []
    for k, peer in enumerate(peers):
        copy = pltpu.make_async_remote_copy(
            src_ref=src_of(k, peer),
            dst_ref=dst_of(k, peer),
            send_sem=sems.at[0, k],
            recv_sem=sems.at[1, k],
            device_id=peer,
            device_id_type=MESH,
        )
        copy.start()
        copies.append(copy)
    return copies


def send_near(near, sems, src, dst):
    copies = []
    for p in (0, 3, 1, 2):
        copy = pltpu.make_async_remote_copy(
            src_ref=src.at[p],
            dst_ref=dst.at[3 - p],
            send_sem=sems.at[0, p],
            recv_sem=sems.at[1, 3 - p],
            device_id=near[p],
            device_id_type=MESH,
        )
        copy.start()
        copies.append(copy)
    return copies


def copy_all(pairs, sems, first):
    copies = []
    for k, (src, dst) in enumerate(pairs):
        copy = pltpu.make_async_copy(src, dst, sems.at[first + k])
        copy.start()
        copies.append(copy)
    return copies


def wait_all(copies):
    for copy in copies:
        copy.wait()


def by_place(layers):
    return jnp.concatenate([x.reshape(16, 8, 256) for x in layers], axis=1).astype(BF16)


def by_brick(layers, stage, out):
    for which, value in enumerate(layers):
        for half in range(2):
            lanes = slice(half * 128, half * 128 + 128)
            stage[which, half] = value[:, lanes]
            for b in range(8):
                out[which * 8 + b, :, lanes] = stage[which, half, pl.ds(b, 16, stride=8), :].astype(BF16)


def pick_slots(numbers, faces, out):
    for p in range(4):
        for i in range(SLOTS):
            row = jnp.clip(numbers[p * 8 + i, 0] - 1, 0, ENTRIES - 1)
            out[p, i] = faces[row]


def unpack_slots(slots, spread, table):
    for p in range(4):
        for i in range(SLOTS):
            face = slots[p, i].astype(F32)
            for half in range(2):
                spread[half, pl.ds(p * 8 + i, 16, stride=32), :] = face[:, half * 128 : half * 128 + 128]
    for half in range(2):
        table[:, ENTRIES:SOURCES, half * 128 : half * 128 + 128] = (
            spread[half].reshape(16, 32, 128).astype(BF16)
        )


def build_mats(w_fine, m0, mx, my, mz):
    zero = jnp.zeros((128, 128), BF16)
    none = jnp.zeros((64, 64), BF16)

    def put(ref, i, j, value):
        ref[i * 128 : (i + 1) * 128, j * 128 : (j + 1) * 128] = value

    def quad(a, b, c, d):
        return jnp.concatenate(
            [jnp.concatenate([a, b], axis=1), jnp.concatenate([c, d], axis=1)], axis=0
        )

    w = [w_fine[t] for t in range(7)]
    c = quad(w[0], w[6], w[5], w[0])
    d1, d2, d3, d4 = (quad(w[t], none, none, w[t]) for t in range(1, 5))
    ez = quad(none, w[5], w[6], none)
    for a in range(2):
        for e in range(2):
            i = a * 2 + e
            put(m0, i, i, c)
            put(m0, i, (1 - a) * 2 + e, d1 if a == 1 else d2)
            put(m0, i, a * 2 + (1 - e), d3 if e == 1 else d4)
            put(m0, i, 3 - i, zero)
    for i in range(2):
        for j in range(2):
            put(mx.at[0], i, j, d1 if i == j else zero)
            put(mx.at[1], i, j, d2 if i == j else zero)
            put(mz, i, j, ez if i == j else zero)
    put(my, 0, 0, zero)
    put(my, 1, 1, zero)
    put(my, 0, 1, d3)
    put(my, 1, 0, d4)


def block_kernel(
    groups, subs,
    feats_in, grad_in, neighbours, w_fine, w_down_in, w_up_in, nbrs, w_lift_in, w_coarse_in, w_back_in,
    fine_to, feats_grad, up_all, down_all, fine_all, taps_to, mean_to, grad_to, coarse_to, dpre_to, in_to, back_to, sum_to,
    feats, grad, w_down, w_up, w_lift, w_coarse, w_back,
    fine_out, taps_out, out_mean, out_grad, out_coarse, out_dpre, out_in, out_back, out_sum,
    q, g, sx, sy, sz, hidden, slope, pooled, pool_slope, grad_merged, slab, back_add,
    wide, faces, border, table, slot_wide, spread_out, rim, asked, wanted, source_of, entry_of,
    asked_at, source_at, entry_at, send, send_2, recv_2, m0, mx, my, mz, base, node, first, pack,
    flat, taps, inner, merged, dpre, x_back, y_back, z_back,
    up_parts, up_core, up_mid, up_in, up_slots, down_parts, down_core, down_mid, down_in, down_slots,
    fine_parts, fine_core, fine_mid, fine_in, fine_slots,
    sems_in, sems_out, sems_s, sems_a, sems_b, sems_c, sems_d, sems_n,
    up_a, up_b, up_c, up_d, up_e, down_a, down_b, down_c, down_d, down_e, fine_a, fine_b, fine_c, fine_d, fine_e,
):
    gi, si = lax.axis_index("grp"), lax.axis_index("sub")
    near, over_grp, over_sub = peers_of(groups, subs)
    over_a, rank_a, heard, ai, over_b, bi = squares(groups, subs)
    na, nb = len(over_a) + 1, len(over_b) + 1
    ci = lax.rem(gi, 2)
    twin = [(gi + 1 - 2 * ci, si)]
    greeted = greet(near + over_grp + over_sub + over_a)
    up_rows, down_rows, fine_rows = 256 // na, 512 // na, 128 // na

    def add(own, incoming, copies):
        wait_all(copies)
        value = own.astype(F32)
        for k in range(len(copies)):
            value = value + incoming[k].astype(F32)
        return value.astype(BF16)

    def join(slots, copies, count):
        wait_all(copies)
        value = slots[0].astype(F32)
        for k in range(1, count):
            value = value + slots[k].astype(F32)
        return value.astype(BF16)

    def to_twin(parts, core_in, sems):
        return send_all(twin, sems, lambda k, peer: parts.at[1 - ci], lambda k, peer: core_in)

    def over_chips(parts, core_in, mid, incoming, copies, sems):
        wait_all(copies)
        mid[...] = (parts[ci].astype(F32) + core_in[...].astype(F32)).astype(BF16)
        return send_all(over_a, sems, lambda k, peer: mid.at[rank_a[k]], lambda k, peer: incoming.at[k])

    def across(mid, incoming, slots, copies, sems):
        slots[bi] = add(mid[ai], incoming, copies)
        return send_all(over_b, sems, lambda k, peer: slots.at[bi], lambda k, peer: slots.at[bi])

    def spread(slots, everything, copies, sems):
        everything[ci, ai] = join(slots, copies, nb)
        return send_all(
            over_a, sems, lambda k, peer: everything.at[ci, ai], lambda k, peer: everything.at[ci, ai]
        )

    def share(everything, copies, sems):
        sent = []
        for k in range(na):
            if k > 0:
                copies[k - 1].wait_recv()
            part = everything.at[ci, ai if k == 0 else heard[k - 1]]
            copy = pltpu.make_async_remote_copy(
                src_ref=part,
                dst_ref=part,
                send_sem=sems.at[0, k],
                recv_sem=sems.at[1, k],
                device_id=twin[0],
                device_id_type=MESH,
            )
            copy.start()
            sent.append(copy)
        for copy in copies:
            copy.wait_send()
        return sent

    loads = copy_all(
        ((feats_in, feats), (grad_in, grad), (w_up_in, w_up), (w_down_in, w_down)), sems_in, 0
    )
    local, slot, number, source = entries(neighbours, gi * subs + si)
    wanted[...] = dot_tn(slot, (number + 1).astype(F32).astype(BF16))[0:32].reshape(4, 8, 128).astype(jnp.int32)
    greeted()
    asking = send_near(near, sems_a, wanted, asked)
    entry = (iota(ENTRIES, 128, 0) + 1).astype(F32).astype(BF16)
    entry_of[...] = dot_tn(slot, entry)[0:32].astype(jnp.int32)
    source_of[...] = source
    numbers = copy_all(((source_of, source_at), (entry_of, entry_at)), sems_s, 0)
    loads += copy_all(
        ((w_lift_in, w_lift), (w_coarse_in, w_coarse), (w_back_in, w_back)), sems_in, len(loads)
    )

    perm = perm_to()
    loads[0].wait()
    pooled_rows(load_natural(feats), perm, q, wide)
    by_brick([layer(wide, *where) for where in FACES], rim, border)
    faces[SOURCES] = jnp.zeros((16, 256), BF16)
    wait_all(asking)
    asked_copy = copy_all(((asked, asked_at),), sems_s, 2)
    eye = one_hot(iota(ENTRIES, 128, 0) == iota(ENTRIES, 128, 1))
    given = one_hot(asked[...].reshape(32, 128) - 1 == iota(32, 128, 1))
    wait_all(asked_copy)
    for p in range(4):
        for i in range(SLOTS):
            row = jnp.clip(asked_at[p, i, 0] - 1, 0, ENTRIES - 1)
            send[p, i] = border[row]
    sending = []
    for p in (0, 3, 1, 2):
        copy = pltpu.make_async_remote_copy(
            src_ref=send.at[p],
            dst_ref=faces.at[pl.ds(ENTRIES + (3 - p) * 8, SLOTS)],
            send_sem=sems_b.at[0, p],
            recv_sem=sems_b.at[1, 3 - p],
            device_id=near[p],
            device_id_type=MESH,
        )
        copy.start()
        sending.append(copy)

    local_back = dot_tn(local, eye)[0:ENTRIES].astype(BF16)
    given_back = dot_tn(given, eye[0:32])[0:ENTRIES].astype(BF16)
    back_add[...] = local_back + rolled(given_back, ENTRIES)
    spread_out[...] = jnp.zeros_like(spread_out)
    faces[0:ENTRIES] = border[...]
    loads[1].wait()
    pooled_rows(load_natural(grad), perm, g)
    build_mats(w_fine, m0, mx, my, mz)
    base[...] = dot(q[...], m0[...])
    loads[2].wait()
    merged_grad = dot_nt(g[...], w_up[...])
    grad_merged[...] = merged_grad
    total = jnp.sum(g[...].astype(F32), axis=0, keepdims=True).astype(BF16).astype(F32)
    low = low_lanes(512)
    for z in range(4):
        at = z * 128
        sx[at : at + 96, 0:256] = q[at + 32 : at + 128, 0:256]
        sx[at + 32 : at + 128, 256:512] = q[at : at + 96, 256:512]
    wait_all(numbers)
    loads[3].wait()

    wait_all(sending)
    for d in range(6):
        for b in range(8):
            row = jnp.clip(source_at[d * 8 + b, 0], 0, SOURCES)
            face = faces[row].astype(F32)
            for half in range(2):
                rim[d, half, pl.ds(b, 16, stride=8), :] = face[:, half * 128 : half * 128 + 128]
    for z in range(4):
        at = z * 128
        for half in range(2):
            first_lanes, last_lanes = slice(half * 128, half * 128 + 128), slice(half * 128 + 256, half * 128 + 384)
            sx[at + 96 : at + 128, first_lanes] = rim[0, half, z * 32 : z * 32 + 32, :].astype(BF16)
            sx[at : at + 32, last_lanes] = rim[1, half, z * 32 : z * 32 + 32, :].astype(BF16)
    for a in range(2):
        lanes = slice(a * 256, a * 256 + 128)
        part = wide[:, lanes].reshape(16, 32, 128)
        edge = rim[2, a].reshape(16, 8, 128)
        sy[:, lanes] = jnp.concatenate([part[:, 8:], edge], axis=1).reshape(512, 128).astype(BF16)
        lanes = slice(a * 256 + 128, a * 256 + 256)
        part = wide[:, lanes].reshape(16, 32, 128)
        edge = rim[3, a].reshape(16, 8, 128)
        sy[:, lanes] = jnp.concatenate([edge, part[:, :24]], axis=1).reshape(512, 128).astype(BF16)
        above, below = rim[4, a], rim[5, a]
        for e in range(2):
            lanes = slice((a * 2 + e) * 128, (a * 2 + e) * 128 + 128)
            part = wide[:, lanes]
            edge_up = above if e == 0 else pltpu.roll(above, 64, 1)
            edge_down = pltpu.roll(below, 64, 1) if e == 0 else below
            up = jnp.concatenate([part[128:], edge_up], axis=0)
            down = jnp.concatenate([edge_down, part[:384]], axis=0)
            sz[:, lanes] = jnp.where(low, up, down).astype(BF16)
    for a in range(2):
        lanes = slice(a * 256, a * 256 + 256)
        other = slice(256 - a * 256, 512 - a * 256)
        pre = (
            base[:, lanes]
            + dot(sx[:, other], mx[1 - a])
            + dot(sy[:, lanes], my[...])
            + dot(sz[:, lanes], mz[...])
        )
        s = sigmoid(pre)
        hidden[:, lanes] = (pre * s).astype(BF16)
        slope[:, lanes] = s * (1.0 + pre * (1.0 - s))
    pre = dot(hidden[...], w_down[...])
    s = sigmoid(pre)
    value = (pre * s).astype(BF16)
    mean = jnp.sum(value.astype(F32), axis=0, keepdims=True) * (1.0 / 512.0)
    mean = mean.astype(BF16).astype(F32)
    for k in range(2):
        node[k : k + 1, :] = mean[:, k * 128 : k * 128 + 128]
    for k in range(4):
        node[2 + k : 3 + k, :] = total[:, k * 128 : k * 128 + 128]
    sending = send_all(over_grp, sems_c, lambda k, peer: node, lambda k, peer: first.at[gi])
    pooled[...] = value
    pool_slope[...] = s * (1.0 + pre * (1.0 - s))
    first[gi] = node[...]
    part = dot_tn(value, g[...])
    for c in range(2):
        for i in range(na):
            for k in range(2):
                up_parts[c, i, k * up_rows : (k + 1) * up_rows, :] = part[
                    i * up_rows : (i + 1) * up_rows, c * 256 + k * 128 : c * 256 + (k + 1) * 128
                ].astype(BF16)
    up_sent = to_twin(up_parts, up_core, up_a)
    wait_all(sending)
    for i in range(groups):
        pack[6 * i : 6 * i + 6, :] = first[i]
    slab[si] = pack[...].astype(BF16)
    sending = send_all(over_sub, sems_d, lambda k, peer: slab.at[si], lambda k, peer: slab.at[si])
    wait_all(sending)
    up_sent = over_chips(up_parts, up_core, up_mid, up_in, up_sent, up_b)

    nodes = groups * subs
    me = gi * subs + si
    for s in range(subs):
        flat[s * groups * 6 : (s + 1) * groups * 6, :] = slab[s].astype(F32)
    pieces = [flat[pl.ds(k, nodes, stride=6), :] for k in range(6)]
    rows, cols = iota(nodes, nodes, 0), iota(nodes, nodes, 1)
    order = one_hot(lax.rem(rows, subs) * groups + rows // subs == cols)
    gathered = dot(order, jnp.concatenate(pieces, axis=1).astype(BF16)).astype(BF16)
    node_mean, grad_sum = gathered[:, :256], gathered[:, 256:]
    node_grad = dot_nt(grad_sum, w_up[...]).astype(BF16)
    wait_all(loads[4:])
    coarse_in = dot(node_mean, w_lift[...]).astype(BF16)
    picks = [one_hot(nbrs[d : d + 1, :] == rows) for d in range(6)]
    taps[:, 0:512] = coarse_in
    for d in range(6):
        taps[:, (d + 1) * 512 : (d + 2) * 512] = dot_tn(picks[d], coarse_in).astype(BF16)
    coarse_pre = jnp.zeros((nodes, 512), F32)
    for t in range(7):
        coarse_pre = coarse_pre + dot(taps[:, t * 512 : (t + 1) * 512], w_coarse[t])
    s = sigmoid(coarse_pre)
    coarse_out = (coarse_pre * s).astype(BF16)
    coarse_slope = s * (1.0 + coarse_pre * (1.0 - s))
    coarse_dpre = (dot_nt(node_grad, w_back[...]) * coarse_slope).astype(BF16)
    in_grad = dot_nt(coarse_dpre, w_coarse[0])
    for d in range(6):
        moved = dot(picks[d], coarse_dpre).astype(BF16)
        in_grad = in_grad + dot_nt(moved, w_coarse[d + 1])
    in_grad = in_grad.astype(BF16)
    mine = one_hot(iota(16, nodes, 1) == me)
    mean_grad = dot_nt(dot(mine, in_grad).astype(BF16), w_lift[...])[0:1] * (1.0 / 512.0)


    pool_dpre = ((grad_merged[...] + mean_grad) * pool_slope[...]).astype(BF16)
    part = dot_tn(hidden[...], pool_dpre)
    for c in range(2):
        down_parts[c] = part[:, c * 128 : (c + 1) * 128].reshape(na, down_rows, 128).astype(BF16)
    down_sent = to_twin(down_parts, down_core, down_a)
    up_sent = across(up_mid, up_in, up_slots, up_sent, up_c)
    dpre[...] = ((g[...].astype(F32) + dot_nt(pool_dpre, w_down[...])) * slope[...]).astype(BF16)

    def block(value, i, j):
        return value[i * 128 : (i + 1) * 128, j * 128 : (j + 1) * 128]

    def fold(value):
        return value[:64] + pltpu.roll(value[64:], 64, 1)

    down_sent = over_chips(down_parts, down_core, down_mid, down_in, down_sent, down_b)
    centre = dot_tn(q[...], dpre[...])
    gx0 = dot_tn(sx[:, 0:256], dpre[:, 256:512])
    gx1 = dot_tn(sx[:, 256:512], dpre[:, 0:256])
    gy = [dot_tn(sy[:, a * 256 : a * 256 + 256], dpre[:, a * 256 : a * 256 + 256]) for a in range(2)]
    gz = [dot_tn(sz[:, a * 256 : a * 256 + 256], dpre[:, a * 256 : a * 256 + 256]) for a in range(2)]
    middle = sum(block(centre, i, i) for i in range(4))
    x_up = block(centre, 2, 0) + block(centre, 3, 1) + block(gx0, 0, 0) + block(gx0, 1, 1)
    x_down = block(centre, 0, 2) + block(centre, 1, 3) + block(gx1, 0, 0) + block(gx1, 1, 1)
    y_up = block(centre, 1, 0) + block(centre, 3, 2) + block(gy[0], 0, 1) + block(gy[1], 0, 1)
    y_down = block(centre, 0, 1) + block(centre, 2, 3) + block(gy[0], 1, 0) + block(gy[1], 1, 0)
    between = sum(block(value, i, i) for value in gz for i in range(2))
    z_up = middle[64:] + pltpu.roll(between[:64], 64, 1)
    z_down = pltpu.roll(middle[:64], 64, 1) + between[64:]
    tap_sums = [fold(middle), fold(x_up), fold(x_down), fold(y_up), fold(y_down), z_up, z_down]
    tap_sums.append(jnp.zeros((64, 128), F32))
    low = low_lanes(64)
    for pair in range(4):
        both = jnp.where(low, tap_sums[2 * pair], pltpu.roll(tap_sums[2 * pair + 1], 64, 1))
        each = fine_rows if fine_rows < 64 else 64
        for i in range(64 // each):
            row = pair * 64 + i * each
            half, at = row // 128, row % 128
            fine_parts[half, at // fine_rows, at % fine_rows : at % fine_rows + each, :] = both[
                i * each : (i + 1) * each
            ].astype(BF16)
    fine_sent = to_twin(fine_parts, fine_core, fine_a)

    x_back[:, 0:256] = dot_nt(dpre[:, 256:512], mx[0])
    x_back[:, 256:512] = dot_nt(dpre[:, 0:256], mx[1])
    for a in range(2):
        lanes = slice(a * 256, a * 256 + 256)
        y_back[:, lanes] = dot_nt(dpre[:, lanes], my[...])
        z_back[:, lanes] = dot_nt(dpre[:, lanes], mz[...])
    fine_sent = over_chips(fine_parts, fine_core, fine_mid, fine_in, fine_sent, fine_b)
    down_sent = across(down_mid, down_in, down_slots, down_sent, down_c)
    backs = (x_back, y_back, z_back)
    layers = [layer(backs[where[0]], *where) for where in BEYOND]
    by_brick(layers, rim, border)
    pick_slots(entry_at, border, send_2)
    slots_sent = send_near(near, sems_n, send_2, recv_2)
    fine_sent = across(fine_mid, fine_in, fine_slots, fine_sent, fine_c)
    up_sent = spread(up_slots, up_all, up_sent, up_d)
    down_sent = spread(down_slots, down_all, down_sent, down_d)
    table[:, 0:ENTRIES, :] = by_place(layers)
    for ref, value in (
        (out_mean, node_mean), (out_grad, node_grad), (out_coarse, coarse_out),
        (out_dpre, coarse_dpre), (out_in, in_grad),
        (out_back, dot(coarse_out, w_back[...]).astype(BF16)), (out_sum, grad_sum),
    ):
        ref[...] = value
    stores = copy_all(
        (
            (out_dpre, dpre_to), (out_mean, mean_to), (out_grad, grad_to),
            (out_coarse, coarse_to), (out_in, in_to), (out_back, back_to), (out_sum, sum_to),
        ),
        sems_out,
        0,
    )

    turned = dot_tn(coarse_in, one_hot(rows == cols)).astype(BF16)
    taps_out[0:512, :] = turned
    for d in range(6):
        taps_out[(d + 1) * 512 : (d + 2) * 512, :] = dot(turned, picks[d]).astype(BF16)
    stores += copy_all(((taps_out, taps_to),), sems_out, len(stores))
    back = dot(dot(mine, coarse_out).astype(BF16), w_back[...])[0:1]
    merged[...] = (pooled[...].astype(F32) + back).astype(BF16)
    inner[...] = g[...].astype(F32) + dot_nt(dpre[...], m0[...])
    fine_sent = spread(fine_slots, fine_all, fine_sent, fine_d)

    for z in range(4):
        at = z * 128
        inner[at + 32 : at + 128, 0:256] += x_back[at : at + 96, 0:256]
        inner[at : at + 96, 256:512] += x_back[at + 32 : at + 128, 256:512]
    for zu in range(16):
        at = zu * 32
        for a in range(2):
            low_half, high_half = slice(a * 256, a * 256 + 128), slice(a * 256 + 128, a * 256 + 256)
            inner[at + 8 : at + 32, low_half] += y_back[at : at + 24, low_half]
            inner[at : at + 24, high_half] += y_back[at + 8 : at + 32, high_half]
    low = low_lanes(384)
    for i in range(4):
        lanes = slice(i * 128, i * 128 + 128)
        inner[128:512, lanes] += jnp.where(low, z_back[0:384, lanes], 0.0)
        inner[0:384, lanes] += jnp.where(low, 0.0, z_back[128:512, lanes])
    back_perm = perm_from()
    out = q[...].astype(F32) + hidden[...].astype(F32) + dot(merged[...], w_up[...])
    fine_out[...] = natural_rows(out.astype(BF16), back_perm)
    stores += copy_all(((fine_out, fine_to),), sems_out, len(stores))

    up_sent = share(up_all, up_sent, up_e)
    down_sent = share(down_all, down_sent, down_e)
    wait_all(slots_sent)
    unpack_slots(recv_2, spread_out, table)
    for place in range(16):
        slot_wide[place] = dot(back_add[:, 0:SOURCES], table[place])
    for f in range(6):
        add_layer(inner, *FACES[f], slot_wide[:, f * 8 : f * 8 + 8, :].reshape(128, 256))
    feats_grad[...] = natural_rows(inner[...].astype(BF16), back_perm)
    fine_sent = share(fine_all, fine_sent, fine_e)
    wait_all(up_sent)
    wait_all(fine_sent)
    wait_all(down_sent)
    wait_all(stores)


def finish_kernel(
    groups, subs,
    fine_in, feats_in, up_in, down_in, fine_sum_in, taps_in, mean_in, grad_in, coarse_in, dpre_in, in_grad_in, back_in, sum_in,
    fine_to, feats_to, w_fine_to, w_down_to, w_lift_to, w_coarse_to, w_back_to, w_up_to,
    fine_out, feats_out, up_all, down_all, fine_all, taps, node_mean, node_grad, coarse_out, dpre, in_grad, back, grad_sum,
    w_fine_grad, w_down_grad, w_lift_grad, w_coarse_grad, w_back_grad, w_up_grad,
    sems_in, sems_out,
):
    first = copy_all(
        ((dpre_in, dpre),) + tuple((taps_in.at[pl.ds(t * 512, 512)], taps.at[pl.ds(t * 512, 512)]) for t in range(7)),
        sems_in,
        0,
    )
    rest = copy_all(
        (
            (back_in, back), (sum_in, grad_sum), (up_in, up_all), (down_in, down_all), (fine_sum_in, fine_all), (coarse_in, coarse_out),
            (grad_in, node_grad), (mean_in, node_mean), (in_grad_in, in_grad), (fine_in, fine_out), (feats_in, feats_out),
        ),
        sems_in,
        8,
    )
    stores = []

    def store(src, dst):
        stores.extend(copy_all(((src, dst),), sems_out, len(stores)))

    first[0].wait()
    for t in range(7):
        first[t + 1].wait()
        w_coarse_grad[t] = dot(taps[t * 512 : (t + 1) * 512, :], dpre[...])
        store(w_coarse_grad.at[t], w_coarse_to.at[t])
    na = groups
    up_rows = 256 // na
    wait_all(rest[0:3])
    w_up_grad[...] = dot_tn(back[...], grad_sum[...])
    for c in range(2):
        for i in range(na):
            for k in range(2):
                w_up_grad[i * up_rows : (i + 1) * up_rows, c * 256 + k * 128 : c * 256 + (k + 1) * 128] += up_all[
                    c, i, k * up_rows : (k + 1) * up_rows, :
                ].astype(F32)
    store(w_up_grad, w_up_to)
    rest[3].wait()
    for c in range(2):
        w_down_grad[:, c * 128 : (c + 1) * 128] = down_all[c].astype(F32).reshape(512, 128)
    store(w_down_grad, w_down_to)
    rest[4].wait()
    sums = fine_all[...].astype(F32).reshape(256, 128)
    for pair in range(4):
        both = sums[pair * 64 : (pair + 1) * 64]
        w_fine_grad[2 * pair] = both[:, 0:64]
        if pair < 3:
            w_fine_grad[2 * pair + 1] = pltpu.roll(both, 64, 1)[:, 0:64]
    store(w_fine_grad, w_fine_to)
    wait_all(rest[5:9])
    w_back_grad[...] = dot_tn(coarse_out[...], node_grad[...])
    store(w_back_grad, w_back_to)
    w_lift_grad[...] = dot_tn(node_mean[...], in_grad[...])
    store(w_lift_grad, w_lift_to)
    rest[9].wait()
    store(fine_out, fine_to)
    rest[10].wait()
    store(feats_out, feats_to)
    wait_all(stores)


def spec(space=pltpu.VMEM):
    return pl.BlockSpec(memory_space=space)


def shape(dims, dtype):
    return jax.ShapeDtypeStruct(dims, dtype)


def buf(dims, dtype=BF16):
    return pltpu.VMEM(dims, dtype)


def pairs(count):
    return pltpu.SemaphoreType.DMA((2, count))


def body(groups, subs, feats, neighbours, w_fine, w_down, w_lift, coarse_nbrs, w_coarse, w_back, w_up, grad_out):
    nodes = groups * subs
    vmem, anywhere = spec(), spec(pl.ANY)
    sq16, sq32 = buf((512, 512)), buf((512, 512), F32)
    natural = shape((64, 8, 512), BF16)
    na, nb = groups, subs // 2
    chunk, fine_chunk = (512 // na, 128), (128 // na, 128)
    sums = (
        shape((2, na) + chunk, BF16), shape((2, na) + chunk, BF16), shape((2, na) + fine_chunk, BF16),
    )
    coarse = (
        shape((7 * 512, nodes), BF16), shape((nodes, 256), BF16), shape((nodes, 256), BF16),
        shape((nodes, 512), BF16), shape((nodes, 512), BF16), shape((nodes, 512), BF16),
        shape((nodes, 256), BF16), shape((nodes, 512), BF16),
    )
    slots = buf((4, SLOTS, 16, 256))

    def reduction(part):
        return [
            buf((2, na) + part), buf((na,) + part), buf((na,) + part), buf((na - 1,) + part), buf((nb,) + part),
        ]

    reduction_sems = [pairs(1), pairs(na - 1), pairs(nb - 1), pairs(na - 1), pairs(na)]

    def like(x):
        return buf(x.shape, x.dtype)

    results = pl.pallas_call(
        functools.partial(block_kernel, groups, subs),
        out_shape=(natural, natural) + sums + coarse,
        in_specs=[anywhere, anywhere, vmem, vmem, anywhere, anywhere, vmem, anywhere, anywhere, anywhere],
        out_specs=(anywhere,) + (vmem,) * 4 + (anywhere,) * 8,
        scratch_shapes=[like(natural), like(natural)]
        + [buf((512, 256)), buf((256, 512)), buf((256, 512)), buf((7, 512, 512)), buf((512, 256))]
        + [like(natural)]
        + [like(x) for x in coarse]
        + [sq16] * 6
        + [sq32, buf((512, 256)), buf((512, 256), F32), buf((512, 256), F32)]
        + [buf((subs, groups * 6, 128)), buf((ENTRIES, 128))]
        + [sq32, buf((SOURCES + 1, 16, 256)), buf((ENTRIES, 16, 256))]
        + [buf((16, SOURCES, 256)), buf((16, ENTRIES, 256), F32), buf((2, 512, 128), F32), buf((6, 2, 128, 128), F32)]
        + [buf((4, 8, 128), I32), buf((4, 8, 128), I32), buf((ENTRIES, 128), I32), buf((32, 128), I32)]
        + [pltpu.SMEM((4, 8, 128), I32), pltpu.SMEM((ENTRIES, 128), I32), pltpu.SMEM((32, 128), I32)]
        + [slots, slots, slots]
        + [sq16, buf((2, 256, 256)), buf((256, 256)), buf((256, 256))]
        + [sq32, buf((6, 128), F32), buf((groups, 6, 128), F32), buf((groups * 6, 128), F32)]
        + [buf((nodes * 6, 128), F32), buf((nodes, 7 * 512)), sq32, buf((512, 256)), sq16, sq32, sq32, sq32]
        + reduction(chunk)
        + reduction(chunk)
        + reduction(fine_chunk)
        + [pltpu.SemaphoreType.DMA((7,)), pltpu.SemaphoreType.DMA((9,)), pltpu.SemaphoreType.DMA((3,))]
        + [pairs(4), pairs(4), pairs(groups - 1), pairs(subs - 1), pairs(4)]
        + reduction_sems * 3,
        compiler_params=pltpu.CompilerParams(collective_id=1, has_side_effects=True, vmem_limit_bytes=MEMORY),
        name="block",
    )(
        feats.reshape(64, 8, 512), grad_out.reshape(64, 8, 512), neighbours,
        w_fine, w_down, w_up, coarse_nbrs.T, w_lift, w_coarse, w_back,
    )

    grads = (
        shape((7, 64, 64), F32), shape((512, 256), F32), shape((256, 512), F32),
        shape((7, 512, 512), F32), shape((512, 256), F32), shape((256, 512), F32),
    )
    outs = pl.pallas_call(
        functools.partial(finish_kernel, groups, subs),
        out_shape=(natural, natural) + grads,
        in_specs=[anywhere] * 13,
        out_specs=(anywhere,) * 8,
        scratch_shapes=[like(natural), like(natural)]
        + [like(x) for x in sums + coarse + grads]
        + [pltpu.SemaphoreType.DMA((19,)), pltpu.SemaphoreType.DMA((14,))],
        compiler_params=pltpu.CompilerParams(vmem_limit_bytes=MEMORY),
        name="finish",
    )(*results)
    return (outs[0].reshape(8, 8, 8, 512), outs[1].reshape(8, 8, 8, 512)) + tuple(outs[2:])


def solution(mesh):
    groups, subs = mesh.shape["grp"], mesh.shape["sub"]
    split4 = P(("grp", "sub"), None, None, None)
    return jax.shard_map(
        functools.partial(body, groups, subs),
        mesh=mesh,
        in_specs=(split4, P(("grp", "sub"), None)) + (P(),) * 7 + (split4,),
        out_specs=(split4, split4) + (P(),) * 6,
        check_vma=False,
    )
```

```python
import functools

import jax
import jax.numpy as jnp
from jax import lax
from jax.experimental import pallas as pl
from jax.experimental.pallas import tpu as pltpu
from jax.sharding import PartitionSpec as P

F32 = jnp.float32
BF16 = jnp.bfloat16
I32 = jnp.int32
MESH = pl.DeviceIdType.MESH
OFFSETS = (-2, -1, 1, 2)
MEMORY = 58 << 20
ENTRIES = 48
SOURCES = ENTRIES + 32
SLOTS = 6


def dot(x, y):
    return jnp.dot(x, y, preferred_element_type=F32)


def dot_nt(x, y):
    return lax.dot_general(x, y, (((1,), (1,)), ((), ())), preferred_element_type=F32)


def dot_tn(x, y):
    return lax.dot_general(x, y, (((0,), (0,)), ((), ())), preferred_element_type=F32)


def sigmoid(v):
    return 1.0 / (1.0 + jnp.exp(-v))


def perm_index(y):
    a, e = (y >> 8) & 1, (y >> 7) & 1
    u, w, b = (y >> 5) & 3, (y >> 3) & 3, y & 7
    return b * 64 + (2 * u + a) * 8 + 2 * w + e


def perm_to():
    rows = lax.broadcasted_iota(jnp.int32, (512, 512), 0)
    cols = lax.broadcasted_iota(jnp.int32, (512, 512), 1)
    return (perm_index(rows) == cols).astype(F32).astype(BF16)


def perm_from():
    rows = lax.broadcasted_iota(jnp.int32, (512, 512), 0)
    cols = lax.broadcasted_iota(jnp.int32, (512, 512), 1)
    return (perm_index(cols) == rows).astype(F32).astype(BF16)


def load_natural(ref):
    return ref[...].astype(F32).reshape(512, 512).astype(BF16)


def pooled_rows(x, perm, out_ref, wide_ref=None):
    y = dot(perm, x)
    for z in range(4):
        for ae in range(4):
            block = y[ae * 128 : (ae + 1) * 128, z * 128 : (z + 1) * 128]
            where = (pl.ds(z * 128, 128), pl.ds(ae * 128, 128))
            out_ref[where] = block.astype(BF16)
            if wide_ref is not None:
                wide_ref[where] = block


def natural_rows(q, perm_back):
    y = jnp.concatenate(
        [
            jnp.concatenate(
                [q[z * 128 : (z + 1) * 128, ae * 128 : (ae + 1) * 128] for z in range(4)], axis=1
            )
            for ae in range(4)
        ],
        axis=0,
    )
    return dot(perm_back, y).reshape(64, 8, 512).astype(BF16)


def low_lanes(rows):
    return lax.broadcasted_iota(jnp.int32, (rows, 128), 1) < 64


def layer(ref, axis, place, parity):
    if axis == 0:
        return jnp.concatenate(
            [
                ref[z * 128 + place * 32 : z * 128 + place * 32 + 32, parity * 256 : parity * 256 + 256]
                for z in range(4)
            ],
            axis=0,
        )
    if axis == 1:
        parts = []
        for a in range(2):
            lane = (a * 2 + parity) * 128
            parts.append(
                jnp.concatenate(
                    [ref[zu * 32 + place * 8 : zu * 32 + place * 8 + 8, lane : lane + 128] for zu in range(16)],
                    axis=0,
                )
            )
        return jnp.concatenate(parts, axis=1)
    parts = []
    for a in range(2):
        first = ref[place * 128 : place * 128 + 128, a * 256 : a * 256 + 128]
        second = ref[place * 128 : place * 128 + 128, a * 256 + 128 : a * 256 + 256]
        if parity == 0:
            second = pltpu.roll(second, 64, 1)
        else:
            first = pltpu.roll(first, 64, 1)
        parts.append(jnp.where(low_lanes(128), first, second))
    return jnp.concatenate(parts, axis=1)


def add_layer(ref, axis, place, parity, value):
    if axis == 0:
        for z in range(4):
            rows = pl.ds(z * 128 + place * 32, 32)
            ref[rows, parity * 256 : parity * 256 + 256] += value[z * 32 : z * 32 + 32]
    elif axis == 1:
        for a in range(2):
            lane = (a * 2 + parity) * 128
            for zu in range(16):
                rows = pl.ds(zu * 32 + place * 8, 8)
                ref[rows, lane : lane + 128] += value[zu * 8 : zu * 8 + 8, a * 128 : a * 128 + 128]
    else:
        low = low_lanes(128)
        rows = pl.ds(place * 128, 128)
        for a in range(2):
            part = value[:, a * 128 : a * 128 + 128]
            turned = pltpu.roll(part, 64, 1)
            first, second = (part, turned) if parity == 0 else (turned, part)
            keep = low if parity == 0 else ~low
            ref[rows, a * 256 : a * 256 + 128] += jnp.where(keep, first, 0.0)
            ref[rows, a * 256 + 128 : a * 256 + 256] += jnp.where(keep, second, 0.0)


FACES = ((0, 3, 1), (0, 0, 0), (1, 3, 1), (1, 0, 0), (2, 3, 1), (2, 0, 0))
BEYOND = ((0, 3, 0), (0, 0, 1), (1, 3, 0), (1, 0, 1), (2, 3, 0), (2, 0, 1))


def one_hot(mask):
    return mask.astype(F32).astype(BF16)


def iota(rows, cols, axis):
    return lax.broadcasted_iota(jnp.int32, (rows, cols), axis)


def entries(neighbours, me):
    nb = neighbours[...]
    n = jnp.concatenate([jnp.broadcast_to(nb[:, d : d + 1], (8, 128)) for d in range(6)], axis=0)
    lane = iota(ENTRIES, 128, 1)
    direction = iota(ENTRIES, 128, 0) >> 3
    offset = (n >> 3) - me
    number = (direction ^ 1) * 8 + (n & 7)
    local = (n >= 0) & (offset == 0)
    peer = lane >> 3
    peer_offset = jnp.where(peer < 2, peer - 2, peer - 1)
    far = (n >= 0) & (lane < 32) & (offset == peer_offset)
    before = one_hot(iota(ENTRIES, ENTRIES, 1) < iota(ENTRIES, ENTRIES, 0))
    count = dot(before, one_hot(far))
    slot = far & (count == (lane & 7).astype(F32))
    place = jnp.sum(jnp.where(slot, lane + 1, 0), axis=1, keepdims=True)
    source = jnp.where(local, number, jnp.where(place > 0, ENTRIES - 1 + place, SOURCES))
    return one_hot(local & (lane == number)), one_hot(slot), number, source


def rolled(x, by):
    return pltpu.roll(x.astype(F32), by, 1).astype(BF16)


def coords(groups, subs, offset):
    nodes = groups * subs
    at = lax.axis_index("grp") * subs + lax.axis_index("sub")
    to = lax.rem(at + offset + nodes, nodes)
    return (to // subs, lax.rem(to, subs))


def ring(a, b, size):
    return min((a - b) % size, (b - a) % size)


def peers_of(groups, subs):
    g, s = lax.axis_index("grp"), lax.axis_index("sub")
    near = [coords(groups, subs, off) for off in OFFSETS]
    y, core = g // 2, lax.rem(g, 2)
    steps = [(dy, dc) for dy in range(groups // 2) for dc in range(2) if dy or dc]
    steps.sort(key=lambda d: -4 * ring(d[0], 0, groups // 2) - d[1])
    over_grp = [(lax.rem(y + dy, groups // 2) * 2 + lax.rem(core + dc, 2), s) for dy, dc in steps]
    wide = min(4, subs)
    deep = subs // wide
    z, x = s // wide, lax.rem(s, wide)
    steps = [(dz, dx) for dz in range(deep) for dx in range(wide) if dz or dx]
    steps.sort(key=lambda d: -ring(d[0], 0, deep) - ring(d[1], 0, wide))
    over_sub = [(g, lax.rem(z + dz, deep) * wide + lax.rem(x + dx, wide)) for dz, dx in steps]
    return near, over_grp, over_sub


def squares(groups, subs):
    g, s = lax.axis_index("grp"), lax.axis_index("sub")
    ys, deep = groups // 2, subs // 4
    y, core = g // 2, lax.rem(g, 2)
    z, x = s // 4, lax.rem(s, 4)
    low, high = (x ^ (x >> 1)) & 1, x >> 1
    steps = [(d, f) for d in range(ys) for f in range(2) if d or f]
    steps.sort(key=lambda d: -ring(d[0], 0, ys) - d[1])
    first = [(lax.rem(y + d, ys) * 2 + core, z * 4 + (x ^ f)) for d, f in steps]
    first_rank = [lax.rem(y + d, ys) * 2 + (low ^ f) for d, f in steps]
    heard_rank = [lax.rem(y + ys - d, ys) * 2 + (low ^ f) for d, f in steps]
    steps = [(d, f) for d in range(deep) for f in range(2) if d or f]
    steps.sort(key=lambda d: -ring(d[0], 0, deep) - d[1])
    second = [(g, lax.rem(z + d, deep) * 4 + (x ^ (3 * f))) for d, f in steps]
    return first, first_rank, heard_rank, y * 2 + low, second, z * 2 + high


def greet(peers):
    barrier = pltpu.get_barrier_semaphore()
    for peer in peers:
        pl.semaphore_signal(barrier, inc=1, device_id=peer, device_id_type=MESH)
    return lambda: pl.semaphore_wait(barrier, len(peers))


def send_all(peers, sems, src_of, dst_of):
    copies = []
    for k, peer in enumerate(peers):
        copy = pltpu.make_async_remote_copy(
            src_ref=src_of(k, peer),
            dst_ref=dst_of(k, peer),
            send_sem=sems.at[0, k],
            recv_sem=sems.at[1, k],
            device_id=peer,
            device_id_type=MESH,
        )
        copy.start()
        copies.append(copy)
    return copies


def send_near(near, sems, src, dst):
    copies = []
    for p in (0, 3, 1, 2):
        copy = pltpu.make_async_remote_copy(
            src_ref=src.at[p],
            dst_ref=dst.at[3 - p],
            send_sem=sems.at[0, p],
            recv_sem=sems.at[1, 3 - p],
            device_id=near[p],
            device_id_type=MESH,
        )
        copy.start()
        copies.append(copy)
    return copies


def copy_all(pairs, sems, first):
    copies = []
    for k, (src, dst) in enumerate(pairs):
        copy = pltpu.make_async_copy(src, dst, sems.at[first + k])
        copy.start()
        copies.append(copy)
    return copies


def wait_all(copies):
    for copy in copies:
        copy.wait()


def by_place(layers):
    return jnp.concatenate([x.reshape(16, 8, 256) for x in layers], axis=1).astype(BF16)


def by_brick(layers, stage, out):
    for which, value in enumerate(layers):
        for half in range(2):
            lanes = slice(half * 128, half * 128 + 128)
            stage[which, half] = value[:, lanes]
            for b in range(8):
                out[which * 8 + b, :, lanes] = stage[which, half, pl.ds(b, 16, stride=8), :].astype(BF16)


def pick_slots(numbers, faces, out):
    for p in range(4):
        for i in range(SLOTS):
            row = jnp.clip(numbers[p * 8 + i, 0] - 1, 0, ENTRIES - 1)
            out[p, i] = faces[row]


def unpack_slots(slots, spread, table):
    for p in range(4):
        for i in range(SLOTS):
            face = slots[p, i].astype(F32)
            for half in range(2):
                spread[half, pl.ds(p * 8 + i, 16, stride=32), :] = face[:, half * 128 : half * 128 + 128]
    for half in range(2):
        table[:, ENTRIES:SOURCES, half * 128 : half * 128 + 128] = (
            spread[half].reshape(16, 32, 128).astype(BF16)
        )


def build_mats(w_fine, m0, mx, my, mz):
    zero = jnp.zeros((128, 128), BF16)
    none = jnp.zeros((64, 64), BF16)

    def put(ref, i, j, value):
        ref[i * 128 : (i + 1) * 128, j * 128 : (j + 1) * 128] = value

    def quad(a, b, c, d):
        return jnp.concatenate(
            [jnp.concatenate([a, b], axis=1), jnp.concatenate([c, d], axis=1)], axis=0
        )

    w = [w_fine[t] for t in range(7)]
    c = quad(w[0], w[6], w[5], w[0])
    d1, d2, d3, d4 = (quad(w[t], none, none, w[t]) for t in range(1, 5))
    ez = quad(none, w[5], w[6], none)
    for a in range(2):
        for e in range(2):
            i = a * 2 + e
            put(m0, i, i, c)
            put(m0, i, (1 - a) * 2 + e, d1 if a == 1 else d2)
            put(m0, i, a * 2 + (1 - e), d3 if e == 1 else d4)
            put(m0, i, 3 - i, zero)
    for i in range(2):
        for j in range(2):
            put(mx.at[0], i, j, d1 if i == j else zero)
            put(mx.at[1], i, j, d2 if i == j else zero)
            put(mz, i, j, ez if i == j else zero)
    put(my, 0, 0, zero)
    put(my, 1, 1, zero)
    put(my, 0, 1, d3)
    put(my, 1, 0, d4)


def block_kernel(
    groups, subs,
    feats_in, grad_in, neighbours, w_fine, w_down_in, w_up_in, nbrs, w_lift_in, w_coarse_in, w_back_in,
    fine_to, feats_to, up_to, down_to, fine_sum_to, taps_to, mean_to, grad_to, coarse_to, dpre_to, in_to, back_to, sum_to,
    feats, grad, w_down, w_up, w_lift, w_coarse, w_back,
    fine_out, feats_grad, up_all, down_all, fine_all, taps_out, out_mean, out_grad, out_coarse, out_dpre, out_in, out_back, out_sum,
    q, g, sx, sy, sz, hidden, slope, pooled, pool_slope, grad_merged, slab, back_add,
    wide, faces, border, table, slot_wide, spread_out, rim, asked, wanted, source_of, entry_of,
    asked_at, source_at, entry_at, send, send_2, recv_2, m0, mx, my, mz, base, node, first, pack,
    flat, taps, inner, merged, dpre, x_back, y_back, z_back,
    up_parts, up_core, up_mid, up_in, up_slots, down_parts, down_core, down_mid, down_in, down_slots,
    fine_parts, fine_core, fine_mid, fine_in, fine_slots,
    sems_in, sems_out, sems_s, sems_a, sems_b, sems_c, sems_d, sems_n,
    up_a, up_b, up_c, up_d, up_e, down_a, down_b, down_c, down_d, down_e, fine_a, fine_b, fine_c, fine_d, fine_e,
):
    gi, si = lax.axis_index("grp"), lax.axis_index("sub")
    near, over_grp, over_sub = peers_of(groups, subs)
    over_a, rank_a, heard, ai, over_b, bi = squares(groups, subs)
    na, nb = len(over_a) + 1, len(over_b) + 1
    ci = lax.rem(gi, 2)
    twin = [(gi + 1 - 2 * ci, si)]
    greeted = greet(near + over_grp + over_sub + over_a)
    up_rows, down_rows, fine_rows = 256 // na, 512 // na, 128 // na

    def add(own, incoming, copies):
        wait_all(copies)
        value = own.astype(F32)
        for k in range(len(copies)):
            value = value + incoming[k].astype(F32)
        return value.astype(BF16)

    def join(slots, copies, count):
        wait_all(copies)
        value = slots[0].astype(F32)
        for k in range(1, count):
            value = value + slots[k].astype(F32)
        return value.astype(BF16)

    def to_twin(parts, core_in, sems):
        return send_all(twin, sems, lambda k, peer: parts.at[1 - ci], lambda k, peer: core_in)

    def over_chips(parts, core_in, mid, incoming, copies, sems):
        wait_all(copies)
        mid[...] = (parts[ci].astype(F32) + core_in[...].astype(F32)).astype(BF16)
        return send_all(over_a, sems, lambda k, peer: mid.at[rank_a[k]], lambda k, peer: incoming.at[k])

    def across(mid, incoming, slots, copies, sems):
        slots[bi] = add(mid[ai], incoming, copies)
        return send_all(over_b, sems, lambda k, peer: slots.at[bi], lambda k, peer: slots.at[bi])

    def spread(slots, everything, copies, sems):
        everything[ci, ai] = join(slots, copies, nb)
        return send_all(
            over_a, sems, lambda k, peer: everything.at[ci, ai], lambda k, peer: everything.at[ci, ai]
        )

    def share(everything, copies, sems):
        sent = []
        for k in range(na):
            if k > 0:
                copies[k - 1].wait_recv()
            part = everything.at[ci, ai if k == 0 else heard[k - 1]]
            copy = pltpu.make_async_remote_copy(
                src_ref=part,
                dst_ref=part,
                send_sem=sems.at[0, k],
                recv_sem=sems.at[1, k],
                device_id=twin[0],
                device_id_type=MESH,
            )
            copy.start()
            sent.append(copy)
        for copy in copies:
            copy.wait_send()
        return sent

    loads = copy_all(
        ((feats_in, feats), (grad_in, grad), (w_up_in, w_up), (w_down_in, w_down)), sems_in, 0
    )
    local, slot, number, source = entries(neighbours, gi * subs + si)
    wanted[...] = dot_tn(slot, (number + 1).astype(F32).astype(BF16))[0:32].reshape(4, 8, 128).astype(jnp.int32)
    greeted()
    asking = send_near(near, sems_a, wanted, asked)
    entry = (iota(ENTRIES, 128, 0) + 1).astype(F32).astype(BF16)
    entry_of[...] = dot_tn(slot, entry)[0:32].astype(jnp.int32)
    source_of[...] = source
    numbers = copy_all(((source_of, source_at), (entry_of, entry_at)), sems_s, 0)
    loads += copy_all(
        ((w_lift_in, w_lift), (w_coarse_in, w_coarse), (w_back_in, w_back)), sems_in, len(loads)
    )

    perm = perm_to()
    loads[0].wait()
    pooled_rows(load_natural(feats), perm, q, wide)
    by_brick([layer(wide, *where) for where in FACES], rim, border)
    faces[SOURCES] = jnp.zeros((16, 256), BF16)
    wait_all(asking)
    asked_copy = copy_all(((asked, asked_at),), sems_s, 2)
    eye = one_hot(iota(ENTRIES, 128, 0) == iota(ENTRIES, 128, 1))
    given = one_hot(asked[...].reshape(32, 128) - 1 == iota(32, 128, 1))
    wait_all(asked_copy)
    for p in range(4):
        for i in range(SLOTS):
            row = jnp.clip(asked_at[p, i, 0] - 1, 0, ENTRIES - 1)
            send[p, i] = border[row]
    sending = []
    for p in (0, 3, 1, 2):
        copy = pltpu.make_async_remote_copy(
            src_ref=send.at[p],
            dst_ref=faces.at[pl.ds(ENTRIES + (3 - p) * 8, SLOTS)],
            send_sem=sems_b.at[0, p],
            recv_sem=sems_b.at[1, 3 - p],
            device_id=near[p],
            device_id_type=MESH,
        )
        copy.start()
        sending.append(copy)

    local_back = dot_tn(local, eye)[0:ENTRIES].astype(BF16)
    given_back = dot_tn(given, eye[0:32])[0:ENTRIES].astype(BF16)
    back_add[...] = local_back + rolled(given_back, ENTRIES)
    spread_out[...] = jnp.zeros_like(spread_out)
    faces[0:ENTRIES] = border[...]
    loads[1].wait()
    pooled_rows(load_natural(grad), perm, g)
    build_mats(w_fine, m0, mx, my, mz)
    base[...] = dot(q[...], m0[...])
    loads[2].wait()
    merged_grad = dot_nt(g[...], w_up[...])
    grad_merged[...] = merged_grad
    total = jnp.sum(g[...].astype(F32), axis=0, keepdims=True).astype(BF16).astype(F32)
    low = low_lanes(512)
    for z in range(4):
        at = z * 128
        sx[at : at + 96, 0:256] = q[at + 32 : at + 128, 0:256]
        sx[at + 32 : at + 128, 256:512] = q[at : at + 96, 256:512]
    wait_all(numbers)
    loads[3].wait()

    wait_all(sending)
    for d in range(6):
        for b in range(8):
            row = jnp.clip(source_at[d * 8 + b, 0], 0, SOURCES)
            face = faces[row].astype(F32)
            for half in range(2):
                rim[d, half, pl.ds(b, 16, stride=8), :] = face[:, half * 128 : half * 128 + 128]
    for z in range(4):
        at = z * 128
        for half in range(2):
            first_lanes, last_lanes = slice(half * 128, half * 128 + 128), slice(half * 128 + 256, half * 128 + 384)
            sx[at + 96 : at + 128, first_lanes] = rim[0, half, z * 32 : z * 32 + 32, :].astype(BF16)
            sx[at : at + 32, last_lanes] = rim[1, half, z * 32 : z * 32 + 32, :].astype(BF16)
    for a in range(2):
        lanes = slice(a * 256, a * 256 + 128)
        part = wide[:, lanes].reshape(16, 32, 128)
        edge = rim[2, a].reshape(16, 8, 128)
        sy[:, lanes] = jnp.concatenate([part[:, 8:], edge], axis=1).reshape(512, 128).astype(BF16)
        lanes = slice(a * 256 + 128, a * 256 + 256)
        part = wide[:, lanes].reshape(16, 32, 128)
        edge = rim[3, a].reshape(16, 8, 128)
        sy[:, lanes] = jnp.concatenate([edge, part[:, :24]], axis=1).reshape(512, 128).astype(BF16)
        above, below = rim[4, a], rim[5, a]
        for e in range(2):
            lanes = slice((a * 2 + e) * 128, (a * 2 + e) * 128 + 128)
            part = wide[:, lanes]
            edge_up = above if e == 0 else pltpu.roll(above, 64, 1)
            edge_down = pltpu.roll(below, 64, 1) if e == 0 else below
            up = jnp.concatenate([part[128:], edge_up], axis=0)
            down = jnp.concatenate([edge_down, part[:384]], axis=0)
            sz[:, lanes] = jnp.where(low, up, down).astype(BF16)
    for a in range(2):
        lanes = slice(a * 256, a * 256 + 256)
        other = slice(256 - a * 256, 512 - a * 256)
        pre = (
            base[:, lanes]
            + dot(sx[:, other], mx[1 - a])
            + dot(sy[:, lanes], my[...])
            + dot(sz[:, lanes], mz[...])
        )
        s = sigmoid(pre)
        hidden[:, lanes] = (pre * s).astype(BF16)
        slope[:, lanes] = s * (1.0 + pre * (1.0 - s))
    pre = dot(hidden[...], w_down[...])
    s = sigmoid(pre)
    value = (pre * s).astype(BF16)
    mean = jnp.sum(value.astype(F32), axis=0, keepdims=True) * (1.0 / 512.0)
    mean = mean.astype(BF16).astype(F32)
    for k in range(2):
        node[k : k + 1, :] = mean[:, k * 128 : k * 128 + 128]
    for k in range(4):
        node[2 + k : 3 + k, :] = total[:, k * 128 : k * 128 + 128]
    sending = send_all(over_grp, sems_c, lambda k, peer: node, lambda k, peer: first.at[gi])
    pooled[...] = value
    pool_slope[...] = s * (1.0 + pre * (1.0 - s))
    first[gi] = node[...]
    part = dot_tn(value, g[...])
    for c in range(2):
        for i in range(na):
            for k in range(2):
                up_parts[c, i, k * up_rows : (k + 1) * up_rows, :] = part[
                    i * up_rows : (i + 1) * up_rows, c * 256 + k * 128 : c * 256 + (k + 1) * 128
                ].astype(BF16)
    up_sent = to_twin(up_parts, up_core, up_a)
    wait_all(sending)
    for i in range(groups):
        pack[6 * i : 6 * i + 6, :] = first[i]
    slab[si] = pack[...].astype(BF16)
    sending = send_all(over_sub, sems_d, lambda k, peer: slab.at[si], lambda k, peer: slab.at[si])
    wait_all(sending)
    up_sent = over_chips(up_parts, up_core, up_mid, up_in, up_sent, up_b)

    nodes = groups * subs
    me = gi * subs + si
    for s in range(subs):
        flat[s * groups * 6 : (s + 1) * groups * 6, :] = slab[s].astype(F32)
    pieces = [flat[pl.ds(k, nodes, stride=6), :] for k in range(6)]
    rows, cols = iota(nodes, nodes, 0), iota(nodes, nodes, 1)
    order = one_hot(lax.rem(rows, subs) * groups + rows // subs == cols)
    gathered = dot(order, jnp.concatenate(pieces, axis=1).astype(BF16)).astype(BF16)
    node_mean, grad_sum = gathered[:, :256], gathered[:, 256:]
    node_grad = dot_nt(grad_sum, w_up[...]).astype(BF16)
    wait_all(loads[4:])
    coarse_in = dot(node_mean, w_lift[...]).astype(BF16)
    picks = [one_hot(nbrs[d : d + 1, :] == rows) for d in range(6)]
    taps[:, 0:512] = coarse_in
    for d in range(6):
        taps[:, (d + 1) * 512 : (d + 2) * 512] = dot_tn(picks[d], coarse_in).astype(BF16)
    coarse_pre = jnp.zeros((nodes, 512), F32)
    for t in range(7):
        coarse_pre = coarse_pre + dot(taps[:, t * 512 : (t + 1) * 512], w_coarse[t])
    s = sigmoid(coarse_pre)
    coarse_out = (coarse_pre * s).astype(BF16)
    coarse_slope = s * (1.0 + coarse_pre * (1.0 - s))
    coarse_dpre = (dot_nt(node_grad, w_back[...]) * coarse_slope).astype(BF16)
    in_grad = dot_nt(coarse_dpre, w_coarse[0])
    for d in range(6):
        moved = dot(picks[d], coarse_dpre).astype(BF16)
        in_grad = in_grad + dot_nt(moved, w_coarse[d + 1])
    in_grad = in_grad.astype(BF16)
    mine = one_hot(iota(16, nodes, 1) == me)
    mean_grad = dot_nt(dot(mine, in_grad).astype(BF16), w_lift[...])[0:1] * (1.0 / 512.0)


    pool_dpre = ((grad_merged[...] + mean_grad) * pool_slope[...]).astype(BF16)
    part = dot_tn(hidden[...], pool_dpre)
    for c in range(2):
        down_parts[c] = part[:, c * 128 : (c + 1) * 128].reshape(na, down_rows, 128).astype(BF16)
    down_sent = to_twin(down_parts, down_core, down_a)
    up_sent = across(up_mid, up_in, up_slots, up_sent, up_c)
    dpre[...] = ((g[...].astype(F32) + dot_nt(pool_dpre, w_down[...])) * slope[...]).astype(BF16)

    def block(value, i, j):
        return value[i * 128 : (i + 1) * 128, j * 128 : (j + 1) * 128]

    def fold(value):
        return value[:64] + pltpu.roll(value[64:], 64, 1)

    down_sent = over_chips(down_parts, down_core, down_mid, down_in, down_sent, down_b)
    centre = dot_tn(q[...], dpre[...])
    gx0 = dot_tn(sx[:, 0:256], dpre[:, 256:512])
    gx1 = dot_tn(sx[:, 256:512], dpre[:, 0:256])
    gy = [dot_tn(sy[:, a * 256 : a * 256 + 256], dpre[:, a * 256 : a * 256 + 256]) for a in range(2)]
    gz = [dot_tn(sz[:, a * 256 : a * 256 + 256], dpre[:, a * 256 : a * 256 + 256]) for a in range(2)]
    middle = sum(block(centre, i, i) for i in range(4))
    x_up = block(centre, 2, 0) + block(centre, 3, 1) + block(gx0, 0, 0) + block(gx0, 1, 1)
    x_down = block(centre, 0, 2) + block(centre, 1, 3) + block(gx1, 0, 0) + block(gx1, 1, 1)
    y_up = block(centre, 1, 0) + block(centre, 3, 2) + block(gy[0], 0, 1) + block(gy[1], 0, 1)
    y_down = block(centre, 0, 1) + block(centre, 2, 3) + block(gy[0], 1, 0) + block(gy[1], 1, 0)
    between = sum(block(value, i, i) for value in gz for i in range(2))
    z_up = middle[64:] + pltpu.roll(between[:64], 64, 1)
    z_down = pltpu.roll(middle[:64], 64, 1) + between[64:]
    tap_sums = [fold(middle), fold(x_up), fold(x_down), fold(y_up), fold(y_down), z_up, z_down]
    tap_sums.append(jnp.zeros((64, 128), F32))
    low = low_lanes(64)
    for pair in range(4):
        both = jnp.where(low, tap_sums[2 * pair], pltpu.roll(tap_sums[2 * pair + 1], 64, 1))
        each = fine_rows if fine_rows < 64 else 64
        for i in range(64 // each):
            row = pair * 64 + i * each
            half, at = row // 128, row % 128
            fine_parts[half, at // fine_rows, at % fine_rows : at % fine_rows + each, :] = both[
                i * each : (i + 1) * each
            ].astype(BF16)
    fine_sent = to_twin(fine_parts, fine_core, fine_a)

    x_back[:, 0:256] = dot_nt(dpre[:, 256:512], mx[0])
    x_back[:, 256:512] = dot_nt(dpre[:, 0:256], mx[1])
    for a in range(2):
        lanes = slice(a * 256, a * 256 + 256)
        y_back[:, lanes] = dot_nt(dpre[:, lanes], my[...])
        z_back[:, lanes] = dot_nt(dpre[:, lanes], mz[...])
    fine_sent = over_chips(fine_parts, fine_core, fine_mid, fine_in, fine_sent, fine_b)
    down_sent = across(down_mid, down_in, down_slots, down_sent, down_c)
    backs = (x_back, y_back, z_back)
    layers = [layer(backs[where[0]], *where) for where in BEYOND]
    by_brick(layers, rim, border)
    pick_slots(entry_at, border, send_2)
    slots_sent = send_near(near, sems_n, send_2, recv_2)
    fine_sent = across(fine_mid, fine_in, fine_slots, fine_sent, fine_c)
    up_sent = spread(up_slots, up_all, up_sent, up_d)
    down_sent = spread(down_slots, down_all, down_sent, down_d)
    table[:, 0:ENTRIES, :] = by_place(layers)
    for ref, value in (
        (out_mean, node_mean), (out_grad, node_grad), (out_coarse, coarse_out),
        (out_dpre, coarse_dpre), (out_in, in_grad),
        (out_back, dot(coarse_out, w_back[...]).astype(BF16)), (out_sum, grad_sum),
    ):
        ref[...] = value
    stores = copy_all(
        (
            (out_dpre, dpre_to), (out_mean, mean_to), (out_grad, grad_to),
            (out_coarse, coarse_to), (out_in, in_to), (out_back, back_to), (out_sum, sum_to),
        ),
        sems_out,
        0,
    )

    turned = dot_tn(coarse_in, one_hot(rows == cols)).astype(BF16)
    taps_out[0:512, :] = turned
    for d in range(6):
        taps_out[(d + 1) * 512 : (d + 2) * 512, :] = dot(turned, picks[d]).astype(BF16)
    stores += copy_all(((taps_out, taps_to),), sems_out, len(stores))
    back = dot(dot(mine, coarse_out).astype(BF16), w_back[...])[0:1]
    merged[...] = (pooled[...].astype(F32) + back).astype(BF16)
    inner[...] = g[...].astype(F32) + dot_nt(dpre[...], m0[...])
    fine_sent = spread(fine_slots, fine_all, fine_sent, fine_d)

    for z in range(4):
        at = z * 128
        inner[at + 32 : at + 128, 0:256] += x_back[at : at + 96, 0:256]
        inner[at : at + 96, 256:512] += x_back[at + 32 : at + 128, 256:512]
    for zu in range(16):
        at = zu * 32
        for a in range(2):
            low_half, high_half = slice(a * 256, a * 256 + 128), slice(a * 256 + 128, a * 256 + 256)
            inner[at + 8 : at + 32, low_half] += y_back[at : at + 24, low_half]
            inner[at : at + 24, high_half] += y_back[at + 8 : at + 32, high_half]
    low = low_lanes(384)
    for i in range(4):
        lanes = slice(i * 128, i * 128 + 128)
        inner[128:512, lanes] += jnp.where(low, z_back[0:384, lanes], 0.0)
        inner[0:384, lanes] += jnp.where(low, 0.0, z_back[128:512, lanes])
    back_perm = perm_from()
    out = q[...].astype(F32) + hidden[...].astype(F32) + dot(merged[...], w_up[...])
    fine_out[...] = natural_rows(out.astype(BF16), back_perm)
    stores += copy_all(((fine_out, fine_to),), sems_out, len(stores))

    up_sent = share(up_all, up_sent, up_e)
    down_sent = share(down_all, down_sent, down_e)
    wait_all(slots_sent)
    unpack_slots(recv_2, spread_out, table)
    for place in range(16):
        slot_wide[place] = dot(back_add[:, 0:SOURCES], table[place])
    for f in range(6):
        add_layer(inner, *FACES[f], slot_wide[:, f * 8 : f * 8 + 8, :].reshape(128, 256))
    feats_grad[...] = natural_rows(inner[...].astype(BF16), back_perm)
    stores += copy_all(((feats_grad, feats_to),), sems_out, len(stores))
    fine_sent = share(fine_all, fine_sent, fine_e)
    for copies, src, dst in (
        (up_sent, up_all, up_to), (down_sent, down_all, down_to), (fine_sent, fine_all, fine_sum_to),
    ):
        wait_all(copies)
        stores += copy_all(((src, dst),), sems_out, len(stores))
    wait_all(stores)


def finish_kernel(
    groups, subs,
    fine_in, feats_in, up_in, down_in, fine_sum_in, taps_in, mean_in, grad_in, coarse_in, dpre_in, in_grad_in, back_in, sum_in,
    fine_to, feats_to, w_fine_to, w_down_to, w_lift_to, w_coarse_to, w_back_to, w_up_to,
    fine_out, feats_out, up_all, down_all, fine_all, taps, node_mean, node_grad, coarse_out, dpre, in_grad, back, grad_sum,
    w_fine_grad, w_down_grad, w_lift_grad, w_coarse_grad, w_back_grad, w_up_grad,
    sems_in, sems_out,
):
    first = copy_all(
        ((dpre_in, dpre),) + tuple((taps_in.at[pl.ds(t * 512, 512)], taps.at[pl.ds(t * 512, 512)]) for t in range(7)),
        sems_in,
        0,
    )
    rest = copy_all(
        (
            (back_in, back), (sum_in, grad_sum), (up_in, up_all), (down_in, down_all), (fine_sum_in, fine_all), (coarse_in, coarse_out),
            (grad_in, node_grad), (mean_in, node_mean), (in_grad_in, in_grad), (fine_in, fine_out), (feats_in, feats_out),
        ),
        sems_in,
        8,
    )
    stores = []

    def store(src, dst):
        stores.extend(copy_all(((src, dst),), sems_out, len(stores)))

    first[0].wait()
    for t in range(7):
        first[t + 1].wait()
        w_coarse_grad[t] = dot(taps[t * 512 : (t + 1) * 512, :], dpre[...])
        store(w_coarse_grad.at[t], w_coarse_to.at[t])
    na = groups
    up_rows = 256 // na
    wait_all(rest[0:3])
    w_up_grad[...] = dot_tn(back[...], grad_sum[...])
    for c in range(2):
        for i in range(na):
            for k in range(2):
                w_up_grad[i * up_rows : (i + 1) * up_rows, c * 256 + k * 128 : c * 256 + (k + 1) * 128] += up_all[
                    c, i, k * up_rows : (k + 1) * up_rows, :
                ].astype(F32)
    store(w_up_grad, w_up_to)
    rest[3].wait()
    for c in range(2):
        w_down_grad[:, c * 128 : (c + 1) * 128] = down_all[c].astype(F32).reshape(512, 128)
    store(w_down_grad, w_down_to)
    rest[4].wait()
    sums = fine_all[...].astype(F32).reshape(256, 128)
    for pair in range(4):
        both = sums[pair * 64 : (pair + 1) * 64]
        w_fine_grad[2 * pair] = both[:, 0:64]
        if pair < 3:
            w_fine_grad[2 * pair + 1] = pltpu.roll(both, 64, 1)[:, 0:64]
    store(w_fine_grad, w_fine_to)
    wait_all(rest[5:9])
    w_back_grad[...] = dot_tn(coarse_out[...], node_grad[...])
    store(w_back_grad, w_back_to)
    w_lift_grad[...] = dot_tn(node_mean[...], in_grad[...])
    store(w_lift_grad, w_lift_to)
    rest[9].wait()
    store(fine_out, fine_to)
    rest[10].wait()
    store(feats_out, feats_to)
    wait_all(stores)


def spec(space=pltpu.VMEM):
    return pl.BlockSpec(memory_space=space)


def shape(dims, dtype):
    return jax.ShapeDtypeStruct(dims, dtype)


def buf(dims, dtype=BF16):
    return pltpu.VMEM(dims, dtype)


def pairs(count):
    return pltpu.SemaphoreType.DMA((2, count))


def body(groups, subs, feats, neighbours, w_fine, w_down, w_lift, coarse_nbrs, w_coarse, w_back, w_up, grad_out):
    nodes = groups * subs
    vmem, anywhere = spec(), spec(pl.ANY)
    sq16, sq32 = buf((512, 512)), buf((512, 512), F32)
    natural = shape((64, 8, 512), BF16)
    na, nb = groups, subs // 2
    chunk, fine_chunk = (512 // na, 128), (128 // na, 128)
    sums = (
        shape((2, na) + chunk, BF16), shape((2, na) + chunk, BF16), shape((2, na) + fine_chunk, BF16),
    )
    coarse = (
        shape((7 * 512, nodes), BF16), shape((nodes, 256), BF16), shape((nodes, 256), BF16),
        shape((nodes, 512), BF16), shape((nodes, 512), BF16), shape((nodes, 512), BF16),
        shape((nodes, 256), BF16), shape((nodes, 512), BF16),
    )
    slots = buf((4, SLOTS, 16, 256))

    def reduction(part):
        return [
            buf((2, na) + part), buf((na,) + part), buf((na,) + part), buf((na - 1,) + part), buf((nb,) + part),
        ]

    reduction_sems = [pairs(1), pairs(na - 1), pairs(nb - 1), pairs(na - 1), pairs(na)]

    def like(x):
        return buf(x.shape, x.dtype)

    results = pl.pallas_call(
        functools.partial(block_kernel, groups, subs),
        out_shape=(natural, natural) + sums + coarse,
        in_specs=[anywhere, anywhere, vmem, vmem, anywhere, anywhere, vmem, anywhere, anywhere, anywhere],
        out_specs=(anywhere,) * 13,
        scratch_shapes=[like(natural), like(natural)]
        + [buf((512, 256)), buf((256, 512)), buf((256, 512)), buf((7, 512, 512)), buf((512, 256))]
        + [like(natural), like(natural)]
        + [like(x) for x in sums + coarse]
        + [sq16] * 6
        + [sq32, buf((512, 256)), buf((512, 256), F32), buf((512, 256), F32)]
        + [buf((subs, groups * 6, 128)), buf((ENTRIES, 128))]
        + [sq32, buf((SOURCES + 1, 16, 256)), buf((ENTRIES, 16, 256))]
        + [buf((16, SOURCES, 256)), buf((16, ENTRIES, 256), F32), buf((2, 512, 128), F32), buf((6, 2, 128, 128), F32)]
        + [buf((4, 8, 128), I32), buf((4, 8, 128), I32), buf((ENTRIES, 128), I32), buf((32, 128), I32)]
        + [pltpu.SMEM((4, 8, 128), I32), pltpu.SMEM((ENTRIES, 128), I32), pltpu.SMEM((32, 128), I32)]
        + [slots, slots, slots]
        + [sq16, buf((2, 256, 256)), buf((256, 256)), buf((256, 256))]
        + [sq32, buf((6, 128), F32), buf((groups, 6, 128), F32), buf((groups * 6, 128), F32)]
        + [buf((nodes * 6, 128), F32), buf((nodes, 7 * 512)), sq32, buf((512, 256)), sq16, sq32, sq32, sq32]
        + reduction(chunk)
        + reduction(chunk)
        + reduction(fine_chunk)
        + [pltpu.SemaphoreType.DMA((7,)), pltpu.SemaphoreType.DMA((13,)), pltpu.SemaphoreType.DMA((3,))]
        + [pairs(4), pairs(4), pairs(groups - 1), pairs(subs - 1), pairs(4)]
        + reduction_sems * 3,
        compiler_params=pltpu.CompilerParams(collective_id=1, has_side_effects=True, vmem_limit_bytes=MEMORY),
        name="block",
    )(
        feats.reshape(64, 8, 512), grad_out.reshape(64, 8, 512), neighbours,
        w_fine, w_down, w_up, coarse_nbrs.T, w_lift, w_coarse, w_back,
    )

    grads = (
        shape((7, 64, 64), F32), shape((512, 256), F32), shape((256, 512), F32),
        shape((7, 512, 512), F32), shape((512, 256), F32), shape((256, 512), F32),
    )
    outs = pl.pallas_call(
        functools.partial(finish_kernel, groups, subs),
        out_shape=(natural, natural) + grads,
        in_specs=[anywhere] * 13,
        out_specs=(anywhere,) * 8,
        scratch_shapes=[like(natural), like(natural)]
        + [like(x) for x in sums + coarse + grads]
        + [pltpu.SemaphoreType.DMA((19,)), pltpu.SemaphoreType.DMA((14,))],
        compiler_params=pltpu.CompilerParams(vmem_limit_bytes=MEMORY),
        name="finish",
    )(*results)
    return (outs[0].reshape(8, 8, 8, 512), outs[1].reshape(8, 8, 8, 512)) + tuple(outs[2:])


def solution(mesh):
    groups, subs = mesh.shape["grp"], mesh.shape["sub"]
    split4 = P(("grp", "sub"), None, None, None)
    return jax.shard_map(
        functools.partial(body, groups, subs),
        mesh=mesh,
        in_specs=(split4, P(("grp", "sub"), None)) + (P(),) * 7 + (split4,),
        out_specs=(split4, split4) + (P(),) * 6,
        check_vma=False,
    )
```
